256 devices in a mesh: slab: 128 (over z, x, y), ch: 2 (over core).
Axes of the slice: x: 4, y: 4, z: 8, core: 2. Of those that a mesh axis runs over, the one named last changes fastest.
Arguments:
- features: bfloat16 [6144, 64, 256], P('slab', None, 'ch'), may hold values from -6 to 6
- cotangent: bfloat16 [6144, 64, 256], P('slab', None, 'ch'), may hold values from -6 to 6
- weight: bfloat16 [27, 256, 256], P(None, 'ch'), may hold values from -0.078125 to 0.078125
- gain: float32 [256], P('ch'), may hold values from 0.1 to 1.9
- shift: float32 [256], P('ch'), may hold values from -3 to 3
- counts: int32 [128], P('slab'), may hold values from 6 to 48, as said below
- neighbours: int32 [6144, 27], P('slab'), may hold values from 0 to 144, as said below
Outputs:
- grad_features: bfloat16 [6144, 64, 256], P('slab', None, 'ch')
- grad_weight: float32 [27, 256, 256], P(None, 'ch')
- grad_gain: float32 [256], P('ch')
- grad_shift: float32 [256], P('ch')
The draws below stay inside these ranges and needn't reach their ends.
Inputs may be any that keep to these rules, and one draw needn't show every extreme that they name: `counts`: occupied blocks fill the first slots of each slab's list; some slab has exactly 48. `neighbours`: entries are as the steps state; a slot that is not occupied has 144 in every entry; entries of the first slab never name the slab before it, those of the last never the slab after it.
All inputs are finite; a program needn't handle non-finite values.
Results may differ from the reference program's by a relative error of at most 0.003.
Values may be sent and summed in bfloat16 or wider, within the bound.
No kernel may reach another device: no remote copies, remote signals or barrier semaphores. Data moves between devices by JAX's collectives and lax.ppermute only.
A program may use at most 128 MiB of HBM per device.

```python
import jax
import jax.numpy as jnp
from jax import lax

C = 256
GROUP_CH = 8
CAP = 48
GY = 128
GZ = 16
BLOCKS = 6144


def scene(key):
    key_count, key_full, key_road, key_order = jax.random.split(key, 4)
    slabs = BLOCKS // CAP
    counts = jax.random.randint(key_count, (slabs,), CAP // 8, CAP + 1)
    fullest = jax.random.randint(key_full, (), 0, slabs)
    counts = jnp.where(jnp.arange(slabs) == fullest, CAP, counts).astype(jnp.int32)
    drift = jax.random.randint(key_road, (slabs,), -1, 2)
    start = jnp.clip(GY // 3 + jnp.cumsum(drift), 0, GY - CAP // 4).astype(jnp.int32)
    scores = jax.random.randint(key_order, (slabs, CAP), 0, 1 << 20)
    places = jnp.arange(CAP, dtype=jnp.int32)[None, :]
    scores = jnp.where(places < counts[:, None], scores * CAP + places, (1 << 20) * CAP + places)
    road = jnp.argsort(scores, axis=1, stable=True).astype(jnp.int32)
    return (counts, start, road)


def draw_counts(key, part):
    counts, start, road = scene(key)
    return counts


def draw_neighbours(key, part):
    counts, start, road = scene(key)
    slabs = BLOCKS // CAP
    places = jnp.arange(CAP, dtype=jnp.int32)[None, :]
    slab_ids = jnp.broadcast_to(jnp.arange(slabs, dtype=jnp.int32)[:, None], (slabs, CAP))
    ypos = start[:, None] + road // 4
    zpos = road % 4
    valid = places < counts[:, None]
    slots = jnp.broadcast_to(places, (slabs, CAP))
    table = jnp.full((slabs, GY, GZ), -1, jnp.int32)
    table = table.at[slab_ids, ypos, zpos].set(jnp.where(valid, slots, -1))
    offsets = jnp.arange(27, dtype=jnp.int32)
    step_x = offsets // 9 - 1
    step_y = offsets // 3 % 3 - 1
    step_z = offsets % 3 - 1
    near_slab = slab_ids[:, :, None] + step_x
    near_y = ypos[:, :, None] + step_y
    near_z = zpos[:, :, None] + step_z
    inside = (near_slab >= 0) & (near_slab < slabs) & (near_y >= 0) & (near_y < GY) & (near_z >= 0) & (near_z < GZ)
    found = table[jnp.clip(near_slab, 0, slabs - 1), jnp.clip(near_y, 0, GY - 1), jnp.clip(near_z, 0, GZ - 1)]
    usable = inside & (found >= 0) & valid[:, :, None]
    result = jnp.where(usable, (step_x + 1) * CAP + found, 3 * CAP)
    return result.reshape(BLOCKS, 27).astype(jnp.int32)


def levels(rng, dims, cuts, smallest, high):
    factor_of, own = 1.0, jax.random.fold_in(rng, 6)
    for axis_at, parts in cuts:
        heights = jnp.exp(jax.random.uniform(jax.random.fold_in(own, axis_at), (parts,), jnp.float32, smallest / len(cuts), high / len(cuts)))
        factor_of = factor_of * jnp.repeat(heights, dims[axis_at] // parts).reshape([-1 if axis == axis_at else 1 for axis in range(len(dims))])
    return factor_of


def gaussian(stream_key, shape, width, limit, cuts=(), held_as=jnp.bfloat16):
    values = width * jax.random.normal(stream_key, shape, jnp.float32)
    if cuts:
        values = values * levels(stream_key, shape, cuts, -0.22, 0.18)
    return jnp.clip(values, -limit, limit).astype(held_as)


def setup_inputs(seed: int = 0) -> dict:
    keys = jax.random.split(jax.random.key(seed), 8)
    features = gaussian(keys[0], (BLOCKS, 64, C), 1.0, 6.0, ((0, 128), (2, 2)))
    cotangent = gaussian(keys[1], (BLOCKS, 64, C), 1.0, 6.0, ((0, 128), (2, 2)))
    weight = gaussian(keys[2], (27, C, C), (27 * C) ** -0.5, 0.078125, ((1, 2),))
    gain = jnp.clip(1.0 + 0.18 * jax.random.normal(keys[3], (C,), jnp.float32), 0.1, 1.9)
    shift = gaussian(keys[4], (C,), 0.5, 3.0, ((0, 2),), jnp.float32)
    counts = draw_counts(jax.random.fold_in(keys[7], 71), 0)
    neighbours = draw_neighbours(jax.random.fold_in(keys[7], 71), 0)
    return {"features": features, "cotangent": cotangent, "weight": weight, "gain": gain, "shift": shift, "counts": counts, "neighbours": neighbours}


def windows(extended, index_rows):
    count = index_rows.shape[0]
    chans = extended.shape[2]
    blocks = jnp.take(extended, index_rows.reshape(-1), axis=0).reshape(count, 3, 3, 3, 4, 4, 4, chans)
    grid = blocks.transpose(0, 1, 4, 2, 5, 3, 6, 7).reshape(count, 12, 12, 12, chans)
    return grid[:, 3:9, 3:9, 3:9, :]

def block_terms(grid, act_rows, weight):
    chans = grid.shape[4]
    grads = jnp.zeros((act_rows.shape[0], weight.shape[1]), jnp.float32)
    pieces = []
    for offset in range(27):
        step_x = offset // 9 - 1
        step_y = offset // 3 % 3 - 1
        step_z = offset % 3 - 1
        window = grid[:, 1 - step_x:5 - step_x, 1 - step_y:5 - step_y, 1 - step_z:5 - step_z, :].reshape(-1, chans)
        grads = grads + lax.dot_general(window, weight[offset], (((1,), (1,)), ((), ())), preferred_element_type=jnp.float32)
        pieces.append(lax.dot_general(act_rows, window, (((0,), (0,)), ((), ())), preferred_element_type=jnp.float32))
    return (grads, jnp.stack(pieces))

def reference(features, cotangent, weight, gain, shift, counts, neighbours):
    chans = features.shape[2]
    groups = chans // GROUP_CH
    rows = jnp.arange(BLOCKS, dtype=jnp.int32)
    slabs_of = rows // CAP
    occupied = (rows % CAP < jnp.take(counts, slabs_of)).astype(jnp.float32)[:, None, None]
    values = features.astype(jnp.float32)
    voxels = jnp.sum(counts).astype(jnp.float32) * 64.0 * GROUP_CH

    def group_sum(array):
        return array.reshape(BLOCKS, 64, groups, GROUP_CH).sum(axis=(0, 1, 3))

    def spread_out(vector):
        return jnp.repeat(vector, GROUP_CH)[None, None, :]
    mean = group_sum(values * occupied) / voxels
    centred = (values - spread_out(mean)) * occupied
    variance = group_sum(centred * centred) / voxels
    rstd = lax.rsqrt(variance + 1e-05)
    normed = (values - spread_out(mean)) * spread_out(rstd)
    pre = normed * gain + shift
    act = (jax.nn.silu(pre) * occupied).astype(jnp.bfloat16)
    part = neighbours // CAP
    source = (slabs_of[:, None] + part - 1) * CAP + neighbours % CAP
    source = jnp.where(neighbours == 3 * CAP, BLOCKS, source).astype(jnp.int32)
    extended = jnp.concatenate([cotangent, jnp.zeros((1, 64, chans), jnp.bfloat16)], axis=0)
    count_groups = BLOCKS // 8

    def step(carry, inputs):
        index_rows, act_rows = inputs
        grads, pieces = block_terms(windows(extended, index_rows), act_rows, weight)
        return (carry + pieces, grads)
    grad_weight, grad_act = lax.scan(step, jnp.zeros((27, chans, chans), jnp.float32), (source.reshape(count_groups, 8, 27), act.reshape(count_groups, 8 * 64, chans)))
    grad_act = grad_act.reshape(BLOCKS, 64, chans)
    sig = jax.nn.sigmoid(pre)
    grad_pre = occupied * grad_act * sig * (1.0 + pre * (1.0 - sig))
    grad_shift = lax.optimization_barrier(jnp.sum(grad_pre, axis=(0, 1)))
    grad_gain = lax.optimization_barrier(jnp.sum(grad_pre * normed, axis=(0, 1)))
    first = (gain * grad_shift).reshape(groups, GROUP_CH).sum(axis=1)
    second = (gain * grad_gain).reshape(groups, GROUP_CH).sum(axis=1)
    inner = gain * grad_pre - spread_out(first) / voxels - normed * spread_out(second) / voxels
    grad_features = (occupied * (cotangent.astype(jnp.float32) + spread_out(rstd) * inner)).astype(jnp.bfloat16)
    return (grad_features, grad_weight, grad_gain, grad_shift)
```

```python
import functools

import jax
import jax.numpy as jnp
from jax import lax
from jax.experimental import pallas as pl
from jax.experimental.pallas import tpu as pltpu
from jax.sharding import Mesh
from jax.sharding import PartitionSpec as P

GROUP_CH = 8
CUT = {128: (8, 4, 4), 8: (2, 2, 2), 4: (2, 2, 1)}
SLABS = ("z", "x", "y")
PLANE = ("x", "y")
F32 = jnp.float32
BF16 = jnp.bfloat16
VMEM = pl.BlockSpec(memory_space=pltpu.VMEM)
SMEM = pl.BlockSpec(memory_space=pltpu.SMEM)
ANY = pl.BlockSpec(memory_space=pl.ANY)


def call(kernel, out_shape, in_specs, scratch=(), flops=0, bytes_accessed=0):
    several = isinstance(out_shape, (list, tuple))
    return pl.pallas_call(
        kernel,
        out_shape=out_shape,
        in_specs=in_specs,
        out_specs=[VMEM] * len(out_shape) if several else VMEM,
        scratch_shapes=list(scratch),
        compiler_params=pltpu.CompilerParams(vmem_limit_bytes=48 * 1024 * 1024),
        cost_estimate=pl.CostEstimate(
            flops=flops, bytes_accessed=bytes_accessed, transcendentals=0
        ),
    )


def exact_dot(left, right):
    return jnp.dot(left, right, precision=lax.Precision.HIGHEST, preferred_element_type=F32)


def iota(shape, dim):
    return lax.broadcasted_iota(jnp.int32, shape, dim)


def turned(rows_ref, out_ref):
    slots = out_ref.shape[1]
    for voxel in range(64):
        out_ref[voxel] = rows_ref[pl.ds(voxel, slots, stride=64), :].astype(out_ref.dtype)


def turn_kernel(in_ref, out_ref, low_ref, high_ref, rows_ref):
    rows_ref[...] = in_ref[...].astype(F32)
    turned(rows_ref, out_ref)
    low_ref[...] = out_ref[0:16]
    high_ref[...] = out_ref[48:64]


def sums_kernel(counts_ref, in_ref, out_ref, sent_ref, rows_ref):
    slots = out_ref.shape[1]
    count = counts_ref[0]
    rows_ref[...] = in_ref[...].astype(F32)

    def over_slots(term):
        total = jnp.zeros((8, 128), F32)
        for slot in range(slots):
            rows = term(rows_ref[slot * 64 : slot * 64 + 64, :]).reshape(8, 8, 128).sum(axis=0)
            total = total + jnp.where(slot < count, rows, 0.0)
        return jnp.broadcast_to(jnp.sum(total, axis=0, keepdims=True), (8, 128))

    lane_in, lane_out = iota((128, 128), 0), iota((128, 128), 1)
    same = (lane_in // GROUP_CH == lane_out // GROUP_CH).astype(F32)
    to_sum = (lane_in // GROUP_CH == lane_out).astype(F32)
    to_square = (lane_in // GROUP_CH + 16 == lane_out).astype(F32)
    total = over_slots(lambda rows: rows)
    entries = count.astype(F32) * (64.0 * GROUP_CH)
    mean = (exact_dot(total, same) / entries)[0:1]

    def centred(rows):
        apart = rows - mean
        return apart * apart

    squares = over_slots(centred)
    row = exact_dot(total, to_sum) + exact_dot(squares, to_square)
    row = row + jnp.where(iota((8, 128), 1) == 32, count.astype(F32), 0.0)
    sent_ref[...] = jnp.broadcast_to(row[0:1].reshape(1, 1, 128), sent_ref.shape)
    turned(rows_ref, out_ref)


def halo_kernel(
    core_ref,
    near_ref,
    own_ref,
    own_other_ref,
    before_ref,
    before_other_ref,
    after_ref,
    after_other_ref,
    grid_ref,
    low_ref,
    high_ref,
    pick_ref,
    sems,
):
    slots = near_ref.shape[0]
    core = core_ref[0]
    mine = pl.ds(pl.multiple_of(core * 128, 128), 128)
    other = pl.ds(pl.multiple_of((1 - core) * 128, 128), 128)
    centre = grid_ref.at[1:5, 1:5, 1:5]
    copies = [
        pltpu.make_async_copy(own_ref, centre.at[:, :, :, :, mine], sems.at[0]),
        pltpu.make_async_copy(own_other_ref, centre.at[:, :, :, :, other], sems.at[1]),
        pltpu.make_async_copy(before_ref, low_ref.at[:, :, :, mine], sems.at[2]),
        pltpu.make_async_copy(before_other_ref, low_ref.at[:, :, :, other], sems.at[3]),
        pltpu.make_async_copy(after_ref, high_ref.at[:, :, :, mine], sems.at[4]),
        pltpu.make_async_copy(after_other_ref, high_ref.at[:, :, :, other], sems.at[5]),
    ]
    for copy in copies:
        copy.start()
    near = near_ref[...]
    columns = iota((slots, 3 * slots), 1)
    for offset in range(27):
        pick_ref[offset] = (near[:, offset : offset + 1] == columns).astype(F32)
    for copy in copies:
        copy.wait()

    def side(at):
        return -1 if at == 0 else (1 if at == 5 else 0)

    def source(at):
        return {0: 4, 5: 1}.get(at, at)

    places = [(a, b, c) for a in range(6) for b in range(6) for c in range(6)]
    for a, b, c in places:
        dx, dy, dz = side(a), side(b), side(c)
        if (dx, dy, dz) == (0, 0, 0):
            continue
        offset = 9 * (dx + 1) + 3 * (dy + 1) + dz + 1
        inside = grid_ref[source(a), source(b), source(c)]
        if dx == 0:
            pick = pick_ref[offset, :, slots : 2 * slots]
            table = inside
        elif dx < 0:
            pick = pick_ref[offset, :, 0 : 2 * slots]
            table = jnp.concatenate([low_ref[source(b) - 1, source(c) - 1], inside], axis=0)
        else:
            pick = pick_ref[offset, :, slots : 3 * slots]
            table = jnp.concatenate([inside, high_ref[source(b) - 1, source(c) - 1]], axis=0)
        grid_ref[a, b, c] = jnp.dot(pick.astype(BF16), table, preferred_element_type=F32).astype(
            BF16
        )


def window(grid_ref, plane, turn):
    slots = grid_ref.shape[3]
    block = grid_ref[plane, pl.ds(2 - turn // 3, 4), pl.ds(2 - turn % 3, 4)]
    return block.reshape(16 * slots, 256)


def planes_of(plane):
    return max(0, plane - 2), min(3, plane) + 1


def weight_grad_kernel(
    counts_ref,
    table_ref,
    gain_ref,
    shift_ref,
    values_ref,
    grid_hbm,
    out_ref,
    norm_ref,
    grid_ref,
    act_ref,
    total_ref,
    sem,
):
    slots = values_ref.shape[1]
    copy = pltpu.make_async_copy(grid_hbm, grid_ref, sem)
    copy.start()
    table = table_ref[...]
    held = jnp.sum(table, axis=0)
    voxels = held[:, 32:33] * (64.0 * GROUP_CH)
    entries = table[:, :, 32:33] * (64.0 * GROUP_CH)
    mean = held / voxels
    apart = table / entries - mean.reshape(1, 1, 128)
    between = jnp.sum(apart * apart * entries, axis=0)
    lane_in, lane_out = iota((128, 128), 0), iota((128, 128), 1)
    from_sum = (lane_in == lane_out // GROUP_CH).astype(F32)
    from_square = (lane_in == lane_out // GROUP_CH + 16).astype(F32)

    def spread(row, matrix):
        return exact_dot(jnp.broadcast_to(row, (8, 128)), matrix)[0:1]

    mean = spread(mean, from_sum)
    variance = (spread(between, from_sum) + spread(held, from_square)) / voxels
    rstd = lax.rsqrt(variance + 1e-05)
    norm_ref[0:1, :] = mean
    norm_ref[1:2, :] = rstd
    norm_ref[2:3, :] = jnp.broadcast_to(voxels, (1, 128))
    norm_ref[3:8, :] = jnp.zeros((5, 128), F32)
    gain, shift = gain_ref[...], shift_ref[...]
    live = iota((slots, 128), 0) < counts_ref[0]
    for plane in range(4):
        pieces = []
        for voxel in range(plane * 16, plane * 16 + 16):
            normed = (values_ref[voxel].astype(F32) - mean) * rstd
            pre = normed * gain + shift
            pieces.append(jnp.where(live, pre / (1.0 + jnp.exp(-pre)), 0.0))
        rows = jnp.concatenate(pieces, axis=0)
        act_ref[plane * 128 : plane * 128 + 128, :] = rows.T.astype(BF16)
    copy.wait()

    @pl.loop(0, 9)
    def _(turn):
        for plane in range(6):
            first, last = planes_of(plane)
            part = jnp.dot(
                act_ref[first * 128 : last * 128, :],
                window(grid_ref, plane, turn),
                preferred_element_type=F32,
            )
            for at in range(first, last):
                step = at - plane + 2
                term = part[(at - first) * 128 : (at - first) * 128 + 128]
                if at == 0:
                    total_ref[step] = term
                else:
                    total_ref[step] += term
        for step in range(3):
            out_ref[step, turn] = total_ref[step].astype(BF16)


def act_grad_kernel(
    counts_ref,
    norm_ref,
    gain_ref,
    shift_ref,
    values_ref,
    weight_ref,
    grid_ref,
    out_ref,
    sums_ref,
    total_ref,
):
    slots = values_ref.shape[1]
    total_ref[...] = jnp.zeros_like(total_ref)

    @pl.loop(0, 9)
    def _(turn):
        for plane in range(6):
            first, last = planes_of(plane)
            low, high = first - plane + 2, last - plane + 2
            part = lax.dot_general(
                window(grid_ref, plane, turn),
                weight_ref[low:high, turn].reshape((high - low) * 128, 256),
                (((1,), (1,)), ((), ())),
                preferred_element_type=F32,
            )
            for at in range(first, last):
                term = part[:, (at - first) * 128 : (at - first) * 128 + 128]
                total_ref[at] += term.reshape(16, slots, 128)

    mean, rstd = norm_ref[0:1, :], norm_ref[1:2, :]
    gain, shift = gain_ref[...], shift_ref[...]
    live = iota((slots, 128), 0) < counts_ref[0]
    shift_sum = jnp.zeros((8, 128), F32)
    gain_sum = jnp.zeros((8, 128), F32)
    for voxel in range(64):
        normed = (values_ref[voxel].astype(F32) - mean) * rstd
        pre = normed * gain + shift
        sig = 1.0 / (1.0 + jnp.exp(-pre))
        grad = total_ref[voxel // 16, voxel % 16] * sig * (1.0 + pre * (1.0 - sig))
        grad = jnp.where(live, grad, 0.0)
        out_ref[voxel] = grad
        shift_sum = shift_sum + grad.reshape(slots // 8, 8, 128).sum(axis=0)
        gain_sum = gain_sum + (grad * normed).reshape(slots // 8, 8, 128).sum(axis=0)
    sums_ref[:, 0:128] = jnp.sum(shift_sum, axis=0, keepdims=True)
    sums_ref[:, 128:256] = jnp.sum(gain_sum, axis=0, keepdims=True)


def last_kernel(
    counts_ref, norm_ref, gain_ref, sums_ref, values_ref, cotangent_ref, grad_ref, out_ref
):
    slots = grad_ref.shape[0] // 64
    mean, rstd, voxels = norm_ref[0:1, :], norm_ref[1:2, :], norm_ref[2:3, :]
    gain = gain_ref[...]
    lane_in, lane_out = iota((128, 128), 0), iota((128, 128), 1)
    same = (lane_in // GROUP_CH == lane_out // GROUP_CH).astype(F32)

    def grouped(row):
        return exact_dot(jnp.broadcast_to(row, (8, 128)), same)[0:1]

    first = grouped(gain * sums_ref[:, 0:128]) / voxels
    second = grouped(gain * sums_ref[:, 128:256]) / voxels
    for slot in range(slots):
        rows = slice(slot * 64, slot * 64 + 64)
        normed = (values_ref[rows, :].astype(F32) - mean) * rstd
        grad = grad_ref[pl.ds(slot, 64, stride=slots), :]
        inner = gain * grad - first - normed * second
        result = cotangent_ref[rows, :].astype(F32) + rstd * inner
        out_ref[rows, :] = jnp.where(slot < counts_ref[0], result, 0.0).astype(BF16)


def body(features, cotangent, weight, gain, shift, counts, neighbours):
    slots, voxels, width = features.shape
    rows = slots * voxels
    n_plane = lax.axis_size("x") * lax.axis_size("y")
    n_line = lax.axis_size("z")
    n_slab = n_plane * n_line
    core = lax.axis_index("ch").astype(jnp.int32).reshape(1)
    swap = [(0, 1), (1, 0)]
    turned_shape = jax.ShapeDtypeStruct((voxels, slots, width), BF16)
    face_shape = jax.ShapeDtypeStruct((16, slots, width), BF16)
    rows_scratch = pltpu.VMEM((rows, width), F32)
    gain_row, shift_row = gain.reshape(1, width), shift.reshape(1, width)

    own, low, high = call(
        turn_kernel, [turned_shape, face_shape, face_shape], [VMEM], [rows_scratch]
    )(cotangent.reshape(rows, width))
    before = lax.ppermute(high, SLABS, [(i, i + 1) for i in range(n_slab - 1)])
    after = lax.ppermute(low, SLABS, [(i + 1, i) for i in range(n_slab - 1)])
    own_other = lax.ppermute(own, "ch", swap)
    values, sent = call(
        sums_kernel,
        [turned_shape, jax.ShapeDtypeStruct((n_slab, 1, 128), F32)],
        [SMEM, VMEM],
        [rows_scratch],
    )(counts, features.reshape(rows, width))
    table = lax.all_to_all(sent, SLABS, 0, 0, tiled=True)
    before_other = lax.ppermute(before, "ch", swap)
    after_other = lax.ppermute(after, "ch", swap)

    cube = (4, 4, 4, slots, width)
    face = (4, 4, slots, width)
    grid_shape = (6, 6, 6, slots, 2 * width)
    grid = call(
        halo_kernel,
        jax.ShapeDtypeStruct(grid_shape, BF16),
        [SMEM, VMEM] + [ANY] * 6,
        [
            pltpu.VMEM((4, 4, slots, 2 * width), BF16),
            pltpu.VMEM((4, 4, slots, 2 * width), BF16),
            pltpu.VMEM((27, slots, 3 * slots), F32),
            pltpu.SemaphoreType.DMA((6,)),
        ],
        flops=10**9,
    )(
        core,
        neighbours,
        own.reshape(cube),
        own_other.reshape(cube),
        before.reshape(face),
        before_other.reshape(face),
        after.reshape(face),
        after_other.reshape(face),
    )

    weight_term, norm = call(
        weight_grad_kernel,
        [
            jax.ShapeDtypeStruct((3, 9, width, 2 * width), BF16),
            jax.ShapeDtypeStruct((8, 128), F32),
        ],
        [SMEM, VMEM, VMEM, VMEM, VMEM, ANY],
        [
            pltpu.VMEM(grid_shape, BF16),
            pltpu.VMEM((4 * width, 16 * slots), BF16),
            pltpu.VMEM((3, width, 2 * width), F32),
            pltpu.SemaphoreType.DMA,
        ],
        flops=2 * rows * 27 * width * 2 * width,
    )(counts, table, gain_row, shift_row, values, grid)
    piece = 27 * width // n_plane
    parts = lax.all_to_all(
        weight_term.reshape(n_plane, piece, 2 * width), PLANE, 0, 0, tiled=True
    )

    grad_pre, sums = call(
        act_grad_kernel,
        [
            jax.ShapeDtypeStruct((voxels, slots, width), F32),
            jax.ShapeDtypeStruct((1, 2 * width), F32),
        ],
        [SMEM] + [VMEM] * 6,
        [pltpu.VMEM((4, 16, slots, width), F32)],
        flops=2 * rows * 27 * width * 2 * width,
    )(
        counts,
        norm,
        gain_row,
        shift_row,
        values,
        weight.reshape(3, 9, width, 2 * width),
        grid,
    )

    part = jnp.sum(parts.astype(F32), axis=0).reshape(n_line, piece // n_line, 2 * width)
    part = jnp.concatenate(
        [part, jnp.broadcast_to(sums.reshape(1, 1, 2 * width), (n_line, 1, 2 * width))], axis=1
    )
    part = jnp.sum(lax.all_to_all(part, "z", 0, 0, tiled=True), axis=0)
    final, line_sums = part[:-1].astype(BF16), part[-1:]
    line = jnp.broadcast_to(final[None], (n_line,) + final.shape)
    line = lax.all_to_all(line, "z", 0, 0, tiled=True).reshape(piece, 2 * width)
    split = []
    rest = line_sums
    for _ in range(3):
        top = lax.reduce_precision(rest, 8, 7)
        split.append(top.astype(BF16))
        rest = rest - top
    line = jnp.concatenate([line] + split + [jnp.zeros((5, 2 * width), BF16)], axis=0)
    plane = jnp.broadcast_to(line[None], (n_plane,) + line.shape)
    plane = lax.all_to_all(plane, PLANE, 0, 0, tiled=True)
    grad_weight = plane[:, :piece].astype(F32).reshape(27, width, 2 * width)
    totals = jnp.sum(plane[:, piece : piece + 3].astype(F32), axis=(0, 1)).reshape(1, 2 * width)

    grad_features = call(
        last_kernel,
        jax.ShapeDtypeStruct((rows, width), BF16),
        [SMEM] + [VMEM] * 6,
    )(
        counts,
        norm,
        gain_row,
        totals,
        features.reshape(rows, width),
        cotangent.reshape(rows, width),
        grad_pre.reshape(rows, width),
    )
    return (
        grad_features.reshape(features.shape),
        grad_weight,
        totals[0, width:],
        totals[0, :width],
    )


def solution(mesh):
    slabs = mesh.devices.shape[0]
    inner = Mesh(mesh.devices.reshape(CUT[slabs] + (2,)), SLABS + ("ch",))
    in_specs = (
        P(SLABS, None, "ch"),
        P(SLABS, None, "ch"),
        P(None, "ch", None),
        P("ch"),
        P("ch"),
        P(SLABS),
        P(SLABS, None),
    )
    out_specs = (P(SLABS, None, "ch"), P(None, "ch", None), P("ch"), P("ch"))
    return jax.shard_map(body, mesh=inner, in_specs=in_specs, out_specs=out_specs, check_vma=False)
```

```python
import functools

import jax
import jax.numpy as jnp
from jax import lax
from jax.experimental import pallas as pl
from jax.experimental.pallas import tpu as pltpu
from jax.sharding import Mesh
from jax.sharding import PartitionSpec as P

GROUP_CH = 8
CUT = {128: (8, 4, 4), 8: (2, 2, 2), 4: (2, 2, 1)}
SLABS = ("z", "x", "y")
PLANE = ("x", "y")
F32 = jnp.float32
BF16 = jnp.bfloat16
VMEM = pl.BlockSpec(memory_space=pltpu.VMEM)
SMEM = pl.BlockSpec(memory_space=pltpu.SMEM)
ANY = pl.BlockSpec(memory_space=pl.ANY)
HBM = pl.BlockSpec(memory_space=pltpu.HBM)


def call(kernel, out_shape, in_specs, scratch=(), out_specs=VMEM, flops=0, mib=20):
    if isinstance(out_shape, (list, tuple)) and out_specs is VMEM:
        out_specs = [VMEM] * len(out_shape)
    return pl.pallas_call(
        kernel,
        out_shape=out_shape,
        in_specs=in_specs,
        out_specs=out_specs,
        scratch_shapes=list(scratch),
        compiler_params=pltpu.CompilerParams(vmem_limit_bytes=mib * 1024 * 1024),
        cost_estimate=pl.CostEstimate(flops=flops, bytes_accessed=0, transcendentals=0),
    )


def exact_dot(left, right):
    return jnp.dot(left, right, precision=lax.Precision.HIGHEST, preferred_element_type=F32)


def iota(shape, dim):
    return lax.broadcasted_iota(jnp.int32, shape, dim)


def turned(rows_ref, out_ref):
    slots = out_ref.shape[1]
    for voxel in range(64):
        out_ref[voxel] = rows_ref[pl.ds(voxel, slots, stride=64), :].astype(out_ref.dtype)


def prepare_kernel(
    counts_ref,
    values_hbm,
    cotangent_hbm,
    values_hbm_out,
    own_hbm,
    low_hbm,
    high_hbm,
    sent_ref,
    held_ref,
    rows_ref,
    values_out,
    own_ref,
    sems,
    out_sems,
):
    slots = own_ref.shape[1]
    count = counts_ref[0]
    chunk = 64 * (slots // 4)
    copies = [
        pltpu.make_async_copy(
            source.at[pl.ds(at * chunk, chunk)],
            held_ref.at[which, pl.ds(at * chunk, chunk)],
            sems.at[which, at],
        )
        for which, source in enumerate((cotangent_hbm, values_hbm))
        for at in range(4)
    ]
    for copy in copies:
        copy.start()
    for at in range(4):
        copies[at].wait()
        rows_ref[0, at * chunk : at * chunk + chunk] = held_ref[
            0, at * chunk : at * chunk + chunk
        ].astype(F32)
    turned(rows_ref.at[0], own_ref)
    sends = [
        pltpu.make_async_copy(own_ref.at[0:16], low_hbm, out_sems.at[0]),
        pltpu.make_async_copy(own_ref.at[48:64], high_hbm, out_sems.at[1]),
        pltpu.make_async_copy(own_ref, own_hbm, out_sems.at[2]),
        pltpu.make_async_copy(values_out, values_hbm_out, out_sems.at[3]),
    ]
    for send in sends[:3]:
        send.start()
    for at in range(4):
        copies[4 + at].wait()
        rows_ref[1, at * chunk : at * chunk + chunk] = held_ref[
            1, at * chunk : at * chunk + chunk
        ].astype(F32)

    turned(rows_ref.at[1], values_out)
    sends[3].start()

    def over_slots(term):
        total = jnp.zeros((8, 128), F32)
        for slot in range(slots):
            rows = term(rows_ref[1, slot * 64 : slot * 64 + 64, :]).reshape(8, 8, 128).sum(axis=0)
            total = total + jnp.where(slot < count, rows, 0.0)
        return jnp.broadcast_to(jnp.sum(total, axis=0, keepdims=True), (8, 128))

    lane_in, lane_out = iota((128, 128), 0), iota((128, 128), 1)
    same = (lane_in // GROUP_CH == lane_out // GROUP_CH).astype(F32)
    to_sum = (lane_in // GROUP_CH == lane_out).astype(F32)
    to_square = (lane_in // GROUP_CH + 16 == lane_out).astype(F32)
    total = over_slots(lambda rows: rows)
    entries = count.astype(F32) * (64.0 * GROUP_CH)
    mean = (exact_dot(total, same) / entries)[0:1]

    def centred(rows):
        apart = rows - mean
        return apart * apart

    squares = over_slots(centred)
    row = exact_dot(total, to_sum) + exact_dot(squares, to_square)
    row = row + jnp.where(iota((8, 128), 1) == 32, count.astype(F32), 0.0)
    sent_ref[...] = jnp.broadcast_to(row[0:1].reshape(1, 1, 128), sent_ref.shape)
    for send in sends:
        send.wait()


def halo_kernel(
    core_ref,
    near_ref,
    own_ref,
    own_other_ref,
    before_ref,
    before_other_ref,
    after_ref,
    after_other_ref,
    grid_ref,
    low_ref,
    high_ref,
    pick_ref,
    sems,
):
    slots = near_ref.shape[0]
    core = core_ref[0]
    mine = pl.ds(pl.multiple_of(core * 128, 128), 128)
    other = pl.ds(pl.multiple_of((1 - core) * 128, 128), 128)
    centre = grid_ref.at[1:5, 1:5, 1:5]
    copies = [
        pltpu.make_async_copy(own_ref, centre.at[:, :, :, :, mine], sems.at[0]),
        pltpu.make_async_copy(own_other_ref, centre.at[:, :, :, :, other], sems.at[1]),
        pltpu.make_async_copy(before_ref, low_ref.at[:, :, :, mine], sems.at[2]),
        pltpu.make_async_copy(before_other_ref, low_ref.at[:, :, :, other], sems.at[3]),
        pltpu.make_async_copy(after_ref, high_ref.at[:, :, :, mine], sems.at[4]),
        pltpu.make_async_copy(after_other_ref, high_ref.at[:, :, :, other], sems.at[5]),
    ]
    for copy in copies:
        copy.start()
    near = near_ref[...]
    columns = iota((slots, 3 * slots), 1)
    for offset in range(27):
        pick_ref[offset] = (near[:, offset : offset + 1] == columns).astype(F32)
    for copy in copies:
        copy.wait()

    def side(at):
        return -1 if at == 0 else (1 if at == 5 else 0)

    def source(at):
        return {0: 4, 5: 1}.get(at, at)

    places = [(a, b, c) for a in range(6) for b in range(6) for c in range(6)]
    for a, b, c in places:
        dx, dy, dz = side(a), side(b), side(c)
        if (dx, dy, dz) == (0, 0, 0):
            continue
        offset = 9 * (dx + 1) + 3 * (dy + 1) + dz + 1
        inside = grid_ref[source(a), source(b), source(c)]
        if dx == 0:
            pick = pick_ref[offset, :, slots : 2 * slots]
            table = inside
        elif dx < 0:
            pick = pick_ref[offset, :, 0 : 2 * slots]
            table = jnp.concatenate([low_ref[source(b) - 1, source(c) - 1], inside], axis=0)
        else:
            pick = pick_ref[offset, :, slots : 3 * slots]
            table = jnp.concatenate([inside, high_ref[source(b) - 1, source(c) - 1]], axis=0)
        grid_ref[a, b, c] = jnp.dot(pick.astype(BF16), table, preferred_element_type=F32).astype(
            BF16
        )


def window(grid_ref, plane, turn):
    slots = grid_ref.shape[3]
    block = grid_ref[plane, pl.ds(2 - turn // 3, 4), pl.ds(2 - turn % 3, 4)]
    return block.reshape(16 * slots, 256)


def planes_of(plane):
    return max(0, plane - 2), min(3, plane) + 1


def weight_grad_kernel(
    counts_ref,
    table_ref,
    gain_ref,
    shift_ref,
    values_ref,
    grid_ref,
    out_ref,
    norm_ref,
    act_ref,
    total_ref,
):
    slots = values_ref.shape[1]
    table = table_ref[...]
    held = jnp.sum(table, axis=0)
    voxels = held[:, 32:33] * (64.0 * GROUP_CH)
    entries = table[:, :, 32:33] * (64.0 * GROUP_CH)
    mean = held / voxels
    apart = table / entries - mean.reshape(1, 1, 128)
    between = jnp.sum(apart * apart * entries, axis=0)
    lane_in, lane_out = iota((128, 128), 0), iota((128, 128), 1)
    from_sum = (lane_in == lane_out // GROUP_CH).astype(F32)
    from_square = (lane_in == lane_out // GROUP_CH + 16).astype(F32)

    def spread(row, matrix):
        return exact_dot(jnp.broadcast_to(row, (8, 128)), matrix)[0:1]

    mean = spread(mean, from_sum)
    variance = (spread(between, from_sum) + spread(held, from_square)) / voxels
    rstd = lax.rsqrt(variance + 1e-05)
    norm_ref[0:1, :] = mean
    norm_ref[1:2, :] = rstd
    norm_ref[2:3, :] = jnp.broadcast_to(voxels, (1, 128))
    norm_ref[3:8, :] = jnp.zeros((5, 128), F32)
    gain, shift = gain_ref[...], shift_ref[...]
    live = iota((slots, 128), 0) < counts_ref[0]
    for plane in range(4):
        pieces = []
        for voxel in range(plane * 16, plane * 16 + 16):
            normed = (values_ref[voxel].astype(F32) - mean) * rstd
            pre = normed * gain + shift
            pieces.append(jnp.where(live, pre / (1.0 + jnp.exp(-pre)), 0.0))
        rows = jnp.concatenate(pieces, axis=0)
        act_ref[plane * 128 : plane * 128 + 128, :] = rows.T.astype(BF16)
    for turn in range(9):
        for plane in range(6):
            first, last = planes_of(plane)
            part = jnp.dot(
                act_ref[first * 128 : last * 128, :],
                window(grid_ref, plane, turn),
                preferred_element_type=F32,
            )
            for at in range(first, last):
                step = at - plane + 2
                term = part[(at - first) * 128 : (at - first) * 128 + 128]
                if at == 0:
                    total_ref[step] = term
                else:
                    total_ref[step] += term
        for step in range(3):
            out_ref[step, turn] = total_ref[step].astype(BF16)


def act_grad_kernel(
    counts_ref,
    norm_ref,
    gain_ref,
    shift_ref,
    values_ref,
    weight_ref,
    grid_ref,
    out_ref,
    sums_ref,
    total_ref,
):
    slots = values_ref.shape[1]
    total_ref[...] = jnp.zeros_like(total_ref)

    @pl.loop(0, 9)
    def _(turn):
        for plane in range(6):
            first, last = planes_of(plane)
            low, high = first - plane + 2, last - plane + 2
            part = lax.dot_general(
                window(grid_ref, plane, turn),
                weight_ref[low:high, turn].reshape((high - low) * 128, 256),
                (((1,), (1,)), ((), ())),
                preferred_element_type=F32,
            )
            for at in range(first, last):
                term = part[:, (at - first) * 128 : (at - first) * 128 + 128]
                total_ref[at] += term.reshape(16, slots, 128)

    mean, rstd = norm_ref[0:1, :], norm_ref[1:2, :]
    gain, shift = gain_ref[...], shift_ref[...]
    live = iota((slots, 128), 0) < counts_ref[0]
    shift_sum = jnp.zeros((8, 128), F32)
    gain_sum = jnp.zeros((8, 128), F32)
    for voxel in range(64):
        normed = (values_ref[voxel].astype(F32) - mean) * rstd
        pre = normed * gain + shift
        sig = 1.0 / (1.0 + jnp.exp(-pre))
        grad = total_ref[voxel // 16, voxel % 16] * sig * (1.0 + pre * (1.0 - sig))
        grad = jnp.where(live, grad, 0.0)
        out_ref[voxel] = grad
        shift_sum = shift_sum + grad.reshape(slots // 8, 8, 128).sum(axis=0)
        gain_sum = gain_sum + (grad * normed).reshape(slots // 8, 8, 128).sum(axis=0)
    sums_ref[:, 0:128] = jnp.sum(shift_sum, axis=0, keepdims=True)
    sums_ref[:, 128:256] = jnp.sum(gain_sum, axis=0, keepdims=True)


def last_kernel(
    counts_ref,
    norm_ref,
    gain_ref,
    plane_ref,
    values_ref,
    cotangent_ref,
    grad_ref,
    out_hbm,
    weight_hbm,
    sums_ref,
    out_ref,
    weight_ref,
    out_sems,
    weight_sems,
):
    slots = grad_ref.shape[0] // 64
    pieces = plane_ref.shape[0]
    piece = weight_ref.shape[0] // pieces
    copies = []
    totals = jnp.zeros((1, 256), F32)
    for at in range(pieces):
        block = plane_ref[at].astype(F32)
        rows = pl.ds(at * piece, piece)
        weight_ref[rows] = block[0:piece]
        totals = totals + (block[piece : piece + 1] + block[piece + 1 : piece + 2])
        totals = totals + block[piece + 2 : piece + 3]
        copies.append(
            pltpu.make_async_copy(weight_ref.at[rows], weight_hbm.at[rows], weight_sems.at[at])
        )
        copies[-1].start()
    shift_sum, gain_sum = totals[:, 0:128], totals[:, 128:256]
    sums_ref[0:1] = gain_sum
    sums_ref[1:2] = shift_sum
    mean, rstd, voxels = norm_ref[0:1, :], norm_ref[1:2, :], norm_ref[2:3, :]
    gain = gain_ref[...]
    lane_in, lane_out = iota((128, 128), 0), iota((128, 128), 1)
    same = (lane_in // GROUP_CH == lane_out // GROUP_CH).astype(F32)

    def grouped(row):
        return exact_dot(jnp.broadcast_to(row, (8, 128)), same)[0:1]

    first = grouped(gain * shift_sum) / voxels
    second = grouped(gain * gain_sum) / voxels
    chunk = slots // 4
    for slot in range(slots):
        rows = slice(slot * 64, slot * 64 + 64)
        normed = (values_ref[rows, :].astype(F32) - mean) * rstd
        grad = grad_ref[pl.ds(slot, 64, stride=slots), :]
        inner = gain * grad - first - normed * second
        result = cotangent_ref[rows, :].astype(F32) + rstd * inner
        out_ref[rows, :] = jnp.where(slot < counts_ref[0], result, 0.0).astype(BF16)
        if slot % chunk == chunk - 1:
            at = slot // chunk
            rows = pl.ds(at * chunk * 64, chunk * 64)
            copies.append(
                pltpu.make_async_copy(out_ref.at[rows], out_hbm.at[rows], out_sems.at[at])
            )
            copies[-1].start()
    for copy in copies:
        copy.wait()


def body(features, cotangent, weight, gain, shift, counts, neighbours):
    slots, voxels, width = features.shape
    rows = slots * voxels
    n_plane = lax.axis_size("x") * lax.axis_size("y")
    n_line = lax.axis_size("z")
    n_slab = n_plane * n_line
    core = lax.axis_index("ch").astype(jnp.int32).reshape(1)
    turned_shape = jax.ShapeDtypeStruct((voxels, slots, width), BF16)
    face_shape = jax.ShapeDtypeStruct((16, slots, width), BF16)
    gain_row, shift_row = gain.reshape(1, width), shift.reshape(1, width)

    values, own, low, high, sent = call(
        prepare_kernel,
        [
            turned_shape,
            turned_shape,
            face_shape,
            face_shape,
            jax.ShapeDtypeStruct((n_slab, 1, 128), F32),
        ],
        [SMEM, HBM, HBM],
        [
            pltpu.VMEM((2, rows, width), BF16),
            pltpu.VMEM((2, rows, width), F32),
            pltpu.VMEM(turned_shape.shape, BF16),
            pltpu.VMEM(turned_shape.shape, BF16),
            pltpu.SemaphoreType.DMA((2, 4)),
            pltpu.SemaphoreType.DMA((4,)),
        ],
        [HBM, HBM, HBM, HBM, VMEM],
        mib=60,
    )(counts, features.reshape(rows, width), cotangent.reshape(rows, width))
    every = SLABS + ("ch",)
    ups = [(i, i + 1) for i in range(n_slab - 1)]
    straight = [(2 * i + c, 2 * j + c) for i, j in ups for c in range(2)]
    across = [(2 * i + c, 2 * j + 1 - c) for i, j in ups for c in range(2)]
    before = lax.ppermute(high, every, straight)
    before_other = lax.ppermute(high, every, across)
    after = lax.ppermute(low, every, [(j, i) for i, j in straight])
    after_other = lax.ppermute(low, every, [(j, i) for i, j in across])
    own_other = lax.ppermute(own, "ch", [(0, 1), (1, 0)])
    table = lax.all_to_all(sent, SLABS, 0, 0, tiled=True)

    cube = (4, 4, 4, slots, width)
    face = (4, 4, slots, width)
    grid_shape = (6, 6, 6, slots, 2 * width)
    grid = call(
        halo_kernel,
        jax.ShapeDtypeStruct(grid_shape, BF16),
        [SMEM, VMEM] + [ANY] * 6,
        [
            pltpu.VMEM((4, 4, slots, 2 * width), BF16),
            pltpu.VMEM((4, 4, slots, 2 * width), BF16),
            pltpu.VMEM((27, slots, 3 * slots), F32),
            pltpu.SemaphoreType.DMA((6,)),
        ],
        flops=10**9,
    )(
        core,
        neighbours,
        own.reshape(cube),
        own_other.reshape(cube),
        before.reshape(face),
        before_other.reshape(face),
        after.reshape(face),
        after_other.reshape(face),
    )

    weight_term, norm = call(
        weight_grad_kernel,
        [
            jax.ShapeDtypeStruct((3, 9, width, 2 * width), BF16),
            jax.ShapeDtypeStruct((8, 128), F32),
        ],
        [SMEM] + [VMEM] * 5,
        [
            pltpu.VMEM((4 * width, 16 * slots), BF16),
            pltpu.VMEM((3, width, 2 * width), F32),
        ],
        flops=2 * rows * 27 * width * 2 * width,
    )(counts, table, gain_row, shift_row, values, grid)
    piece = 27 * width // n_plane
    parts = lax.all_to_all(
        weight_term.reshape(n_plane, piece, 2 * width), PLANE, 0, 0, tiled=True
    )

    grad_pre, sums = call(
        act_grad_kernel,
        [
            jax.ShapeDtypeStruct((voxels, slots, width), F32),
            jax.ShapeDtypeStruct((1, 2 * width), F32),
        ],
        [SMEM] + [VMEM] * 6,
        [pltpu.VMEM((4, 16, slots, width), F32)],
        flops=2 * rows * 27 * width * 2 * width,
    )(
        counts,
        norm,
        gain_row,
        shift_row,
        values,
        weight.reshape(3, 9, width, 2 * width),
        grid,
    )

    part = jnp.sum(parts.astype(F32), axis=0).reshape(n_line, piece // n_line, 2 * width)
    part = jnp.concatenate(
        [part, jnp.broadcast_to(sums.reshape(1, 1, 2 * width), (n_line, 1, 2 * width))], axis=1
    )
    part = jnp.sum(lax.all_to_all(part, "z", 0, 0, tiled=True), axis=0)
    final, line_sums = part[:-1].astype(BF16), part[-1:]
    line = jnp.broadcast_to(final[None], (n_line,) + final.shape)
    line = lax.all_to_all(line, "z", 0, 0, tiled=True).reshape(piece, 2 * width)
    split = []
    rest = line_sums
    for _ in range(3):
        top = lax.reduce_precision(rest, 8, 7)
        split.append(top.astype(BF16))
        rest = rest - top
    line = jnp.concatenate([line] + split + [jnp.zeros((5, 2 * width), BF16)], axis=0)
    plane = jnp.broadcast_to(line[None], (n_plane,) + line.shape)
    plane = lax.all_to_all(plane, PLANE, 0, 0, tiled=True)
    grad_features, grad_weight, totals = call(
        last_kernel,
        [
            jax.ShapeDtypeStruct((rows, width), BF16),
            jax.ShapeDtypeStruct((27 * width, 2 * width), F32),
            jax.ShapeDtypeStruct((2, width), F32),
        ],
        [SMEM] + [VMEM] * 6,
        [
            pltpu.VMEM((rows, width), BF16),
            pltpu.VMEM((27 * width, 2 * width), F32),
            pltpu.SemaphoreType.DMA((4,)),
            pltpu.SemaphoreType.DMA((n_plane,)),
        ],
        [HBM, HBM, VMEM],
    )(
        counts,
        norm,
        gain_row,
        plane,
        features.reshape(rows, width),
        cotangent.reshape(rows, width),
        grad_pre.reshape(rows, width),
    )
    return (
        grad_features.reshape(features.shape),
        grad_weight.reshape(27, width, 2 * width),
        totals[0],
        totals[1],
    )


def solution(mesh):
    slabs = mesh.devices.shape[0]
    inner = Mesh(mesh.devices.reshape(CUT[slabs] + (2,)), SLABS + ("ch",))
    in_specs = (
        P(SLABS, None, "ch"),
        P(SLABS, None, "ch"),
        P(None, "ch", None),
        P("ch"),
        P("ch"),
        P(SLABS),
        P(SLABS, None),
    )
    out_specs = (P(SLABS, None, "ch"), P(None, "ch", None), P("ch"), P("ch"))
    return jax.shard_map(body, mesh=inner, in_specs=in_specs, out_specs=out_specs, check_vma=False)
```

```python
import functools

import jax
import jax.numpy as jnp
from jax import lax
from jax.experimental import pallas as pl
from jax.experimental.pallas import tpu as pltpu
from jax.sharding import Mesh
from jax.sharding import PartitionSpec as P

GROUP_CH = 8
CUT = {128: (8, 4, 4), 8: (2, 2, 2), 4: (2, 2, 1)}
SLABS = ("z", "x", "y")
PLANE = ("x", "y")
F32 = jnp.float32
BF16 = jnp.bfloat16
VMEM = pl.BlockSpec(memory_space=pltpu.VMEM)
SMEM = pl.BlockSpec(memory_space=pltpu.SMEM)
HBM = pl.BlockSpec(memory_space=pltpu.HBM)
ANY = pl.BlockSpec(memory_space=pl.ANY)


def call(kernel, out_shape, in_specs, scratch=(), out_specs=VMEM, flops=0, mib=52, aliases=None):
    if isinstance(out_shape, (list, tuple)) and out_specs is VMEM:
        out_specs = [VMEM] * len(out_shape)
    return pl.pallas_call(
        kernel,
        out_shape=out_shape,
        in_specs=in_specs,
        out_specs=out_specs,
        scratch_shapes=list(scratch),
        input_output_aliases=aliases or {},
        compiler_params=pltpu.CompilerParams(vmem_limit_bytes=mib * 1024 * 1024),
        cost_estimate=pl.CostEstimate(flops=flops, bytes_accessed=0, transcendentals=0),
    )


def exact_dot(left, right):
    return jnp.dot(left, right, precision=lax.Precision.HIGHEST, preferred_element_type=F32)


def iota(shape, dim):
    return lax.broadcasted_iota(jnp.int32, shape, dim)


def turned(rows_ref, out_ref):
    slots = out_ref.shape[1]
    for voxel in range(64):
        out_ref[voxel] = rows_ref[pl.ds(voxel, slots, stride=64), :].astype(out_ref.dtype)


def fetch(source, target, sems, pieces):
    step = source.shape[0] // pieces
    copies = [
        pltpu.make_async_copy(
            source.at[pl.ds(at * step, step)], target.at[pl.ds(at * step, step)], sems.at[at]
        )
        for at in range(pieces)
    ]
    for copy in copies:
        copy.start()
    return copies


def widen(copies, held_ref, rows_ref):
    step = held_ref.shape[0] // len(copies)
    for at, copy in enumerate(copies):
        copy.wait()
        rows = slice(at * step, at * step + step)
        rows_ref[rows, :] = held_ref[rows, :].astype(F32)


def turn_kernel(in_hbm, own_hbm, low_hbm, high_hbm, held_ref, rows_ref, own_ref, sems, out_sems):
    widen(fetch(in_hbm, held_ref, sems, 4), held_ref, rows_ref)
    turned(rows_ref, own_ref)
    sends = [
        pltpu.make_async_copy(own_ref, own_hbm, out_sems.at[0]),
        pltpu.make_async_copy(own_ref.at[0:16], low_hbm, out_sems.at[1]),
        pltpu.make_async_copy(own_ref.at[48:64], high_hbm, out_sems.at[2]),
    ]
    for send in sends:
        send.start()
    for send in sends:
        send.wait()


def sums_kernel(counts_ref, values_hbm, sent_ref, held_ref, rows_ref, sems):
    slots = held_ref.shape[0] // 64
    count = counts_ref[0]
    widen(fetch(values_hbm, held_ref, sems, 4), held_ref, rows_ref)

    def over_slots(term):
        total = jnp.zeros((8, 128), F32)
        for slot in range(slots):
            rows = term(rows_ref[slot * 64 : slot * 64 + 64, :]).reshape(8, 8, 128).sum(axis=0)
            total = total + jnp.where(slot < count, rows, 0.0)
        return jnp.broadcast_to(jnp.sum(total, axis=0, keepdims=True), (8, 128))

    lane_in, lane_out = iota((128, 128), 0), iota((128, 128), 1)
    same = (lane_in // GROUP_CH == lane_out // GROUP_CH).astype(F32)
    to_sum = (lane_in // GROUP_CH == lane_out).astype(F32)
    to_square = (lane_in // GROUP_CH + 16 == lane_out).astype(F32)
    total = over_slots(lambda rows: rows)
    entries = count.astype(F32) * (64.0 * GROUP_CH)
    mean = (exact_dot(total, same) / entries)[0:1]

    def centred(rows):
        apart = rows - mean
        return apart * apart

    squares = over_slots(centred)
    row = exact_dot(total, to_sum) + exact_dot(squares, to_square)
    row = row + jnp.where(iota((8, 128), 1) == 32, count.astype(F32), 0.0)
    sent_ref[...] = jnp.broadcast_to(row[0:1].reshape(1, 1, 128), sent_ref.shape)


def lanes_of(core):
    mine = pl.ds(pl.multiple_of(core * 128, 128), 128)
    other = pl.ds(pl.multiple_of((1 - core) * 128, 128), 128)
    return mine, other


def side(at):
    return -1 if at == 0 else (1 if at == 5 else 0)


def source(at):
    return {0: 4, 5: 1}.get(at, at)


def offset_of(dx, b, c):
    return 9 * (dx + 1) + 3 * (side(b) + 1) + side(c) + 1


def choose(near, offset, first, last):
    columns = iota((near.shape[0], last - first), 1) + first
    return (near[:, offset : offset + 1] == columns).astype(F32).astype(BF16)


def halo_kernel(core_ref, near_ref, own_ref, own_other_ref, middle_hbm, middle_ref, sems, out_sems):
    slots = near_ref.shape[0]
    mine, other = lanes_of(core_ref[0])
    centre = middle_ref.at[:, 1:5, 1:5]
    copies = [
        pltpu.make_async_copy(own_ref, centre.at[:, :, :, :, mine], sems.at[0]),
        pltpu.make_async_copy(own_other_ref, centre.at[:, :, :, :, other], sems.at[1]),
    ]
    for copy in copies:
        copy.start()
    near = near_ref[...]
    places = [(b, c) for b in range(6) for c in range(6) if side(b) or side(c)]
    picks = {
        offset: choose(near, offset, slots, 2 * slots)
        for offset in sorted({offset_of(0, b, c) for b, c in places})
    }
    for copy in copies:
        copy.wait()
    sends = []
    for plane in range(4):
        for b, c in places:
            middle_ref[plane, b, c] = jnp.dot(
                picks[offset_of(0, b, c)],
                middle_ref[plane, source(b), source(c)],
                preferred_element_type=F32,
            ).astype(BF16)
        sends.append(
            pltpu.make_async_copy(middle_ref.at[plane], middle_hbm.at[plane], out_sems.at[plane])
        )
        sends[-1].start()
    for send in sends:
        send.wait()


def window(plane_ref, turn):
    slots = plane_ref.shape[2]
    block = plane_ref[pl.ds(2 - turn // 3, 4), pl.ds(2 - turn % 3, 4)]
    return block.reshape(16 * slots, 256)


def planes_of(plane):
    return max(0, plane - 2), min(3, plane) + 1


def weight_grad_kernel(
    counts_ref,
    table_ref,
    gain_ref,
    shift_ref,
    values_hbm,
    middle_hbm,
    out_hbm,
    part_hbm,
    edge_ref,
    norm_ref,
    held_ref,
    rows_ref,
    middle_ref,
    act_ref,
    total_ref,
    out_ref,
    part_ref,
    sems,
    plane_sems,
    out_sems,
):
    slots = middle_ref.shape[3]
    copies = fetch(values_hbm, held_ref, sems, 4)
    planes = fetch(middle_hbm, middle_ref, plane_sems, 4)
    table = table_ref[...]
    held = jnp.sum(table, axis=0)
    voxels = held[:, 32:33] * (64.0 * GROUP_CH)
    entries = table[:, :, 32:33] * (64.0 * GROUP_CH)
    mean = held / voxels
    apart = table / entries - mean.reshape(1, 1, 128)
    between = jnp.sum(apart * apart * entries, axis=0)
    lane_in, lane_out = iota((128, 128), 0), iota((128, 128), 1)
    from_sum = (lane_in == lane_out // GROUP_CH).astype(F32)
    from_square = (lane_in == lane_out // GROUP_CH + 16).astype(F32)

    def spread(row, matrix):
        return exact_dot(jnp.broadcast_to(row, (8, 128)), matrix)[0:1]

    mean = spread(mean, from_sum)
    variance = (spread(between, from_sum) + spread(held, from_square)) / voxels
    rstd = lax.rsqrt(variance + 1e-05)
    norm_ref[0:1, :] = mean
    norm_ref[1:2, :] = rstd
    norm_ref[2:3, :] = jnp.broadcast_to(voxels, (1, 128))
    norm_ref[3:8, :] = jnp.zeros((5, 128), F32)
    gain, shift = gain_ref[...], shift_ref[...]
    live = iota((slots, 128), 0) < counts_ref[0]
    widen(copies, held_ref, rows_ref)
    for plane in range(4):
        pieces = []
        for voxel in range(plane * 16, plane * 16 + 16):
            normed = (rows_ref[pl.ds(voxel, slots, stride=64), :] - mean) * rstd
            pre = normed * gain + shift
            pieces.append(jnp.where(live, pre / (1.0 + jnp.exp(-pre)), 0.0))
        rows = jnp.concatenate(pieces, axis=0)
        act_ref[plane * 128 : plane * 128 + 128, :] = rows.T.astype(BF16)
    edge_ref[0] = act_ref[0:128, :]
    edge_ref[1] = act_ref[384:512, :]
    sends = []
    for turn in range(9):
        seen = set()
        for plane in range(1, 5):
            if turn == 0:
                planes[plane - 1].wait()
            first, last = planes_of(plane)
            part = jnp.dot(
                act_ref[first * 128 : last * 128, :],
                window(middle_ref.at[plane - 1], turn),
                preferred_element_type=F32,
            )
            for at in range(first, last):
                step = at - plane + 2
                term = part[(at - first) * 128 : (at - first) * 128 + 128]
                if step in seen:
                    total_ref[step] += term
                else:
                    total_ref[step] = term
                    seen.add(step)
        out_ref[turn] = total_ref[1].astype(BF16)
        part_ref[0, turn] = total_ref[0]
        part_ref[1, turn] = total_ref[2]
        sends += [
            pltpu.make_async_copy(out_ref.at[turn], out_hbm.at[1, turn], out_sems.at[0, turn]),
            pltpu.make_async_copy(part_ref.at[0, turn], part_hbm.at[0, turn], out_sems.at[1, turn]),
            pltpu.make_async_copy(part_ref.at[1, turn], part_hbm.at[1, turn], out_sems.at[2, turn]),
        ]
        for send in sends[-3:]:
            send.start()
    for send in sends:
        send.wait()


def edge_kernel(
    core_ref,
    near_ref,
    edge_ref,
    before_ref,
    before_other_ref,
    after_ref,
    after_other_ref,
    middle_hbm,
    part_hbm,
    in_hbm,
    out_hbm,
    sides_hbm,
    face_ref,
    inner_ref,
    sides_ref,
    part_ref,
    out_ref,
    sems,
    part_sems,
    out_sems,
    side_sems,
):
    slots = near_ref.shape[0]
    mine, other = lanes_of(core_ref[0])
    copies = [
        pltpu.make_async_copy(before_ref, face_ref.at[0, :, :, :, mine], sems.at[0]),
        pltpu.make_async_copy(before_other_ref, face_ref.at[0, :, :, :, other], sems.at[1]),
        pltpu.make_async_copy(after_ref, face_ref.at[1, :, :, :, mine], sems.at[2]),
        pltpu.make_async_copy(after_other_ref, face_ref.at[1, :, :, :, other], sems.at[3]),
        pltpu.make_async_copy(middle_hbm.at[3, 1:5, 1:5], inner_ref.at[0], sems.at[4]),
        pltpu.make_async_copy(middle_hbm.at[0, 1:5, 1:5], inner_ref.at[1], sems.at[5]),
    ]
    for copy in copies:
        copy.start()
    parts = [
        pltpu.make_async_copy(part_hbm.at[which], part_ref.at[which], part_sems.at[which])
        for which in range(2)
    ]
    for part in parts:
        part.start()
    near = near_ref[...]
    places = [(b, c) for b in range(6) for c in range(6)]
    sends = []
    for which, dx in enumerate((-1, 1)):
        lowest = which * slots
        picks = {
            offset: choose(near, offset, lowest, lowest + 2 * slots)
            for offset in sorted({offset_of(dx, b, c) for b, c in places})
        }
        if which == 0:
            for copy in copies:
                copy.wait()
        for b, c in places:
            outer = face_ref[which, source(b) - 1, source(c) - 1]
            inner = inner_ref[which, source(b) - 1, source(c) - 1]
            table = [outer, inner] if which == 0 else [inner, outer]
            sides_ref[which, b, c] = jnp.dot(
                picks[offset_of(dx, b, c)],
                jnp.concatenate(table, axis=0),
                preferred_element_type=F32,
            ).astype(BF16)
        sends.append(
            pltpu.make_async_copy(sides_ref.at[which], sides_hbm.at[which], side_sems.at[which])
        )
        sends[-1].start()
        parts[which].wait()
    for turn in range(9):
        for which in range(2):
            term = jnp.dot(
                edge_ref[which], window(sides_ref.at[which], turn), preferred_element_type=F32
            )
            out_ref[1 - which, turn] = (part_ref[1 - which, turn] + term).astype(BF16)
            sends.append(
                pltpu.make_async_copy(
                    out_ref.at[1 - which, turn],
                    out_hbm.at[2 - 2 * which, turn],
                    out_sems.at[which, turn],
                )
            )
            sends[-1].start()
    for send in sends:
        send.wait()


def act_grad_kernel(
    counts_ref,
    norm_ref,
    gain_ref,
    shift_ref,
    values_ref,
    weight_ref,
    middle_ref,
    sides_ref,
    out_ref,
    sums_ref,
    total_ref,
    rows_ref,
):
    slots = middle_ref.shape[3]
    total_ref[...] = jnp.zeros_like(total_ref)
    rows_ref[...] = values_ref[...].astype(F32)

    @pl.loop(0, 9)
    def _(turn):
        for plane in range(6):
            first, last = planes_of(plane)
            low, high = first - plane + 2, last - plane + 2
            rows = sides_ref.at[plane // 5] if plane in (0, 5) else middle_ref.at[plane - 1]
            part = lax.dot_general(
                window(rows, turn),
                weight_ref[low:high, turn].reshape((high - low) * 128, 256),
                (((1,), (1,)), ((), ())),
                preferred_element_type=F32,
            )
            for at in range(first, last):
                term = part[:, (at - first) * 128 : (at - first) * 128 + 128]
                total_ref[at] += term.reshape(16, slots, 128)

    mean, rstd = norm_ref[0:1, :], norm_ref[1:2, :]
    gain, shift = gain_ref[...], shift_ref[...]
    live = iota((slots, 128), 0) < counts_ref[0]
    shift_sum = jnp.zeros((8, 128), F32)
    gain_sum = jnp.zeros((8, 128), F32)
    for voxel in range(64):
        normed = (rows_ref[pl.ds(voxel, slots, stride=64), :] - mean) * rstd
        pre = normed * gain + shift
        sig = 1.0 / (1.0 + jnp.exp(-pre))
        grad = total_ref[voxel // 16, voxel % 16] * sig * (1.0 + pre * (1.0 - sig))
        grad = jnp.where(live, grad, 0.0)
        out_ref[voxel] = grad
        shift_sum = shift_sum + grad.reshape(slots // 8, 8, 128).sum(axis=0)
        gain_sum = gain_sum + (grad * normed).reshape(slots // 8, 8, 128).sum(axis=0)
    sums_ref[:, 0:128] = jnp.sum(shift_sum, axis=0, keepdims=True)
    sums_ref[:, 128:256] = jnp.sum(gain_sum, axis=0, keepdims=True)


def last_kernel(
    counts_ref,
    norm_ref,
    gain_ref,
    plane_ref,
    values_ref,
    cotangent_ref,
    grad_ref,
    out_hbm,
    weight_hbm,
    sums_ref,
    out_ref,
    weight_ref,
    out_sems,
    weight_sems,
):
    slots = grad_ref.shape[0] // 64
    pieces = plane_ref.shape[0]
    piece = weight_ref.shape[0] // pieces
    copies = []
    totals = jnp.zeros((1, 256), F32)
    for at in range(pieces):
        block = plane_ref[at].astype(F32)
        rows = pl.ds(at * piece, piece)
        weight_ref[rows] = block[0:piece]
        totals = totals + (block[piece : piece + 1] + block[piece + 1 : piece + 2])
        totals = totals + block[piece + 2 : piece + 3]
        copies.append(
            pltpu.make_async_copy(weight_ref.at[rows], weight_hbm.at[rows], weight_sems.at[at])
        )
        copies[-1].start()
    shift_sum, gain_sum = totals[:, 0:128], totals[:, 128:256]
    sums_ref[0:1] = gain_sum
    sums_ref[1:2] = shift_sum
    mean, rstd, voxels = norm_ref[0:1, :], norm_ref[1:2, :], norm_ref[2:3, :]
    gain = gain_ref[...]
    lane_in, lane_out = iota((128, 128), 0), iota((128, 128), 1)
    same = (lane_in // GROUP_CH == lane_out // GROUP_CH).astype(F32)

    def grouped(row):
        return exact_dot(jnp.broadcast_to(row, (8, 128)), same)[0:1]

    first = grouped(gain * shift_sum) / voxels
    second = grouped(gain * gain_sum) / voxels
    chunk = slots // 4
    for slot in range(slots):
        rows = slice(slot * 64, slot * 64 + 64)
        normed = (values_ref[rows, :].astype(F32) - mean) * rstd
        grad = grad_ref[pl.ds(slot, 64, stride=slots), :]
        inner = gain * grad - first - normed * second
        result = cotangent_ref[rows, :].astype(F32) + rstd * inner
        out_ref[rows, :] = jnp.where(slot < counts_ref[0], result, 0.0).astype(BF16)
        if slot % chunk == chunk - 1:
            at = slot // chunk
            rows = pl.ds(at * chunk * 64, chunk * 64)
            copies.append(
                pltpu.make_async_copy(out_ref.at[rows], out_hbm.at[rows], out_sems.at[at])
            )
            copies[-1].start()
    for copy in copies:
        copy.wait()


def body(features, cotangent, weight, gain, shift, counts, neighbours):
    slots, voxels, width = features.shape
    rows = slots * voxels
    n_plane = lax.axis_size("x") * lax.axis_size("y")
    n_line = lax.axis_size("z")
    n_slab = n_plane * n_line
    core = lax.axis_index("ch").astype(jnp.int32).reshape(1)
    turned_shape = jax.ShapeDtypeStruct((voxels, slots, width), BF16)
    face_shape = jax.ShapeDtypeStruct((16, slots, width), BF16)
    gain_row, shift_row = gain.reshape(1, width), shift.reshape(1, width)
    value_rows = features.reshape(rows, width)
    cotangent_rows = cotangent.reshape(rows, width)
    work = 2 * rows * 27 * width * 2 * width

    sent = call(
        sums_kernel,
        jax.ShapeDtypeStruct((n_slab, 1, 128), F32),
        [SMEM, HBM],
        [
            pltpu.VMEM((rows, width), BF16),
            pltpu.VMEM((rows, width), F32),
            pltpu.SemaphoreType.DMA((4,)),
        ],
        mib=60,
    )(counts, value_rows)
    table = lax.all_to_all(sent, SLABS, 0, 0, tiled=True)
    own, low, high = call(
        turn_kernel,
        [turned_shape, face_shape, face_shape],
        [HBM],
        [
            pltpu.VMEM((rows, width), BF16),
            pltpu.VMEM((rows, width), F32),
            pltpu.VMEM(turned_shape.shape, BF16),
            pltpu.SemaphoreType.DMA((4,)),
            pltpu.SemaphoreType.DMA((3,)),
        ],
        [HBM] * 3,
        mib=60,
    )(cotangent_rows)
    own_other = lax.ppermute(own, "ch", [(0, 1), (1, 0)])

    cube = (4, 4, 4, slots, width)
    face = (4, 4, slots, width)
    middle_shape = (4, 6, 6, slots, 2 * width)
    middle = call(
        halo_kernel,
        jax.ShapeDtypeStruct(middle_shape, BF16),
        [SMEM, VMEM, ANY, ANY],
        [
            pltpu.VMEM(middle_shape, BF16),
            pltpu.SemaphoreType.DMA((2,)),
            pltpu.SemaphoreType.DMA((4,)),
        ],
        HBM,
        flops=10**9,
    )(core, neighbours, own.reshape(cube), own_other.reshape(cube))

    table, middle, low, high = lax.optimization_barrier((table, middle, low, high))
    every = SLABS + ("ch",)
    ups = [(i, i + 1) for i in range(n_slab - 1)]
    straight = [(2 * i + c, 2 * j + c) for i, j in ups for c in range(2)]
    across = [(2 * i + c, 2 * j + 1 - c) for i, j in ups for c in range(2)]
    before = lax.ppermute(high, every, straight)
    before_other = lax.ppermute(high, every, across)
    after = lax.ppermute(low, every, [(j, i) for i, j in straight])
    after_other = lax.ppermute(low, every, [(j, i) for i, j in across])

    term_shape = jax.ShapeDtypeStruct((3, 9, width, 2 * width), BF16)
    part_shape = jax.ShapeDtypeStruct((2, 9, width, 2 * width), F32)
    weight_term, part_term, edge, norm = call(
        weight_grad_kernel,
        [
            term_shape,
            part_shape,
            jax.ShapeDtypeStruct((2, width, 16 * slots), BF16),
            jax.ShapeDtypeStruct((8, 128), F32),
        ],
        [SMEM, VMEM, VMEM, VMEM, HBM, HBM],
        [
            pltpu.VMEM((rows, width), BF16),
            pltpu.VMEM((rows, width), F32),
            pltpu.VMEM(middle_shape, BF16),
            pltpu.VMEM((4 * width, 16 * slots), BF16),
            pltpu.VMEM((3, width, 2 * width), F32),
            pltpu.VMEM((9, width, 2 * width), BF16),
            pltpu.VMEM(part_shape.shape, F32),
            pltpu.SemaphoreType.DMA((4,)),
            pltpu.SemaphoreType.DMA((4,)),
            pltpu.SemaphoreType.DMA((3, 9)),
        ],
        [HBM, HBM, VMEM, VMEM],
        flops=work,
    )(counts, table, gain_row, shift_row, value_rows, middle)
    sides_shape = jax.ShapeDtypeStruct((2, 6, 6, slots, 2 * width), BF16)
    weight_term, sides = call(
        edge_kernel,
        [term_shape, sides_shape],
        [SMEM, VMEM, VMEM] + [ANY] * 4 + [HBM] * 3,
        [
            pltpu.VMEM((2, 4, 4, slots, 2 * width), BF16),
            pltpu.VMEM((2, 4, 4, slots, 2 * width), BF16),
            pltpu.VMEM(sides_shape.shape, BF16),
            pltpu.VMEM(part_shape.shape, F32),
            pltpu.VMEM((2, 9, width, 2 * width), BF16),
            pltpu.SemaphoreType.DMA((6,)),
            pltpu.SemaphoreType.DMA((2,)),
            pltpu.SemaphoreType.DMA((2, 9)),
            pltpu.SemaphoreType.DMA((2,)),
        ],
        [HBM, HBM],
        aliases={9: 0},
        flops=work // 6,
    )(
        core,
        neighbours,
        edge,
        before.reshape(face),
        before_other.reshape(face),
        after.reshape(face),
        after_other.reshape(face),
        middle,
        part_term,
        weight_term,
    )
    piece = 27 * width // n_plane
    parts = lax.all_to_all(
        weight_term.reshape(n_plane, piece, 2 * width), PLANE, 0, 0, tiled=True
    )

    grad_pre, sums = call(
        act_grad_kernel,
        [
            jax.ShapeDtypeStruct((voxels, slots, width), F32),
            jax.ShapeDtypeStruct((1, 2 * width), F32),
        ],
        [SMEM] + [VMEM] * 7,
        [pltpu.VMEM((4, 16, slots, width), F32), pltpu.VMEM((rows, width), F32)],
        flops=work,
    )(
        counts,
        norm,
        gain_row,
        shift_row,
        value_rows,
        weight.reshape(3, 9, width, 2 * width),
        middle,
        sides,
    )

    part = jnp.sum(parts.astype(F32), axis=0).reshape(n_line, piece // n_line, 2 * width)
    part = jnp.concatenate(
        [part, jnp.broadcast_to(sums.reshape(1, 1, 2 * width), (n_line, 1, 2 * width))], axis=1
    )
    part = jnp.sum(lax.all_to_all(part, "z", 0, 0, tiled=True), axis=0)
    final, line_sums = part[:-1].astype(BF16), part[-1:]
    line = jnp.broadcast_to(final[None], (n_line,) + final.shape)
    line = lax.all_to_all(line, "z", 0, 0, tiled=True).reshape(piece, 2 * width)
    split = []
    rest = line_sums
    for _ in range(3):
        top = lax.reduce_precision(rest, 8, 7)
        split.append(top.astype(BF16))
        rest = rest - top
    line = jnp.concatenate([line] + split + [jnp.zeros((5, 2 * width), BF16)], axis=0)
    plane = jnp.broadcast_to(line[None], (n_plane,) + line.shape)
    plane = lax.all_to_all(plane, PLANE, 0, 0, tiled=True)
    grad_features, grad_weight, totals = call(
        last_kernel,
        [
            jax.ShapeDtypeStruct((rows, width), BF16),
            jax.ShapeDtypeStruct((27 * width, 2 * width), F32),
            jax.ShapeDtypeStruct((2, width), F32),
        ],
        [SMEM] + [VMEM] * 6,
        [
            pltpu.VMEM((rows, width), BF16),
            pltpu.VMEM((27 * width, 2 * width), F32),
            pltpu.SemaphoreType.DMA((4,)),
            pltpu.SemaphoreType.DMA((n_plane,)),
        ],
        [HBM, HBM, VMEM],
        mib=20,
    )(
        counts,
        norm,
        gain_row,
        plane,
        value_rows,
        cotangent_rows,
        grad_pre.reshape(rows, width),
    )
    return (
        grad_features.reshape(features.shape),
        grad_weight.reshape(27, width, 2 * width),
        totals[0],
        totals[1],
    )


def solution(mesh):
    slabs = mesh.devices.shape[0]
    inner = Mesh(mesh.devices.reshape(CUT[slabs] + (2,)), SLABS + ("ch",))
    in_specs = (
        P(SLABS, None, "ch"),
        P(SLABS, None, "ch"),
        P(None, "ch", None),
        P("ch"),
        P("ch"),
        P(SLABS),
        P(SLABS, None),
    )
    out_specs = (P(SLABS, None, "ch"), P(None, "ch", None), P("ch"), P("ch"))
    return jax.shard_map(body, mesh=inner, in_specs=in_specs, out_specs=out_specs, check_vma=False)
```

```python
import functools

import jax
import jax.numpy as jnp
from jax import lax
from jax.experimental import pallas as pl
from jax.experimental.pallas import tpu as pltpu
from jax.sharding import Mesh
from jax.sharding import PartitionSpec as P

GROUP_CH = 8
CUT = {128: (8, 4, 4), 8: (2, 2, 2), 4: (2, 2, 1)}
SLABS = ("z", "x", "y")
PLANE = ("x", "y")
F32 = jnp.float32
BF16 = jnp.bfloat16
VMEM = pl.BlockSpec(memory_space=pltpu.VMEM)
SMEM = pl.BlockSpec(memory_space=pltpu.SMEM)
HBM = pl.BlockSpec(memory_space=pltpu.HBM)
ANY = pl.BlockSpec(memory_space=pl.ANY)


def call(kernel, out_shape, in_specs, scratch=(), out_specs=VMEM, flops=0, mib=52, aliases=None):
    if isinstance(out_shape, (list, tuple)) and out_specs is VMEM:
        out_specs = [VMEM] * len(out_shape)
    return pl.pallas_call(
        kernel,
        out_shape=out_shape,
        in_specs=in_specs,
        out_specs=out_specs,
        scratch_shapes=list(scratch),
        input_output_aliases=aliases or {},
        compiler_params=pltpu.CompilerParams(vmem_limit_bytes=mib * 1024 * 1024),
        cost_estimate=pl.CostEstimate(flops=flops, bytes_accessed=0, transcendentals=0),
    )


def exact_dot(left, right):
    return jnp.dot(left, right, precision=lax.Precision.HIGHEST, preferred_element_type=F32)


def iota(shape, dim):
    return lax.broadcasted_iota(jnp.int32, shape, dim)


def turned(rows_ref, out_ref):
    slots = out_ref.shape[1]
    for voxel in range(64):
        out_ref[voxel] = rows_ref[pl.ds(voxel, slots, stride=64), :].astype(out_ref.dtype)


def fetch(source, target, sems, pieces):
    step = source.shape[0] // pieces
    copies = [
        pltpu.make_async_copy(
            source.at[pl.ds(at * step, step)], target.at[pl.ds(at * step, step)], sems.at[at]
        )
        for at in range(pieces)
    ]
    for copy in copies:
        copy.start()
    return copies


def widen(copies, held_ref, rows_ref):
    step = held_ref.shape[0] // len(copies)
    for at, copy in enumerate(copies):
        copy.wait()
        rows = slice(at * step, at * step + step)
        rows_ref[rows, :] = held_ref[rows, :].astype(F32)


def turn_kernel(
    core_ref, in_hbm, own_hbm, give_hbm, keep_hbm, held_ref, rows_ref, own_ref, sems, out_sems
):
    copies = fetch(in_hbm, held_ref, sems, 4)
    core = core_ref[0]
    widen(copies, held_ref, rows_ref)
    turned(rows_ref, own_ref)
    sends = [
        pltpu.make_async_copy(own_ref.at[pl.ds(48 * core, 16)], give_hbm, out_sems.at[0]),
        pltpu.make_async_copy(own_ref.at[pl.ds(48 - 48 * core, 16)], keep_hbm, out_sems.at[1]),
        pltpu.make_async_copy(own_ref, own_hbm, out_sems.at[2]),
    ]
    for send in sends:
        send.start()
    for send in sends:
        send.wait()


def sums_kernel(counts_ref, values_hbm, sent_ref, held_ref, rows_ref, sems):
    slots = held_ref.shape[0] // 64
    count = counts_ref[0]
    widen(fetch(values_hbm, held_ref, sems, 4), held_ref, rows_ref)

    def over_slots(term):
        total = jnp.zeros((8, 128), F32)
        for slot in range(slots):
            rows = term(rows_ref[slot * 64 : slot * 64 + 64, :]).reshape(8, 8, 128).sum(axis=0)
            total = total + jnp.where(slot < count, rows, 0.0)
        return jnp.broadcast_to(jnp.sum(total, axis=0, keepdims=True), (8, 128))

    lane_in, lane_out = iota((128, 128), 0), iota((128, 128), 1)
    same = (lane_in // GROUP_CH == lane_out // GROUP_CH).astype(F32)
    to_sum = (lane_in // GROUP_CH == lane_out).astype(F32)
    to_square = (lane_in // GROUP_CH + 16 == lane_out).astype(F32)
    total = over_slots(lambda rows: rows)
    entries = count.astype(F32) * (64.0 * GROUP_CH)
    mean = (exact_dot(total, same) / entries)[0:1]

    def centred(rows):
        apart = rows - mean
        return apart * apart

    squares = over_slots(centred)
    row = exact_dot(total, to_sum) + exact_dot(squares, to_square)
    row = row + jnp.where(iota((8, 128), 1) == 32, count.astype(F32), 0.0)
    sent_ref[...] = jnp.broadcast_to(row[0:1].reshape(1, 1, 128), sent_ref.shape)


def lanes_of(core):
    mine = pl.ds(pl.multiple_of(core * 128, 128), 128)
    other = pl.ds(pl.multiple_of((1 - core) * 128, 128), 128)
    return mine, other


def side(at):
    return -1 if at == 0 else (1 if at == 5 else 0)


def source(at):
    return {0: 4, 5: 1}.get(at, at)


def offset_of(dx, b, c):
    return 9 * (dx + 1) + 3 * (side(b) + 1) + side(c) + 1


def choose(near, offset, first, last):
    columns = iota((near.shape[0], last - first), 1) + first
    return (near[:, offset : offset + 1] == columns).astype(F32).astype(BF16)


def halo_kernel(core_ref, near_ref, own_ref, own_other_ref, middle_hbm, middle_ref, sems, out_sems):
    slots = near_ref.shape[0]
    mine, other = lanes_of(core_ref[0])
    centre = middle_ref.at[:, 1:5, 1:5]
    copies = [
        pltpu.make_async_copy(own_ref, centre.at[:, :, :, :, mine], sems.at[0]),
        pltpu.make_async_copy(own_other_ref, centre.at[:, :, :, :, other], sems.at[1]),
    ]
    for copy in copies:
        copy.start()
    near = near_ref[...]
    places = [(b, c) for b in range(6) for c in range(6) if side(b) or side(c)]
    picks = {
        offset: choose(near, offset, slots, 2 * slots)
        for offset in sorted({offset_of(0, b, c) for b, c in places})
    }
    for copy in copies:
        copy.wait()
    sends = []
    for plane in range(4):
        for b, c in places:
            middle_ref[plane, b, c] = jnp.dot(
                picks[offset_of(0, b, c)],
                middle_ref[plane, source(b), source(c)],
                preferred_element_type=F32,
            ).astype(BF16)
        sends.append(
            pltpu.make_async_copy(middle_ref.at[plane], middle_hbm.at[plane], out_sems.at[plane])
        )
        sends[-1].start()
    for send in sends:
        send.wait()


def window(plane_ref, turn):
    slots = plane_ref.shape[2]
    block = plane_ref[pl.ds(2 - turn // 3, 4), pl.ds(2 - turn % 3, 4)]
    return block.reshape(16 * slots, 256)


def planes_of(plane):
    return max(0, plane - 2), min(3, plane) + 1


def weight_grad_kernel(
    counts_ref,
    table_ref,
    gain_ref,
    shift_ref,
    values_hbm,
    middle_hbm,
    sides_hbm,
    out_hbm,
    norm_ref,
    held_ref,
    rows_ref,
    grid_ref,
    act_ref,
    total_ref,
    out_ref,
    sems,
    plane_sems,
    out_sems,
):
    slots = grid_ref.shape[3]
    copies = fetch(values_hbm, held_ref, sems, 4)
    sources = [sides_hbm.at[0]] + [middle_hbm.at[at] for at in range(4)] + [sides_hbm.at[1]]
    planes = [
        pltpu.make_async_copy(place, grid_ref.at[at], plane_sems.at[at])
        for at, place in enumerate(sources)
    ]
    for plane in planes:
        plane.start()
    table = table_ref[...]
    held = jnp.sum(table, axis=0)
    voxels = held[:, 32:33] * (64.0 * GROUP_CH)
    entries = table[:, :, 32:33] * (64.0 * GROUP_CH)
    mean = held / voxels
    apart = table / entries - mean.reshape(1, 1, 128)
    between = jnp.sum(apart * apart * entries, axis=0)
    lane_in, lane_out = iota((128, 128), 0), iota((128, 128), 1)
    from_sum = (lane_in == lane_out // GROUP_CH).astype(F32)
    from_square = (lane_in == lane_out // GROUP_CH + 16).astype(F32)

    def spread(row, matrix):
        return exact_dot(jnp.broadcast_to(row, (8, 128)), matrix)[0:1]

    mean = spread(mean, from_sum)
    variance = (spread(between, from_sum) + spread(held, from_square)) / voxels
    rstd = lax.rsqrt(variance + 1e-05)
    norm_ref[0:1, :] = mean
    norm_ref[1:2, :] = rstd
    norm_ref[2:3, :] = jnp.broadcast_to(voxels, (1, 128))
    norm_ref[3:8, :] = jnp.zeros((5, 128), F32)
    gain, shift = gain_ref[...], shift_ref[...]
    live = iota((slots, 128), 0) < counts_ref[0]
    widen(copies, held_ref, rows_ref)
    for plane in range(4):
        pieces = []
        for voxel in range(plane * 16, plane * 16 + 16):
            normed = (rows_ref[pl.ds(voxel, slots, stride=64), :] - mean) * rstd
            pre = normed * gain + shift
            pieces.append(jnp.where(live, pre / (1.0 + jnp.exp(-pre)), 0.0))
        rows = jnp.concatenate(pieces, axis=0)
        act_ref[plane * 128 : plane * 128 + 128, :] = rows.T.astype(BF16)
    sends = []
    for turn in range(9):
        seen = set()
        for plane in range(6):
            if turn == 0:
                planes[plane].wait()
            first, last = planes_of(plane)
            part = jnp.dot(
                act_ref[first * 128 : last * 128, :],
                window(grid_ref.at[plane], turn),
                preferred_element_type=F32,
            )
            for at in range(first, last):
                step = at - plane + 2
                term = part[(at - first) * 128 : (at - first) * 128 + 128]
                if step in seen:
                    total_ref[step] += term
                else:
                    total_ref[step] = term
                    seen.add(step)
        for step in range(3):
            out_ref[step, turn] = total_ref[step].astype(BF16)
            sends.append(
                pltpu.make_async_copy(
                    out_ref.at[step, turn], out_hbm.at[step, turn], out_sems.at[step, turn]
                )
            )
            sends[-1].start()
    for send in sends:
        send.wait()


def edge_kernel(
    core_ref,
    near_ref,
    received_ref,
    theirs_ref,
    middle_hbm,
    sides_hbm,
    face_ref,
    inner_ref,
    sides_ref,
    sems,
    side_sems,
):
    slots = near_ref.shape[0]
    core = core_ref[0]
    mine, other = lanes_of(core)
    near_face, far_face = face_ref.at[core], face_ref.at[1 - core]
    copies = [
        pltpu.make_async_copy(received_ref.at[0], near_face.at[:, :, :, mine], sems.at[0]),
        pltpu.make_async_copy(received_ref.at[1], near_face.at[:, :, :, other], sems.at[1]),
        pltpu.make_async_copy(theirs_ref.at[0], far_face.at[:, :, :, other], sems.at[2]),
        pltpu.make_async_copy(theirs_ref.at[1], far_face.at[:, :, :, mine], sems.at[3]),
        pltpu.make_async_copy(middle_hbm.at[3, 1:5, 1:5], inner_ref.at[0], sems.at[4]),
        pltpu.make_async_copy(middle_hbm.at[0, 1:5, 1:5], inner_ref.at[1], sems.at[5]),
    ]
    for copy in copies:
        copy.start()
    near = near_ref[...]
    places = [(b, c) for b in range(6) for c in range(6)]
    sends = []
    for which, dx in enumerate((-1, 1)):
        lowest = which * slots
        picks = {
            offset: choose(near, offset, lowest, lowest + 2 * slots)
            for offset in sorted({offset_of(dx, b, c) for b, c in places})
        }
        if which == 0:
            for copy in copies:
                copy.wait()
        for b, c in places:
            outer = face_ref[which, source(b) - 1, source(c) - 1]
            inner = inner_ref[which, source(b) - 1, source(c) - 1]
            table = [outer, inner] if which == 0 else [inner, outer]
            sides_ref[which, b, c] = jnp.dot(
                picks[offset_of(dx, b, c)],
                jnp.concatenate(table, axis=0),
                preferred_element_type=F32,
            ).astype(BF16)
        sends.append(
            pltpu.make_async_copy(sides_ref.at[which], sides_hbm.at[which], side_sems.at[which])
        )
        sends[-1].start()
    for send in sends:
        send.wait()


def act_grad_kernel(
    counts_ref,
    norm_ref,
    gain_ref,
    shift_ref,
    values_ref,
    weight_ref,
    middle_ref,
    sides_ref,
    out_ref,
    sums_ref,
    total_ref,
    rows_ref,
):
    slots = middle_ref.shape[3]
    total_ref[...] = jnp.zeros_like(total_ref)
    rows_ref[...] = values_ref[...].astype(F32)

    @pl.loop(0, 9)
    def _(turn):
        for plane in range(6):
            first, last = planes_of(plane)
            low, high = first - plane + 2, last - plane + 2
            rows = sides_ref.at[plane // 5] if plane in (0, 5) else middle_ref.at[plane - 1]
            part = lax.dot_general(
                window(rows, turn),
                weight_ref[low:high, turn].reshape((high - low) * 128, 256),
                (((1,), (1,)), ((), ())),
                preferred_element_type=F32,
            )
            for at in range(first, last):
                term = part[:, (at - first) * 128 : (at - first) * 128 + 128]
                total_ref[at] += term.reshape(16, slots, 128)

    mean, rstd = norm_ref[0:1, :], norm_ref[1:2, :]
    gain, shift = gain_ref[...], shift_ref[...]
    live = iota((slots, 128), 0) < counts_ref[0]
    shift_sum = jnp.zeros((8, 128), F32)
    gain_sum = jnp.zeros((8, 128), F32)
    for voxel in range(64):
        normed = (rows_ref[pl.ds(voxel, slots, stride=64), :] - mean) * rstd
        pre = normed * gain + shift
        sig = 1.0 / (1.0 + jnp.exp(-pre))
        grad = total_ref[voxel // 16, voxel % 16] * sig * (1.0 + pre * (1.0 - sig))
        grad = jnp.where(live, grad, 0.0)
        out_ref[voxel] = grad
        shift_sum = shift_sum + grad.reshape(slots // 8, 8, 128).sum(axis=0)
        gain_sum = gain_sum + (grad * normed).reshape(slots // 8, 8, 128).sum(axis=0)
    sums_ref[:, 0:128] = jnp.sum(shift_sum, axis=0, keepdims=True)
    sums_ref[:, 128:256] = jnp.sum(gain_sum, axis=0, keepdims=True)


def last_kernel(
    counts_ref,
    norm_ref,
    gain_ref,
    plane_ref,
    values_ref,
    cotangent_ref,
    grad_ref,
    out_hbm,
    weight_hbm,
    sums_ref,
    out_ref,
    weight_ref,
    out_sems,
    weight_sems,
):
    slots = grad_ref.shape[0] // 64
    pieces = plane_ref.shape[0]
    piece = weight_ref.shape[0] // pieces
    copies = []
    totals = jnp.zeros((1, 256), F32)
    for at in range(pieces):
        block = plane_ref[at].astype(F32)
        rows = pl.ds(at * piece, piece)
        weight_ref[rows] = block[0:piece]
        totals = totals + (block[piece : piece + 1] + block[piece + 1 : piece + 2])
        totals = totals + block[piece + 2 : piece + 3]
        copies.append(
            pltpu.make_async_copy(weight_ref.at[rows], weight_hbm.at[rows], weight_sems.at[at])
        )
        copies[-1].start()
    shift_sum, gain_sum = totals[:, 0:128], totals[:, 128:256]
    sums_ref[0:1] = gain_sum
    sums_ref[1:2] = shift_sum
    mean, rstd, voxels = norm_ref[0:1, :], norm_ref[1:2, :], norm_ref[2:3, :]
    gain = gain_ref[...]
    lane_in, lane_out = iota((128, 128), 0), iota((128, 128), 1)
    same = (lane_in // GROUP_CH == lane_out // GROUP_CH).astype(F32)

    def grouped(row):
        return exact_dot(jnp.broadcast_to(row, (8, 128)), same)[0:1]

    first = grouped(gain * shift_sum) / voxels
    second = grouped(gain * gain_sum) / voxels
    chunk = slots // 4
    for slot in range(slots):
        rows = slice(slot * 64, slot * 64 + 64)
        normed = (values_ref[rows, :].astype(F32) - mean) * rstd
        grad = grad_ref[pl.ds(slot, 64, stride=slots), :]
        inner = gain * grad - first - normed * second
        result = cotangent_ref[rows, :].astype(F32) + rstd * inner
        out_ref[rows, :] = jnp.where(slot < counts_ref[0], result, 0.0).astype(BF16)
        if slot % chunk == chunk - 1:
            at = slot // chunk
            rows = pl.ds(at * chunk * 64, chunk * 64)
            copies.append(
                pltpu.make_async_copy(out_ref.at[rows], out_hbm.at[rows], out_sems.at[at])
            )
            copies[-1].start()
    for copy in copies:
        copy.wait()


def body(features, cotangent, weight, gain, shift, counts, neighbours):
    slots, voxels, width = features.shape
    rows = slots * voxels
    n_plane = lax.axis_size("x") * lax.axis_size("y")
    n_line = lax.axis_size("z")
    n_slab = n_plane * n_line
    core = lax.axis_index("ch").astype(jnp.int32).reshape(1)
    turned_shape = jax.ShapeDtypeStruct((voxels, slots, width), BF16)
    face_shape = jax.ShapeDtypeStruct((16, slots, width), BF16)
    gain_row, shift_row = gain.reshape(1, width), shift.reshape(1, width)
    value_rows = features.reshape(rows, width)
    cotangent_rows = cotangent.reshape(rows, width)
    work = 2 * rows * 27 * width * 2 * width

    sent = call(
        sums_kernel,
        jax.ShapeDtypeStruct((n_slab, 1, 128), F32),
        [SMEM, HBM],
        [
            pltpu.VMEM((rows, width), BF16),
            pltpu.VMEM((rows, width), F32),
            pltpu.SemaphoreType.DMA((4,)),
        ],
        mib=60,
    )(counts, value_rows)
    table = lax.all_to_all(sent, SLABS, 0, 0, tiled=True)
    own, give, keep = call(
        turn_kernel,
        [turned_shape, face_shape, face_shape],
        [SMEM, HBM],
        [
            pltpu.VMEM((rows, width), BF16),
            pltpu.VMEM((rows, width), F32),
            pltpu.VMEM(turned_shape.shape, BF16),
            pltpu.SemaphoreType.DMA((4,)),
            pltpu.SemaphoreType.DMA((3,)),
        ],
        [HBM] * 3,
        mib=60,
    )(core, cotangent_rows)
    cores = [(0, 1), (1, 0)]
    ups = [(i, i + 1) for i in range(n_slab - 1)]
    outward = [(2 * i, 2 * j) for i, j in ups] + [(2 * j + 1, 2 * i + 1) for i, j in ups]
    sent_planes = jnp.stack([keep, lax.ppermute(give, "ch", cores)])
    own_other = lax.ppermute(own, "ch", cores)
    received = lax.ppermute(sent_planes, SLABS + ("ch",), outward)

    cube = (4, 4, 4, slots, width)
    face = (4, 4, slots, width)
    middle_shape = (4, 6, 6, slots, 2 * width)
    middle = call(
        halo_kernel,
        jax.ShapeDtypeStruct(middle_shape, BF16),
        [SMEM, VMEM, ANY, ANY],
        [
            pltpu.VMEM(middle_shape, BF16),
            pltpu.SemaphoreType.DMA((2,)),
            pltpu.SemaphoreType.DMA((4,)),
        ],
        HBM,
        flops=10**9,
    )(core, neighbours, own.reshape(cube), own_other.reshape(cube))

    middle, received = lax.optimization_barrier((middle, received))
    theirs = lax.ppermute(received, "ch", cores)
    sides_shape = jax.ShapeDtypeStruct((2, 6, 6, slots, 2 * width), BF16)
    sides = call(
        edge_kernel,
        sides_shape,
        [SMEM, VMEM, ANY, ANY, HBM],
        [
            pltpu.VMEM((2, 4, 4, slots, 2 * width), BF16),
            pltpu.VMEM((2, 4, 4, slots, 2 * width), BF16),
            pltpu.VMEM(sides_shape.shape, BF16),
            pltpu.SemaphoreType.DMA((6,)),
            pltpu.SemaphoreType.DMA((2,)),
        ],
        HBM,
    )(core, neighbours, received.reshape((2,) + face), theirs.reshape((2,) + face), middle)

    term_shape = jax.ShapeDtypeStruct((3, 9, width, 2 * width), BF16)
    weight_term, norm = call(
        weight_grad_kernel,
        [term_shape, jax.ShapeDtypeStruct((8, 128), F32)],
        [SMEM, VMEM, VMEM, VMEM, HBM, HBM, HBM],
        [
            pltpu.VMEM((rows, width), BF16),
            pltpu.VMEM((rows, width), F32),
            pltpu.VMEM((6, 6, 6, slots, 2 * width), BF16),
            pltpu.VMEM((4 * width, 16 * slots), BF16),
            pltpu.VMEM((3, width, 2 * width), F32),
            pltpu.VMEM(term_shape.shape, BF16),
            pltpu.SemaphoreType.DMA((4,)),
            pltpu.SemaphoreType.DMA((6,)),
            pltpu.SemaphoreType.DMA((3, 9)),
        ],
        [HBM, VMEM],
        flops=work,
    )(counts, table, gain_row, shift_row, value_rows, middle, sides)
    piece = 27 * width // n_plane
    parts = lax.all_to_all(
        weight_term.reshape(n_plane, piece, 2 * width), PLANE, 0, 0, tiled=True
    )

    grad_pre, sums = call(
        act_grad_kernel,
        [
            jax.ShapeDtypeStruct((voxels, slots, width), F32),
            jax.ShapeDtypeStruct((1, 2 * width), F32),
        ],
        [SMEM] + [VMEM] * 7,
        [pltpu.VMEM((4, 16, slots, width), F32), pltpu.VMEM((rows, width), F32)],
        flops=work,
    )(
        counts,
        norm,
        gain_row,
        shift_row,
        value_rows,
        weight.reshape(3, 9, width, 2 * width),
        middle,
        sides,
    )

    part = jnp.sum(parts.astype(F32), axis=0).reshape(n_line, piece // n_line, 2 * width)
    part = jnp.concatenate(
        [part, jnp.broadcast_to(sums.reshape(1, 1, 2 * width), (n_line, 1, 2 * width))], axis=1
    )
    part = jnp.sum(lax.all_to_all(part, "z", 0, 0, tiled=True), axis=0)
    final, line_sums = part[:-1].astype(BF16), part[-1:]
    line = jnp.broadcast_to(final[None], (n_line,) + final.shape)
    line = lax.all_to_all(line, "z", 0, 0, tiled=True).reshape(piece, 2 * width)
    split = []
    rest = line_sums
    for _ in range(3):
        top = lax.reduce_precision(rest, 8, 7)
        split.append(top.astype(BF16))
        rest = rest - top
    line = jnp.concatenate([line] + split + [jnp.zeros((5, 2 * width), BF16)], axis=0)
    plane = jnp.broadcast_to(line[None], (n_plane,) + line.shape)
    plane = lax.all_to_all(plane, PLANE, 0, 0, tiled=True)
    grad_features, grad_weight, totals = call(
        last_kernel,
        [
            jax.ShapeDtypeStruct((rows, width), BF16),
            jax.ShapeDtypeStruct((27 * width, 2 * width), F32),
            jax.ShapeDtypeStruct((2, width), F32),
        ],
        [SMEM] + [VMEM] * 6,
        [
            pltpu.VMEM((rows, width), BF16),
            pltpu.VMEM((27 * width, 2 * width), F32),
            pltpu.SemaphoreType.DMA((4,)),
            pltpu.SemaphoreType.DMA((n_plane,)),
        ],
        [HBM, HBM, VMEM],
        mib=20,
    )(
        counts,
        norm,
        gain_row,
        plane,
        value_rows,
        cotangent_rows,
        grad_pre.reshape(rows, width),
    )
    return (
        grad_features.reshape(features.shape),
        grad_weight.reshape(27, width, 2 * width),
        totals[0],
        totals[1],
    )


def solution(mesh):
    slabs = mesh.devices.shape[0]
    inner = Mesh(mesh.devices.reshape(CUT[slabs] + (2,)), SLABS + ("ch",))
    in_specs = (
        P(SLABS, None, "ch"),
        P(SLABS, None, "ch"),
        P(None, "ch", None),
        P("ch"),
        P("ch"),
        P(SLABS),
        P(SLABS, None),
    )
    out_specs = (P(SLABS, None, "ch"), P(None, "ch", None), P("ch"), P("ch"))
    return jax.shard_map(body, mesh=inner, in_specs=in_specs, out_specs=out_specs, check_vma=False)
```

```python
import functools

import jax
import jax.numpy as jnp
from jax import lax
from jax.experimental import pallas as pl
from jax.experimental.pallas import tpu as pltpu
from jax.sharding import Mesh
from jax.sharding import PartitionSpec as P

GROUP_CH = 8
CUT = {128: (8, 4, 4), 8: (2, 2, 2), 4: (2, 2, 1)}
SLABS = ("z", "x", "y")
PLANE = ("x", "y")
F32 = jnp.float32
BF16 = jnp.bfloat16
VMEM = pl.BlockSpec(memory_space=pltpu.VMEM)
SMEM = pl.BlockSpec(memory_space=pltpu.SMEM)
HBM = pl.BlockSpec(memory_space=pltpu.HBM)
ANY = pl.BlockSpec(memory_space=pl.ANY)


def call(kernel, out_shape, in_specs, scratch=(), out_specs=VMEM, flops=0, mib=52, aliases=None):
    if isinstance(out_shape, (list, tuple)) and out_specs is VMEM:
        out_specs = [VMEM] * len(out_shape)
    return pl.pallas_call(
        kernel,
        out_shape=out_shape,
        in_specs=in_specs,
        out_specs=out_specs,
        scratch_shapes=list(scratch),
        input_output_aliases=aliases or {},
        compiler_params=pltpu.CompilerParams(vmem_limit_bytes=mib * 1024 * 1024),
        cost_estimate=pl.CostEstimate(flops=flops, bytes_accessed=0, transcendentals=0),
    )


def exact_dot(left, right):
    return jnp.dot(left, right, precision=lax.Precision.HIGHEST, preferred_element_type=F32)


def iota(shape, dim):
    return lax.broadcasted_iota(jnp.int32, shape, dim)


def turned(rows_ref, out_ref):
    slots = out_ref.shape[1]
    for voxel in range(64):
        out_ref[voxel] = rows_ref[pl.ds(voxel, slots, stride=64), :].astype(out_ref.dtype)


def fetch(source, target, sems, pieces):
    step = source.shape[0] // pieces
    copies = [
        pltpu.make_async_copy(
            source.at[pl.ds(at * step, step)], target.at[pl.ds(at * step, step)], sems.at[at]
        )
        for at in range(pieces)
    ]
    for copy in copies:
        copy.start()
    return copies


def widen(copies, held_ref, rows_ref):
    step = held_ref.shape[0] // len(copies)
    for at, copy in enumerate(copies):
        copy.wait()
        rows = slice(at * step, at * step + step)
        rows_ref[rows, :] = held_ref[rows, :].astype(F32)


def turn_kernel(
    core_ref, in_hbm, own_hbm, give_hbm, keep_hbm, held_ref, rows_ref, own_ref, sems, out_sems
):
    copies = fetch(in_hbm, held_ref, sems, 4)
    core = core_ref[0]
    widen(copies, held_ref, rows_ref)
    turned(rows_ref, own_ref)
    sends = [
        pltpu.make_async_copy(own_ref.at[pl.ds(48 * core, 16)], give_hbm, out_sems.at[0]),
        pltpu.make_async_copy(own_ref.at[pl.ds(48 - 48 * core, 16)], keep_hbm, out_sems.at[1]),
        pltpu.make_async_copy(own_ref, own_hbm, out_sems.at[2]),
    ]
    for send in sends:
        send.start()
    for send in sends:
        send.wait()


def sums_kernel(counts_ref, values_hbm, sent_ref, held_ref, rows_ref, sems):
    slots = held_ref.shape[0] // 64
    count = counts_ref[0]
    widen(fetch(values_hbm, held_ref, sems, 4), held_ref, rows_ref)

    def over_slots(term):
        total = jnp.zeros((8, 128), F32)
        for slot in range(slots):
            rows = term(rows_ref[slot * 64 : slot * 64 + 64, :]).reshape(8, 8, 128).sum(axis=0)
            total = total + jnp.where(slot < count, rows, 0.0)
        return jnp.broadcast_to(jnp.sum(total, axis=0, keepdims=True), (8, 128))

    lane_in, lane_out = iota((128, 128), 0), iota((128, 128), 1)
    same = (lane_in // GROUP_CH == lane_out // GROUP_CH).astype(F32)
    to_sum = (lane_in // GROUP_CH == lane_out).astype(F32)
    to_square = (lane_in // GROUP_CH + 16 == lane_out).astype(F32)
    total = over_slots(lambda rows: rows)
    entries = count.astype(F32) * (64.0 * GROUP_CH)
    mean = (exact_dot(total, same) / entries)[0:1]

    def centred(rows):
        apart = rows - mean
        return apart * apart

    squares = over_slots(centred)
    row = exact_dot(total, to_sum) + exact_dot(squares, to_square)
    row = row + jnp.where(iota((8, 128), 1) == 32, count.astype(F32), 0.0)
    sent_ref[...] = jnp.broadcast_to(row[0:1].reshape(1, 1, 128), sent_ref.shape)


def lanes_of(core):
    mine = pl.ds(pl.multiple_of(core * 128, 128), 128)
    other = pl.ds(pl.multiple_of((1 - core) * 128, 128), 128)
    return mine, other


def side(at):
    return -1 if at == 0 else (1 if at == 5 else 0)


def source(at):
    return {0: 4, 5: 1}.get(at, at)


def offset_of(dx, b, c):
    return 9 * (dx + 1) + 3 * (side(b) + 1) + side(c) + 1


def choose(near, offset, first, last):
    columns = iota((near.shape[0], last - first), 1) + first
    return (near[:, offset : offset + 1] == columns).astype(F32).astype(BF16)


def halo_kernel(core_ref, near_ref, own_ref, own_other_ref, middle_ref, sems):
    slots = near_ref.shape[0]
    mine, other = lanes_of(core_ref[0])
    centre = middle_ref.at[:, 1:5, 1:5]
    copies = [
        pltpu.make_async_copy(own_ref, centre.at[:, :, :, :, mine], sems.at[0]),
        pltpu.make_async_copy(own_other_ref, centre.at[:, :, :, :, other], sems.at[1]),
    ]
    for copy in copies:
        copy.start()
    near = near_ref[...]
    places = [(b, c) for b in range(6) for c in range(6) if side(b) or side(c)]
    picks = {
        offset: choose(near, offset, slots, 2 * slots)
        for offset in sorted({offset_of(0, b, c) for b, c in places})
    }
    for copy in copies:
        copy.wait()
    for plane in range(4):
        for b, c in places:
            middle_ref[plane, b, c] = jnp.dot(
                picks[offset_of(0, b, c)],
                middle_ref[plane, source(b), source(c)],
                preferred_element_type=F32,
            ).astype(BF16)


def window(plane_ref, turn):
    slots = plane_ref.shape[2]
    block = plane_ref[pl.ds(2 - turn // 3, 4), pl.ds(2 - turn % 3, 4)]
    return block.reshape(16 * slots, 256)


def planes_of(plane):
    return max(0, plane - 2), min(3, plane) + 1


def weight_grad_kernel(
    counts_ref,
    core_ref,
    near_ref,
    table_ref,
    gain_ref,
    shift_ref,
    received_ref,
    theirs_ref,
    values_hbm,
    middle_ref,
    out_hbm,
    grid_hbm,
    norm_ref,
    held_ref,
    rows_ref,
    sides_ref,
    face_ref,
    act_ref,
    total_ref,
    out_ref,
    sems,
    face_sems,
    plane_sems,
    out_sems,
):
    slots = middle_ref.shape[3]
    core = core_ref[0]
    mine, other = lanes_of(core)
    near_face, far_face = face_ref.at[core], face_ref.at[1 - core]
    copies = fetch(values_hbm, held_ref, sems, 4)
    faces = [
        pltpu.make_async_copy(received_ref.at[0], near_face.at[:, :, :, mine], face_sems.at[0]),
        pltpu.make_async_copy(received_ref.at[1], near_face.at[:, :, :, other], face_sems.at[1]),
        pltpu.make_async_copy(theirs_ref.at[0], far_face.at[:, :, :, other], face_sems.at[2]),
        pltpu.make_async_copy(theirs_ref.at[1], far_face.at[:, :, :, mine], face_sems.at[3]),
    ]
    for copy in faces:
        copy.start()
    table = table_ref[...]
    held = jnp.sum(table, axis=0)
    voxels = held[:, 32:33] * (64.0 * GROUP_CH)
    entries = table[:, :, 32:33] * (64.0 * GROUP_CH)
    mean = held / voxels
    apart = table / entries - mean.reshape(1, 1, 128)
    between = jnp.sum(apart * apart * entries, axis=0)
    lane_in, lane_out = iota((128, 128), 0), iota((128, 128), 1)
    from_sum = (lane_in == lane_out // GROUP_CH).astype(F32)
    from_square = (lane_in == lane_out // GROUP_CH + 16).astype(F32)

    stacked = jnp.concatenate([mean, between, held, jnp.zeros((5, 128), F32)], axis=0)
    spread = exact_dot(stacked, jnp.concatenate([from_sum, from_square], axis=1))
    mean = spread[0:1, 0:128]
    variance = (spread[1:2, 0:128] + spread[2:3, 128:256]) / voxels
    rstd = lax.rsqrt(variance + 1e-05)
    norm_ref[0:1, :] = mean
    norm_ref[1:2, :] = rstd
    norm_ref[2:3, :] = jnp.broadcast_to(voxels, (1, 128))
    norm_ref[3:8, :] = jnp.zeros((5, 128), F32)
    gain, shift = gain_ref[...], shift_ref[...]
    live = iota((slots, 128), 0) < counts_ref[0]
    widen(copies, held_ref, rows_ref)
    for plane in range(4):
        pieces = []
        for voxel in range(plane * 16, plane * 16 + 16):
            normed = (rows_ref[pl.ds(voxel, slots, stride=64), :] - mean) * rstd
            pre = normed * gain + shift
            pieces.append(jnp.where(live, pre / (1.0 + jnp.exp(-pre)), 0.0))
        rows = jnp.concatenate(pieces, axis=0)
        act_ref[plane * 128 : plane * 128 + 128, :] = rows.T.astype(BF16)
    for copy in faces:
        copy.wait()
    near = near_ref[...]
    places = [(b, c) for b in range(6) for c in range(6)]
    sends = []
    for which, dx in enumerate((-1, 1)):
        lowest = which * slots
        picks = {
            offset: choose(near, offset, lowest, lowest + 2 * slots)
            for offset in sorted({offset_of(dx, b, c) for b, c in places})
        }
        for b, c in places:
            outer = face_ref[which, source(b) - 1, source(c) - 1]
            inner = middle_ref[3 - 3 * which, source(b), source(c)]
            table = [outer, inner] if which == 0 else [inner, outer]
            sides_ref[which, b, c] = jnp.dot(
                picks[offset_of(dx, b, c)],
                jnp.concatenate(table, axis=0),
                preferred_element_type=F32,
            ).astype(BF16)
    planes = [sides_ref.at[0]] + [middle_ref.at[at] for at in range(4)] + [sides_ref.at[1]]
    for at, plane in enumerate(planes):
        sends.append(pltpu.make_async_copy(plane, grid_hbm.at[at], plane_sems.at[at]))
        sends[-1].start()
    for turn in range(9):
        seen = set()
        for plane in range(6):
            first, last = planes_of(plane)
            part = jnp.dot(
                act_ref[first * 128 : last * 128, :],
                window(planes[plane], turn),
                preferred_element_type=F32,
            )
            for at in range(first, last):
                step = at - plane + 2
                term = part[(at - first) * 128 : (at - first) * 128 + 128]
                if step in seen:
                    total_ref[step] += term
                else:
                    total_ref[step] = term
                    seen.add(step)
        for step in range(3):
            out_ref[step, turn] = total_ref[step].astype(BF16)
            sends.append(
                pltpu.make_async_copy(
                    out_ref.at[step, turn], out_hbm.at[step, turn], out_sems.at[step, turn]
                )
            )
            sends[-1].start()
    for send in sends:
        send.wait()


def act_grad_kernel(
    counts_ref,
    norm_ref,
    gain_ref,
    shift_ref,
    values_ref,
    weight_ref,
    grid_ref,
    out_ref,
    sums_ref,
    total_ref,
    rows_ref,
):
    slots = grid_ref.shape[3]
    total_ref[...] = jnp.zeros_like(total_ref)
    rows_ref[...] = values_ref[...].astype(F32)

    @pl.loop(0, 9)
    def _(turn):
        for plane in range(6):
            first, last = planes_of(plane)
            low, high = first - plane + 2, last - plane + 2
            part = lax.dot_general(
                window(grid_ref.at[plane], turn),
                weight_ref[low:high, turn].reshape((high - low) * 128, 256),
                (((1,), (1,)), ((), ())),
                preferred_element_type=F32,
            )
            for at in range(first, last):
                term = part[:, (at - first) * 128 : (at - first) * 128 + 128]
                total_ref[at] += term.reshape(16, slots, 128)

    mean, rstd = norm_ref[0:1, :], norm_ref[1:2, :]
    gain, shift = gain_ref[...], shift_ref[...]
    live = iota((slots, 128), 0) < counts_ref[0]
    shift_sum = jnp.zeros((8, 128), F32)
    gain_sum = jnp.zeros((8, 128), F32)
    for voxel in range(64):
        normed = (rows_ref[pl.ds(voxel, slots, stride=64), :] - mean) * rstd
        pre = normed * gain + shift
        sig = 1.0 / (1.0 + jnp.exp(-pre))
        grad = total_ref[voxel // 16, voxel % 16] * sig * (1.0 + pre * (1.0 - sig))
        grad = jnp.where(live, grad, 0.0)
        out_ref[voxel] = grad
        shift_sum = shift_sum + grad.reshape(slots // 8, 8, 128).sum(axis=0)
        gain_sum = gain_sum + (grad * normed).reshape(slots // 8, 8, 128).sum(axis=0)
    sums_ref[:, 0:128] = jnp.sum(shift_sum, axis=0, keepdims=True)
    sums_ref[:, 128:256] = jnp.sum(gain_sum, axis=0, keepdims=True)


def last_kernel(
    counts_ref,
    norm_ref,
    gain_ref,
    plane_ref,
    values_ref,
    cotangent_ref,
    grad_ref,
    out_hbm,
    weight_hbm,
    sums_ref,
    out_ref,
    weight_ref,
    out_sems,
    weight_sems,
):
    slots = grad_ref.shape[0] // 64
    pieces = plane_ref.shape[0]
    piece = weight_ref.shape[0] // pieces
    copies = []
    totals = jnp.zeros((1, 256), F32)
    for at in range(pieces):
        block = plane_ref[at].astype(F32)
        rows = pl.ds(at * piece, piece)
        weight_ref[rows] = block[0:piece]
        totals = totals + (block[piece : piece + 1] + block[piece + 1 : piece + 2])
        totals = totals + block[piece + 2 : piece + 3]
        copies.append(
            pltpu.make_async_copy(weight_ref.at[rows], weight_hbm.at[rows], weight_sems.at[at])
        )
        copies[-1].start()
    shift_sum, gain_sum = totals[:, 0:128], totals[:, 128:256]
    sums_ref[0:1] = gain_sum
    sums_ref[1:2] = shift_sum
    mean, rstd, voxels = norm_ref[0:1, :], norm_ref[1:2, :], norm_ref[2:3, :]
    gain = gain_ref[...]
    lane_in, lane_out = iota((128, 128), 0), iota((128, 128), 1)
    same = (lane_in // GROUP_CH == lane_out // GROUP_CH).astype(F32)

    stacked = jnp.concatenate(
        [gain * shift_sum, gain * gain_sum, jnp.zeros((6, 128), F32)], axis=0
    )
    grouped = exact_dot(stacked, same) / voxels
    first, second = grouped[0:1], grouped[1:2]
    chunk = slots // 4
    for slot in range(slots):
        rows = slice(slot * 64, slot * 64 + 64)
        normed = (values_ref[rows, :].astype(F32) - mean) * rstd
        grad = grad_ref[pl.ds(slot, 64, stride=slots), :]
        inner = gain * grad - first - normed * second
        result = cotangent_ref[rows, :].astype(F32) + rstd * inner
        out_ref[rows, :] = jnp.where(slot < counts_ref[0], result, 0.0).astype(BF16)
        if slot % chunk == chunk - 1:
            at = slot // chunk
            rows = pl.ds(at * chunk * 64, chunk * 64)
            copies.append(
                pltpu.make_async_copy(out_ref.at[rows], out_hbm.at[rows], out_sems.at[at])
            )
            copies[-1].start()
    for copy in copies:
        copy.wait()


def body(features, cotangent, weight, gain, shift, counts, neighbours):
    slots, voxels, width = features.shape
    rows = slots * voxels
    n_plane = lax.axis_size("x") * lax.axis_size("y")
    n_line = lax.axis_size("z")
    n_slab = n_plane * n_line
    core = lax.axis_index("ch").astype(jnp.int32).reshape(1)
    turned_shape = jax.ShapeDtypeStruct((voxels, slots, width), BF16)
    face_shape = jax.ShapeDtypeStruct((16, slots, width), BF16)
    gain_row, shift_row = gain.reshape(1, width), shift.reshape(1, width)
    value_rows = features.reshape(rows, width)
    cotangent_rows = cotangent.reshape(rows, width)
    work = 2 * rows * 27 * width * 2 * width

    sent = call(
        sums_kernel,
        jax.ShapeDtypeStruct((n_slab, 1, 128), F32),
        [SMEM, HBM],
        [
            pltpu.VMEM((rows, width), BF16),
            pltpu.VMEM((rows, width), F32),
            pltpu.SemaphoreType.DMA((4,)),
        ],
        mib=60,
    )(counts, value_rows)
    table = lax.all_to_all(sent, SLABS, 0, 0, tiled=True)
    own, give, keep = call(
        turn_kernel,
        [turned_shape, face_shape, face_shape],
        [SMEM, HBM],
        [
            pltpu.VMEM((rows, width), BF16),
            pltpu.VMEM((rows, width), F32),
            pltpu.VMEM(turned_shape.shape, BF16),
            pltpu.SemaphoreType.DMA((4,)),
            pltpu.SemaphoreType.DMA((3,)),
        ],
        [HBM] * 3,
        mib=60,
    )(core, cotangent_rows)
    cores = [(0, 1), (1, 0)]
    ups = [(i, i + 1) for i in range(n_slab - 1)]
    outward = [(2 * i, 2 * j) for i, j in ups] + [(2 * j + 1, 2 * i + 1) for i, j in ups]
    sent_planes = jnp.stack([keep, lax.ppermute(give, "ch", cores)])
    own_other = lax.ppermute(own, "ch", cores)
    received = lax.ppermute(sent_planes, SLABS + ("ch",), outward)

    cube = (4, 4, 4, slots, width)
    face = (4, 4, slots, width)
    middle_shape = (4, 6, 6, slots, 2 * width)
    middle = call(
        halo_kernel,
        jax.ShapeDtypeStruct(middle_shape, BF16),
        [SMEM, VMEM, ANY, ANY],
        [pltpu.SemaphoreType.DMA((2,))],
        flops=10**9,
        mib=24,
    )(core, neighbours, own.reshape(cube), own_other.reshape(cube))

    table, received = lax.optimization_barrier((table, received))
    theirs = lax.ppermute(received, "ch", cores)
    grid_shape = pltpu.HBM((6, 6, 6, slots, 2 * width), BF16)

    term_shape = jax.ShapeDtypeStruct((3, 9, width, 2 * width), BF16)
    weight_term, grid, norm = call(
        weight_grad_kernel,
        [term_shape, grid_shape, jax.ShapeDtypeStruct((8, 128), F32)],
        [SMEM, SMEM, VMEM, VMEM, VMEM, VMEM, ANY, ANY, HBM, VMEM],
        [
            pltpu.VMEM((rows, width), BF16),
            pltpu.VMEM((rows, width), F32),
            pltpu.VMEM((2, 6, 6, slots, 2 * width), BF16),
            pltpu.VMEM((2, 4, 4, slots, 2 * width), BF16),
            pltpu.VMEM((4 * width, 16 * slots), BF16),
            pltpu.VMEM((3, width, 2 * width), F32),
            pltpu.VMEM(term_shape.shape, BF16),
            pltpu.SemaphoreType.DMA((4,)),
            pltpu.SemaphoreType.DMA((4,)),
            pltpu.SemaphoreType.DMA((6,)),
            pltpu.SemaphoreType.DMA((3, 9)),
        ],
        [HBM, HBM, VMEM],
        flops=work,
        mib=24,
    )(
        counts,
        core,
        neighbours,
        table,
        gain_row,
        shift_row,
        received.reshape((2,) + face),
        theirs.reshape((2,) + face),
        value_rows,
        middle,
    )
    piece = 27 * width // n_plane
    parts = lax.all_to_all(
        weight_term.reshape(n_plane, piece, 2 * width), PLANE, 0, 0, tiled=True
    )

    grad_pre, sums = call(
        act_grad_kernel,
        [
            jax.ShapeDtypeStruct((voxels, slots, width), F32),
            jax.ShapeDtypeStruct((1, 2 * width), F32),
        ],
        [SMEM] + [VMEM] * 6,
        [pltpu.VMEM((4, 16, slots, width), F32), pltpu.VMEM((rows, width), F32)],
        flops=work,
        mib=24,
    )(
        counts,
        norm,
        gain_row,
        shift_row,
        value_rows,
        weight.reshape(3, 9, width, 2 * width),
        grid,
    )

    part = jnp.sum(parts.astype(F32), axis=0).reshape(n_line, piece // n_line, 2 * width)
    part = jnp.concatenate(
        [part, jnp.broadcast_to(sums.reshape(1, 1, 2 * width), (n_line, 1, 2 * width))], axis=1
    )
    part = jnp.sum(lax.all_to_all(part, "z", 0, 0, tiled=True), axis=0)
    final, line_sums = part[:-1].astype(BF16), part[-1:]
    line = jnp.broadcast_to(final[None], (n_line,) + final.shape)
    line = lax.all_to_all(line, "z", 0, 0, tiled=True).reshape(piece, 2 * width)
    split = []
    rest = line_sums
    for _ in range(3):
        top = lax.reduce_precision(rest, 8, 7)
        split.append(top.astype(BF16))
        rest = rest - top
    line = jnp.concatenate([line] + split + [jnp.zeros((5, 2 * width), BF16)], axis=0)
    plane = jnp.broadcast_to(line[None], (n_plane,) + line.shape)
    plane = lax.all_to_all(plane, PLANE, 0, 0, tiled=True)
    grad_features, grad_weight, totals = call(
        last_kernel,
        [
            jax.ShapeDtypeStruct((rows, width), BF16),
            jax.ShapeDtypeStruct((27 * width, 2 * width), F32),
            jax.ShapeDtypeStruct((2, width), F32),
        ],
        [SMEM] + [VMEM] * 6,
        [
            pltpu.VMEM((rows, width), BF16),
            pltpu.VMEM((27 * width, 2 * width), F32),
            pltpu.SemaphoreType.DMA((4,)),
            pltpu.SemaphoreType.DMA((n_plane,)),
        ],
        [HBM, HBM, VMEM],
        mib=20,
    )(
        counts,
        norm,
        gain_row,
        plane,
        value_rows,
        cotangent_rows,
        grad_pre.reshape(rows, width),
    )
    return (
        grad_features.reshape(features.shape),
        grad_weight.reshape(27, width, 2 * width),
        totals[0],
        totals[1],
    )


def solution(mesh):
    slabs = mesh.devices.shape[0]
    inner = Mesh(mesh.devices.reshape(CUT[slabs] + (2,)), SLABS + ("ch",))
    in_specs = (
        P(SLABS, None, "ch"),
        P(SLABS, None, "ch"),
        P(None, "ch", None),
        P("ch"),
        P("ch"),
        P(SLABS),
        P(SLABS, None),
    )
    out_specs = (P(SLABS, None, "ch"), P(None, "ch", None), P("ch"), P("ch"))
    return jax.shard_map(body, mesh=inner, in_specs=in_specs, out_specs=out_specs, check_vma=False)
```

```python
import functools

import jax
import jax.numpy as jnp
from jax import lax
from jax.experimental import pallas as pl
from jax.experimental.pallas import tpu as pltpu
from jax.sharding import Mesh
from jax.sharding import PartitionSpec as P

GROUP_CH = 8
CUT = {128: (8, 4, 4), 8: (2, 2, 2), 4: (2, 2, 1)}
SLABS = ("z", "x", "y")
PLANE = ("x", "y")
F32 = jnp.float32
BF16 = jnp.bfloat16
VMEM = pl.BlockSpec(memory_space=pltpu.VMEM)
SMEM = pl.BlockSpec(memory_space=pltpu.SMEM)
HBM = pl.BlockSpec(memory_space=pltpu.HBM)
ANY = pl.BlockSpec(memory_space=pl.ANY)


def call(kernel, out_shape, in_specs, scratch=(), out_specs=VMEM, flops=0, mib=52, aliases=None):
    if isinstance(out_shape, (list, tuple)) and out_specs is VMEM:
        out_specs = [VMEM] * len(out_shape)
    return pl.pallas_call(
        kernel,
        out_shape=out_shape,
        in_specs=in_specs,
        out_specs=out_specs,
        scratch_shapes=list(scratch),
        input_output_aliases=aliases or {},
        compiler_params=pltpu.CompilerParams(vmem_limit_bytes=mib * 1024 * 1024),
        cost_estimate=pl.CostEstimate(flops=flops, bytes_accessed=0, transcendentals=0),
    )


def exact_dot(left, right):
    return jnp.dot(left, right, precision=lax.Precision.HIGHEST, preferred_element_type=F32)


def iota(shape, dim):
    return lax.broadcasted_iota(jnp.int32, shape, dim)


def turned(rows_ref, out_ref):
    slots = out_ref.shape[1]
    for voxel in range(64):
        out_ref[voxel] = rows_ref[pl.ds(voxel, slots, stride=64), :].astype(out_ref.dtype)


def fetch(source, target, sems, pieces):
    step = source.shape[0] // pieces
    copies = [
        pltpu.make_async_copy(
            source.at[pl.ds(at * step, step)], target.at[pl.ds(at * step, step)], sems.at[at]
        )
        for at in range(pieces)
    ]
    for copy in copies:
        copy.start()
    return copies


def widen(copies, held_ref, rows_ref):
    step = held_ref.shape[0] // len(copies)
    for at, copy in enumerate(copies):
        copy.wait()
        rows = slice(at * step, at * step + step)
        rows_ref[rows, :] = held_ref[rows, :].astype(F32)


def prepare_kernel(
    counts_ref,
    core_ref,
    cotangent_hbm,
    values_hbm,
    own_hbm,
    give_hbm,
    keep_hbm,
    sent_ref,
    held_ref,
    rows_ref,
    own_ref,
    sems,
    out_sems,
):
    slots = own_ref.shape[1]
    turns = fetch(cotangent_hbm, held_ref.at[0], sems.at[0], 4)
    copies = fetch(values_hbm, held_ref.at[1], sems.at[1], 4)
    core = core_ref[0]
    count = counts_ref[0]
    widen(turns, held_ref.at[0], rows_ref)
    turned(rows_ref, own_ref)
    sends = [
        pltpu.make_async_copy(own_ref.at[pl.ds(48 * core, 16)], give_hbm, out_sems.at[0]),
        pltpu.make_async_copy(own_ref.at[pl.ds(48 - 48 * core, 16)], keep_hbm, out_sems.at[1]),
        pltpu.make_async_copy(own_ref, own_hbm, out_sems.at[2]),
    ]
    for send in sends:
        send.start()
    widen(copies, held_ref.at[1], rows_ref)

    def over_slots(term):
        total = jnp.zeros((8, 128), F32)
        for slot in range(slots):
            rows = term(rows_ref[slot * 64 : slot * 64 + 64, :]).reshape(8, 8, 128).sum(axis=0)
            total = total + jnp.where(slot < count, rows, 0.0)
        return jnp.broadcast_to(jnp.sum(total, axis=0, keepdims=True), (8, 128))

    lane_in, lane_out = iota((128, 128), 0), iota((128, 128), 1)
    same = (lane_in // GROUP_CH == lane_out // GROUP_CH).astype(F32)
    to_sum = (lane_in // GROUP_CH == lane_out).astype(F32)
    to_square = (lane_in // GROUP_CH + 16 == lane_out).astype(F32)
    total = over_slots(lambda rows: rows)
    entries = count.astype(F32) * (64.0 * GROUP_CH)
    mean = (exact_dot(total, same) / entries)[0:1]

    def centred(rows):
        apart = rows - mean
        return apart * apart

    squares = over_slots(centred)
    row = exact_dot(total, to_sum) + exact_dot(squares, to_square)
    row = row + jnp.where(iota((8, 128), 1) == 32, count.astype(F32), 0.0)
    sent_ref[...] = jnp.broadcast_to(row[0:1].reshape(1, 1, 128), sent_ref.shape)
    for send in sends:
        send.wait()


def lanes_of(core):
    mine = pl.ds(pl.multiple_of(core * 128, 128), 128)
    other = pl.ds(pl.multiple_of((1 - core) * 128, 128), 128)
    return mine, other


def side(at):
    return -1 if at == 0 else (1 if at == 5 else 0)


def source(at):
    return {0: 4, 5: 1}.get(at, at)


def offset_of(dx, b, c):
    return 9 * (dx + 1) + 3 * (side(b) + 1) + side(c) + 1


def choose(near, offset, first, last):
    columns = iota((near.shape[0], last - first), 1) + first
    return (near[:, offset : offset + 1] == columns).astype(F32).astype(BF16)


def halo_kernel(core_ref, near_ref, own_ref, own_other_ref, middle_ref, sems):
    slots = near_ref.shape[0]
    mine, other = lanes_of(core_ref[0])
    centre = middle_ref.at[:, 1:5, 1:5]
    copies = [
        pltpu.make_async_copy(own_ref, centre.at[:, :, :, :, mine], sems.at[0]),
        pltpu.make_async_copy(own_other_ref, centre.at[:, :, :, :, other], sems.at[1]),
    ]
    for copy in copies:
        copy.start()
    near = near_ref[...]
    places = [(b, c) for b in range(6) for c in range(6) if side(b) or side(c)]
    picks = {
        offset: choose(near, offset, slots, 2 * slots)
        for offset in sorted({offset_of(0, b, c) for b, c in places})
    }
    for copy in copies:
        copy.wait()
    for plane in range(4):
        for b, c in places:
            middle_ref[plane, b, c] = jnp.dot(
                picks[offset_of(0, b, c)],
                middle_ref[plane, source(b), source(c)],
                preferred_element_type=F32,
            ).astype(BF16)


def window(plane_ref, turn):
    slots = plane_ref.shape[2]
    block = plane_ref[pl.ds(2 - turn // 3, 4), pl.ds(2 - turn % 3, 4)]
    return block.reshape(16 * slots, 256)


def planes_of(plane):
    return max(0, plane - 2), min(3, plane) + 1


def weight_grad_kernel(
    counts_ref,
    core_ref,
    near_ref,
    table_ref,
    gain_ref,
    shift_ref,
    received_ref,
    theirs_ref,
    values_ref,
    middle_ref,
    out_hbm,
    grid_hbm,
    norm_ref,
    rows_ref,
    sides_ref,
    face_ref,
    act_ref,
    total_ref,
    out_ref,
    face_sems,
    plane_sems,
    out_sems,
):
    slots = middle_ref.shape[3]
    core = core_ref[0]
    mine, other = lanes_of(core)
    near_face, far_face = face_ref.at[core], face_ref.at[1 - core]
    faces = [
        pltpu.make_async_copy(received_ref.at[0], near_face.at[:, :, :, mine], face_sems.at[0]),
        pltpu.make_async_copy(received_ref.at[1], near_face.at[:, :, :, other], face_sems.at[1]),
        pltpu.make_async_copy(theirs_ref.at[0], far_face.at[:, :, :, other], face_sems.at[2]),
        pltpu.make_async_copy(theirs_ref.at[1], far_face.at[:, :, :, mine], face_sems.at[3]),
    ]
    for copy in faces:
        copy.start()
    table = table_ref[...]
    held = jnp.sum(table, axis=0)
    voxels = held[:, 32:33] * (64.0 * GROUP_CH)
    entries = table[:, :, 32:33] * (64.0 * GROUP_CH)
    mean = held / voxels
    apart = table / entries - mean.reshape(1, 1, 128)
    between = jnp.sum(apart * apart * entries, axis=0)
    lane_in, lane_out = iota((128, 128), 0), iota((128, 128), 1)
    from_sum = (lane_in == lane_out // GROUP_CH).astype(F32)
    from_square = (lane_in == lane_out // GROUP_CH + 16).astype(F32)

    stacked = jnp.concatenate([mean, between, held, jnp.zeros((5, 128), F32)], axis=0)
    spread = exact_dot(stacked, jnp.concatenate([from_sum, from_square], axis=1))
    mean = spread[0:1, 0:128]
    variance = (spread[1:2, 0:128] + spread[2:3, 128:256]) / voxels
    rstd = lax.rsqrt(variance + 1e-05)
    norm_ref[0:1, :] = mean
    norm_ref[1:2, :] = rstd
    norm_ref[2:3, :] = jnp.broadcast_to(voxels, (1, 128))
    norm_ref[3:8, :] = jnp.zeros((5, 128), F32)
    gain, shift = gain_ref[...], shift_ref[...]
    live = iota((slots, 128), 0) < counts_ref[0]
    rows_ref[...] = values_ref[...].astype(F32)
    for plane in range(4):
        pieces = []
        for voxel in range(plane * 16, plane * 16 + 16):
            normed = (rows_ref[pl.ds(voxel, slots, stride=64), :] - mean) * rstd
            pre = normed * gain + shift
            pieces.append(jnp.where(live, pre / (1.0 + jnp.exp(-pre)), 0.0))
        rows = jnp.concatenate(pieces, axis=0)
        act_ref[plane * 128 : plane * 128 + 128, :] = rows.T.astype(BF16)
    for copy in faces:
        copy.wait()
    near = near_ref[...]
    places = [(b, c) for b in range(6) for c in range(6)]
    sends = []
    for which, dx in enumerate((-1, 1)):
        lowest = which * slots
        picks = {
            offset: choose(near, offset, lowest, lowest + 2 * slots)
            for offset in sorted({offset_of(dx, b, c) for b, c in places})
        }
        for b, c in places:
            outer = face_ref[which, source(b) - 1, source(c) - 1]
            inner = middle_ref[3 - 3 * which, source(b), source(c)]
            table = [outer, inner] if which == 0 else [inner, outer]
            sides_ref[which, b, c] = jnp.dot(
                picks[offset_of(dx, b, c)],
                jnp.concatenate(table, axis=0),
                preferred_element_type=F32,
            ).astype(BF16)
    planes = [sides_ref.at[0]] + [middle_ref.at[at] for at in range(4)] + [sides_ref.at[1]]
    for at, plane in enumerate(planes):
        sends.append(pltpu.make_async_copy(plane, grid_hbm.at[at], plane_sems.at[at]))
        sends[-1].start()
    for turn in range(9):
        seen = set()
        for plane in range(6):
            first, last = planes_of(plane)
            part = jnp.dot(
                act_ref[first * 128 : last * 128, :],
                window(planes[plane], turn),
                preferred_element_type=F32,
            )
            for at in range(first, last):
                step = at - plane + 2
                term = part[(at - first) * 128 : (at - first) * 128 + 128]
                if step in seen:
                    total_ref[step] += term
                else:
                    total_ref[step] = term
                    seen.add(step)
        for step in range(3):
            out_ref[step, turn] = total_ref[step].astype(BF16)
        if turn in (5, 8):
            part = pl.ds(0, 6) if turn == 5 else pl.ds(6, 3)
            for step in range(3):
                sends.append(
                    pltpu.make_async_copy(
                        out_ref.at[step, part], out_hbm.at[step, part], out_sems.at[step, turn // 8]
                    )
                )
                sends[-1].start()
    for send in sends:
        send.wait()


def act_grad_kernel(
    counts_ref,
    norm_ref,
    gain_ref,
    shift_ref,
    values_ref,
    weight_ref,
    grid_ref,
    out_ref,
    sums_ref,
    total_ref,
    rows_ref,
):
    slots = grid_ref.shape[3]
    total_ref[...] = jnp.zeros_like(total_ref)
    rows_ref[...] = values_ref[...].astype(F32)

    @pl.loop(0, 9)
    def _(turn):
        for plane in range(6):
            first, last = planes_of(plane)
            low, high = first - plane + 2, last - plane + 2
            part = lax.dot_general(
                window(grid_ref.at[plane], turn),
                weight_ref[low:high, turn].reshape((high - low) * 128, 256),
                (((1,), (1,)), ((), ())),
                preferred_element_type=F32,
            )
            for at in range(first, last):
                term = part[:, (at - first) * 128 : (at - first) * 128 + 128]
                total_ref[at] += term.reshape(16, slots, 128)

    mean, rstd = norm_ref[0:1, :], norm_ref[1:2, :]
    gain, shift = gain_ref[...], shift_ref[...]
    live = iota((slots, 128), 0) < counts_ref[0]
    shift_sum = jnp.zeros((8, 128), F32)
    gain_sum = jnp.zeros((8, 128), F32)
    for voxel in range(64):
        normed = (rows_ref[pl.ds(voxel, slots, stride=64), :] - mean) * rstd
        pre = normed * gain + shift
        sig = 1.0 / (1.0 + jnp.exp(-pre))
        grad = total_ref[voxel // 16, voxel % 16] * sig * (1.0 + pre * (1.0 - sig))
        grad = jnp.where(live, grad, 0.0)
        out_ref[voxel] = grad
        shift_sum = shift_sum + grad.reshape(slots // 8, 8, 128).sum(axis=0)
        gain_sum = gain_sum + (grad * normed).reshape(slots // 8, 8, 128).sum(axis=0)
    sums_ref[:, 0:128] = jnp.sum(shift_sum, axis=0, keepdims=True)
    sums_ref[:, 128:256] = jnp.sum(gain_sum, axis=0, keepdims=True)


def last_kernel(
    counts_ref,
    norm_ref,
    gain_ref,
    plane_ref,
    values_ref,
    cotangent_ref,
    grad_ref,
    out_hbm,
    weight_hbm,
    gain_out,
    shift_out,
    out_ref,
    weight_ref,
    out_sems,
    weight_sems,
):
    slots = grad_ref.shape[0] // 64
    pieces = plane_ref.shape[0]
    piece = weight_ref.shape[0] // pieces
    copies = []
    totals = jnp.zeros((1, 256), F32)
    for at in range(pieces):
        block = plane_ref[at].astype(F32)
        rows = pl.ds(at * piece, piece)
        weight_ref[rows] = block[0:piece]
        totals = totals + (block[piece : piece + 1] + block[piece + 1 : piece + 2])
        totals = totals + block[piece + 2 : piece + 3]
        copies.append(
            pltpu.make_async_copy(weight_ref.at[rows], weight_hbm.at[rows], weight_sems.at[at])
        )
        copies[-1].start()
    shift_sum, gain_sum = totals[:, 0:128], totals[:, 128:256]
    gain_out[...] = gain_sum
    shift_out[...] = shift_sum
    mean, rstd, voxels = norm_ref[0:1, :], norm_ref[1:2, :], norm_ref[2:3, :]
    gain = gain_ref[...]
    lane_in, lane_out = iota((128, 128), 0), iota((128, 128), 1)
    same = (lane_in // GROUP_CH == lane_out // GROUP_CH).astype(F32)

    stacked = jnp.concatenate(
        [gain * shift_sum, gain * gain_sum, jnp.zeros((6, 128), F32)], axis=0
    )
    grouped = exact_dot(stacked, same) / voxels
    first, second = grouped[0:1], grouped[1:2]
    chunk = slots // 4
    for slot in range(slots):
        rows = slice(slot * 64, slot * 64 + 64)
        normed = (values_ref[rows, :].astype(F32) - mean) * rstd
        grad = grad_ref[pl.ds(slot, 64, stride=slots), :]
        inner = gain * grad - first - normed * second
        result = cotangent_ref[rows, :].astype(F32) + rstd * inner
        out_ref[rows, :] = jnp.where(slot < counts_ref[0], result, 0.0).astype(BF16)
        if slot % chunk == chunk - 1:
            at = slot // chunk
            rows = pl.ds(at * chunk * 64, chunk * 64)
            copies.append(
                pltpu.make_async_copy(out_ref.at[rows], out_hbm.at[rows], out_sems.at[at])
            )
            copies[-1].start()
    for copy in copies:
        copy.wait()


def body(features, cotangent, weight, gain, shift, counts, neighbours):
    slots, voxels, width = features.shape
    rows = slots * voxels
    n_plane = lax.axis_size("x") * lax.axis_size("y")
    n_line = lax.axis_size("z")
    n_slab = n_plane * n_line
    core = lax.axis_index("ch").astype(jnp.int32).reshape(1)
    turned_shape = jax.ShapeDtypeStruct((voxels, slots, width), BF16)
    face_shape = jax.ShapeDtypeStruct((16, slots, width), BF16)
    gain_row, shift_row = gain.reshape(1, width), shift.reshape(1, width)
    value_rows = features.reshape(rows, width)
    cotangent_rows = cotangent.reshape(rows, width)
    work = 2 * rows * 27 * width * 2 * width

    own, give, keep, sent = call(
        prepare_kernel,
        [
            turned_shape,
            face_shape,
            face_shape,
            jax.ShapeDtypeStruct((n_slab, 1, 128), F32),
        ],
        [SMEM, SMEM, HBM, HBM],
        [
            pltpu.VMEM((2, rows, width), BF16),
            pltpu.VMEM((rows, width), F32),
            pltpu.VMEM(turned_shape.shape, BF16),
            pltpu.SemaphoreType.DMA((2, 4)),
            pltpu.SemaphoreType.DMA((3,)),
        ],
        [HBM, HBM, HBM, VMEM],
        mib=60,
    )(counts, core, cotangent_rows, value_rows)
    table = lax.all_to_all(sent, SLABS, 0, 0, tiled=True)
    cores = [(0, 1), (1, 0)]
    ups = [(i, i + 1) for i in range(n_slab - 1)]
    outward = [(2 * i, 2 * j) for i, j in ups] + [(2 * j + 1, 2 * i + 1) for i, j in ups]
    sent_planes = jnp.stack([keep, lax.ppermute(give, "ch", cores)])
    own_other = lax.ppermute(own, "ch", cores)
    received = lax.ppermute(sent_planes, SLABS + ("ch",), outward)

    cube = (4, 4, 4, slots, width)
    face = (4, 4, slots, width)
    middle_shape = (4, 6, 6, slots, 2 * width)
    middle = call(
        halo_kernel,
        jax.ShapeDtypeStruct(middle_shape, BF16),
        [SMEM, VMEM, ANY, ANY],
        [pltpu.SemaphoreType.DMA((2,))],
        flops=10**9,
        mib=24,
    )(
        core,
        neighbours,
        pltpu.with_memory_space_constraint(own.reshape(cube), pltpu.HBM),
        own_other.reshape(cube),
    )

    table, received = lax.optimization_barrier((table, received))
    theirs = lax.ppermute(received, "ch", cores)
    grid_shape = pltpu.HBM((6, 6, 6, slots, 2 * width), BF16)

    term_shape = jax.ShapeDtypeStruct((3, 9, width, 2 * width), BF16)
    weight_term, grid, norm = call(
        weight_grad_kernel,
        [term_shape, grid_shape, jax.ShapeDtypeStruct((8, 128), F32)],
        [SMEM, SMEM, VMEM, VMEM, VMEM, VMEM, ANY, ANY, VMEM, VMEM],
        [
            pltpu.VMEM((rows, width), F32),
            pltpu.VMEM((2, 6, 6, slots, 2 * width), BF16),
            pltpu.VMEM((2, 4, 4, slots, 2 * width), BF16),
            pltpu.VMEM((4 * width, 16 * slots), BF16),
            pltpu.VMEM((3, width, 2 * width), F32),
            pltpu.VMEM(term_shape.shape, BF16),
            pltpu.SemaphoreType.DMA((4,)),
            pltpu.SemaphoreType.DMA((6,)),
            pltpu.SemaphoreType.DMA((3, 2)),
        ],
        [HBM, HBM, VMEM],
        flops=work,
        mib=24,
    )(
        counts,
        core,
        neighbours,
        table,
        gain_row,
        shift_row,
        received.reshape((2,) + face),
        theirs.reshape((2,) + face),
        value_rows,
        middle,
    )
    piece = 27 * width // n_plane
    parts = lax.all_to_all(
        weight_term.reshape(n_plane, piece, 2 * width), PLANE, 0, 0, tiled=True
    )

    grad_pre, sums = call(
        act_grad_kernel,
        [
            jax.ShapeDtypeStruct((voxels, slots, width), F32),
            jax.ShapeDtypeStruct((1, 2 * width), F32),
        ],
        [SMEM] + [VMEM] * 6,
        [pltpu.VMEM((4, 16, slots, width), F32), pltpu.VMEM((rows, width), F32)],
        flops=work,
        mib=58,
    )(
        counts,
        norm,
        gain_row,
        shift_row,
        value_rows,
        weight.reshape(3, 9, width, 2 * width),
        grid,
    )

    part = jnp.sum(parts.astype(F32), axis=0).reshape(n_line, piece // n_line, 2 * width)
    part = jnp.concatenate(
        [part, jnp.broadcast_to(sums.reshape(1, 1, 2 * width), (n_line, 1, 2 * width))], axis=1
    )
    part = jnp.sum(lax.all_to_all(part, "z", 0, 0, tiled=True), axis=0)
    final, line_sums = part[:-1].astype(BF16), part[-1:]
    line = jnp.broadcast_to(final[None], (n_line,) + final.shape)
    line = lax.all_to_all(line, "z", 0, 0, tiled=True).reshape(piece, 2 * width)
    split = []
    rest = line_sums
    for _ in range(3):
        top = lax.reduce_precision(rest, 8, 7)
        split.append(top.astype(BF16))
        rest = rest - top
    line = jnp.concatenate([line] + split + [jnp.zeros((5, 2 * width), BF16)], axis=0)
    plane = jnp.broadcast_to(line[None], (n_plane,) + line.shape)
    plane = lax.all_to_all(plane, PLANE, 0, 0, tiled=True)
    grad_features, grad_weight, grad_gain, grad_shift = call(
        last_kernel,
        [
            jax.ShapeDtypeStruct((rows, width), BF16),
            jax.ShapeDtypeStruct((27 * width, 2 * width), F32),
            jax.ShapeDtypeStruct((1, width), F32),
            jax.ShapeDtypeStruct((1, width), F32),
        ],
        [SMEM] + [VMEM] * 6,
        [
            pltpu.VMEM((rows, width), BF16),
            pltpu.VMEM((27 * width, 2 * width), F32),
            pltpu.SemaphoreType.DMA((4,)),
            pltpu.SemaphoreType.DMA((n_plane,)),
        ],
        [HBM, HBM, VMEM, VMEM],
        mib=20,
    )(
        counts,
        norm,
        gain_row,
        plane,
        value_rows,
        cotangent_rows,
        grad_pre.reshape(rows, width),
    )
    return (
        grad_features.reshape(features.shape),
        grad_weight.reshape(27, width, 2 * width),
        grad_gain.reshape(width),
        grad_shift.reshape(width),
    )


def solution(mesh):
    slabs = mesh.devices.shape[0]
    inner = Mesh(mesh.devices.reshape(CUT[slabs] + (2,)), SLABS + ("ch",))
    in_specs = (
        P(SLABS, None, "ch"),
        P(SLABS, None, "ch"),
        P(None, "ch", None),
        P("ch"),
        P("ch"),
        P(SLABS),
        P(SLABS, None),
    )
    out_specs = (P(SLABS, None, "ch"), P(None, "ch", None), P("ch"), P("ch"))
    return jax.shard_map(body, mesh=inner, in_specs=in_specs, out_specs=out_specs, check_vma=False)
```

```python
import functools

import jax
import jax.numpy as jnp
from jax import lax
from jax.experimental import pallas as pl
from jax.experimental.pallas import tpu as pltpu
from jax.sharding import Mesh
from jax.sharding import PartitionSpec as P

GROUP_CH = 8
PITCH = 72
BATCHES = (3, 6, 8)
CUT = {128: (8, 4, 4), 8: (2, 2, 2), 4: (2, 2, 1)}
SLABS = ("z", "x", "y")
PLANE = ("x", "y")
F32 = jnp.float32
BF16 = jnp.bfloat16
VMEM = pl.BlockSpec(memory_space=pltpu.VMEM)
SMEM = pl.BlockSpec(memory_space=pltpu.SMEM)
HBM = pl.BlockSpec(memory_space=pltpu.HBM)
ANY = pl.BlockSpec(memory_space=pl.ANY)


def call(kernel, out_shape, in_specs, scratch=(), out_specs=VMEM, flops=0, mib=52, aliases=None):
    if isinstance(out_shape, (list, tuple)) and out_specs is VMEM:
        out_specs = [VMEM] * len(out_shape)
    return pl.pallas_call(
        kernel,
        out_shape=out_shape,
        in_specs=in_specs,
        out_specs=out_specs,
        scratch_shapes=list(scratch),
        input_output_aliases=aliases or {},
        compiler_params=pltpu.CompilerParams(vmem_limit_bytes=mib * 1024 * 1024),
        cost_estimate=pl.CostEstimate(flops=flops, bytes_accessed=0, transcendentals=0),
    )


def exact_dot(left, right):
    return jnp.dot(left, right, precision=lax.Precision.HIGHEST, preferred_element_type=F32)


def iota(shape, dim):
    return lax.broadcasted_iota(jnp.int32, shape, dim)


def turned(rows_ref, out_ref):
    slots = out_ref.shape[1]
    for voxel in range(64):
        out_ref[voxel] = rows_ref[pl.ds(voxel, slots, stride=PITCH), :].astype(out_ref.dtype)


def fetch(source, target, sems, pieces):
    step = source.shape[0] // pieces
    copies = [
        pltpu.make_async_copy(
            source.at[pl.ds(at * step, step)], target.at[pl.ds(at * step, step)], sems.at[at]
        )
        for at in range(pieces)
    ]
    for copy in copies:
        copy.start()
    return copies


def widen(held_ref, rows_ref, copies=()):
    slots = held_ref.shape[0] // 64
    step = slots // max(len(copies), 1)
    for slot in range(slots):
        if copies and slot % step == 0:
            copies[slot // step].wait()
        rows = held_ref[slot * 64 : slot * 64 + 64, :].astype(F32)
        rows_ref[slot * PITCH : slot * PITCH + 64, :] = rows


def prepare_kernel(
    counts_ref,
    core_ref,
    cotangent_hbm,
    values_hbm,
    own_hbm,
    give_hbm,
    keep_hbm,
    sent_ref,
    held_ref,
    rows_ref,
    own_ref,
    sems,
    out_sems,
):
    slots = own_ref.shape[1]
    turns = fetch(cotangent_hbm, held_ref.at[0], sems.at[0], 4)
    copies = fetch(values_hbm, held_ref.at[1], sems.at[1], 4)
    core = core_ref[0]
    count = counts_ref[0]
    widen(held_ref.at[0], rows_ref, turns)
    turned(rows_ref, own_ref)
    sends = [
        pltpu.make_async_copy(own_ref.at[pl.ds(48 * core, 16)], give_hbm, out_sems.at[0]),
        pltpu.make_async_copy(own_ref.at[pl.ds(48 - 48 * core, 16)], keep_hbm, out_sems.at[1]),
        pltpu.make_async_copy(own_ref, own_hbm, out_sems.at[2]),
    ]
    for send in sends:
        send.start()
    widen(held_ref.at[1], rows_ref, copies)

    def over_slots(term):
        total = jnp.zeros((8, 128), F32)
        for slot in range(slots):
            rows = term(rows_ref[slot * PITCH : slot * PITCH + 64, :]).reshape(8, 8, 128).sum(axis=0)
            total = total + jnp.where(slot < count, rows, 0.0)
        return jnp.broadcast_to(jnp.sum(total, axis=0, keepdims=True), (8, 128))

    lane_in, lane_out = iota((128, 128), 0), iota((128, 128), 1)
    same = (lane_in // GROUP_CH == lane_out // GROUP_CH).astype(F32)
    to_sum = (lane_in // GROUP_CH == lane_out).astype(F32)
    to_square = (lane_in // GROUP_CH + 16 == lane_out).astype(F32)
    total = over_slots(lambda rows: rows)
    entries = count.astype(F32) * (64.0 * GROUP_CH)
    mean = (exact_dot(total, same) / entries)[0:1]

    def centred(rows):
        apart = rows - mean
        return apart * apart

    squares = over_slots(centred)
    row = exact_dot(total, to_sum) + exact_dot(squares, to_square)
    row = row + jnp.where(iota((8, 128), 1) == 32, count.astype(F32), 0.0)
    sent_ref[...] = jnp.broadcast_to(row[0:1].reshape(1, 1, 128), sent_ref.shape)
    for send in sends:
        send.wait()


def lanes_of(core):
    mine = pl.ds(pl.multiple_of(core * 128, 128), 128)
    other = pl.ds(pl.multiple_of((1 - core) * 128, 128), 128)
    return mine, other


def side(at):
    return -1 if at == 0 else (1 if at == 5 else 0)


def source(at):
    return {0: 4, 5: 1}.get(at, at)


def offset_of(dx, b, c):
    return 9 * (dx + 1) + 3 * (side(b) + 1) + side(c) + 1


def choose(near, offset, first, last):
    columns = iota((near.shape[0], last - first), 1) + first
    return (near[:, offset : offset + 1] == columns).astype(F32).astype(BF16)


def halo_kernel(core_ref, near_ref, own_ref, own_other_ref, middle_ref, sems):
    slots = near_ref.shape[0]
    mine, other = lanes_of(core_ref[0])
    centre = middle_ref.at[:, 1:5, 1:5]
    copies = [
        pltpu.make_async_copy(own_ref, centre.at[:, :, :, :, mine], sems.at[0]),
        pltpu.make_async_copy(own_other_ref, centre.at[:, :, :, :, other], sems.at[1]),
    ]
    for copy in copies:
        copy.start()
    near = near_ref[...]
    places = [(b, c) for b in range(6) for c in range(6) if side(b) or side(c)]
    picks = {
        offset: choose(near, offset, slots, 2 * slots)
        for offset in sorted({offset_of(0, b, c) for b, c in places})
    }
    for copy in copies:
        copy.wait()
    for plane in range(4):
        for b, c in places:
            middle_ref[plane, b, c] = jnp.dot(
                picks[offset_of(0, b, c)],
                middle_ref[plane, source(b), source(c)],
                preferred_element_type=F32,
            ).astype(BF16)


def window(plane_ref, turn):
    slots = plane_ref.shape[2]
    block = plane_ref[pl.ds(2 - turn // 3, 4), pl.ds(2 - turn % 3, 4)]
    return block.reshape(16 * slots, 256)


def planes_of(plane):
    return max(0, plane - 2), min(3, plane) + 1


def weight_grad_kernel(
    counts_ref,
    core_ref,
    near_ref,
    table_ref,
    gain_ref,
    shift_ref,
    received_ref,
    theirs_ref,
    values_ref,
    middle_ref,
    out_hbm,
    grid_hbm,
    norm_ref,
    rows_ref,
    sides_ref,
    face_ref,
    act_ref,
    total_ref,
    out_ref,
    face_sems,
    plane_sems,
    out_sems,
):
    slots = middle_ref.shape[3]
    core = core_ref[0]
    mine, other = lanes_of(core)
    near_face, far_face = face_ref.at[core], face_ref.at[1 - core]
    faces = [
        pltpu.make_async_copy(received_ref.at[0], near_face.at[:, :, :, mine], face_sems.at[0]),
        pltpu.make_async_copy(received_ref.at[1], near_face.at[:, :, :, other], face_sems.at[1]),
        pltpu.make_async_copy(theirs_ref.at[0], far_face.at[:, :, :, other], face_sems.at[2]),
        pltpu.make_async_copy(theirs_ref.at[1], far_face.at[:, :, :, mine], face_sems.at[3]),
    ]
    for copy in faces:
        copy.start()
    table = table_ref[...]
    held = jnp.sum(table, axis=0)
    voxels = held[:, 32:33] * (64.0 * GROUP_CH)
    entries = table[:, :, 32:33] * (64.0 * GROUP_CH)
    mean = held / voxels
    apart = table / entries - mean.reshape(1, 1, 128)
    between = jnp.sum(apart * apart * entries, axis=0)
    lane_in, lane_out = iota((128, 128), 0), iota((128, 128), 1)
    from_sum = (lane_in == lane_out // GROUP_CH).astype(F32)
    from_square = (lane_in == lane_out // GROUP_CH + 16).astype(F32)

    stacked = jnp.concatenate([mean, between, held, jnp.zeros((5, 128), F32)], axis=0)
    spread = exact_dot(stacked, jnp.concatenate([from_sum, from_square], axis=1))
    mean = spread[0:1, 0:128]
    variance = (spread[1:2, 0:128] + spread[2:3, 128:256]) / voxels
    rstd = lax.rsqrt(variance + 1e-05)
    norm_ref[0:1, :] = mean
    norm_ref[1:2, :] = rstd
    norm_ref[2:3, :] = jnp.broadcast_to(voxels, (1, 128))
    norm_ref[3:8, :] = jnp.zeros((5, 128), F32)
    gain, shift = gain_ref[...], shift_ref[...]
    live = iota((slots, 128), 0) < counts_ref[0]
    widen(values_ref, rows_ref)
    for plane in range(4):
        pieces = []
        for voxel in range(plane * 16, plane * 16 + 16):
            normed = (rows_ref[pl.ds(voxel, slots, stride=PITCH), :] - mean) * rstd
            pre = normed * gain + shift
            pieces.append(jnp.where(live, pre / (1.0 + jnp.exp(-pre)), 0.0))
        rows = jnp.concatenate(pieces, axis=0)
        act_ref[plane * 128 : plane * 128 + 128, :] = rows.T.astype(BF16)
    for copy in faces:
        copy.wait()
    near = near_ref[...]
    places = [(b, c) for b in range(6) for c in range(6)]
    sends = []
    for which, dx in enumerate((-1, 1)):
        lowest = which * slots
        picks = {
            offset: choose(near, offset, lowest, lowest + 2 * slots)
            for offset in sorted({offset_of(dx, b, c) for b, c in places})
        }
        for b, c in places:
            outer = face_ref[which, source(b) - 1, source(c) - 1]
            inner = middle_ref[3 - 3 * which, source(b), source(c)]
            table = [outer, inner] if which == 0 else [inner, outer]
            sides_ref[which, b, c] = jnp.dot(
                picks[offset_of(dx, b, c)],
                jnp.concatenate(table, axis=0),
                preferred_element_type=F32,
            ).astype(BF16)
    planes = [sides_ref.at[0]] + [middle_ref.at[at] for at in range(4)] + [sides_ref.at[1]]
    for at, plane in enumerate(planes):
        sends.append(pltpu.make_async_copy(plane, grid_hbm.at[at], plane_sems.at[at]))
        sends[-1].start()
    for turn in range(9):
        seen = set()
        for plane in range(6):
            first, last = planes_of(plane)
            part = jnp.dot(
                act_ref[first * 128 : last * 128, :],
                window(planes[plane], turn),
                preferred_element_type=F32,
            )
            for at in range(first, last):
                step = at - plane + 2
                term = part[(at - first) * 128 : (at - first) * 128 + 128]
                if step in seen:
                    total_ref[step] += term
                else:
                    total_ref[step] = term
                    seen.add(step)
        for step in range(3):
            out_ref[step, turn] = total_ref[step].astype(BF16)
        if turn in BATCHES:
            batch = BATCHES.index(turn)
            first = BATCHES[batch - 1] + 1 if batch else 0
            part = pl.ds(first, turn + 1 - first)
            for step in range(3):
                sends.append(
                    pltpu.make_async_copy(
                        out_ref.at[step, part], out_hbm.at[step, part], out_sems.at[step, batch]
                    )
                )
                sends[-1].start()
    for send in sends:
        send.wait()


def act_grad_kernel(
    counts_ref,
    norm_ref,
    gain_ref,
    shift_ref,
    values_ref,
    cotangent_ref,
    weight_ref,
    grid_ref,
    out_ref,
    sums_ref,
    total_ref,
    rows_ref,
    cotangent_rows_ref,
):
    slots = grid_ref.shape[3]
    total_ref[...] = jnp.zeros_like(total_ref)
    widen(values_ref, rows_ref)
    widen(cotangent_ref, cotangent_rows_ref)

    @pl.loop(0, 9)
    def _(turn):
        for plane in range(6):
            first, last = planes_of(plane)
            low, high = first - plane + 2, last - plane + 2
            part = lax.dot_general(
                window(grid_ref.at[plane], turn),
                weight_ref[low:high, turn].reshape((high - low) * 128, 256),
                (((1,), (1,)), ((), ())),
                preferred_element_type=F32,
            )
            for at in range(first, last):
                term = part[:, (at - first) * 128 : (at - first) * 128 + 128]
                total_ref[at] += term.reshape(16, slots, 128)

    mean, rstd = norm_ref[0:1, :], norm_ref[1:2, :]
    gain, shift = gain_ref[...], shift_ref[...]
    live = iota((slots, 128), 0) < counts_ref[0]
    scale = rstd * gain
    shift_sum = jnp.zeros((8, 128), F32)
    gain_sum = jnp.zeros((8, 128), F32)
    for voxel in range(64):
        normed = (rows_ref[pl.ds(voxel, slots, stride=PITCH), :] - mean) * rstd
        pre = normed * gain + shift
        sig = 1.0 / (1.0 + jnp.exp(-pre))
        grad = total_ref[voxel // 16, voxel % 16] * sig * (1.0 + pre * (1.0 - sig))
        grad = jnp.where(live, grad, 0.0)
        places = pl.ds(voxel, slots, stride=PITCH)
        out_ref[places, :] = cotangent_rows_ref[places, :] + scale * grad
        shift_sum = shift_sum + grad.reshape(slots // 8, 8, 128).sum(axis=0)
        gain_sum = gain_sum + (grad * normed).reshape(slots // 8, 8, 128).sum(axis=0)
    sums_ref[:, 0:128] = jnp.sum(shift_sum, axis=0, keepdims=True)
    sums_ref[:, 128:256] = jnp.sum(gain_sum, axis=0, keepdims=True)


def last_kernel(
    counts_ref,
    norm_ref,
    gain_ref,
    plane_ref,
    values_ref,
    part_ref,
    out_hbm,
    weight_hbm,
    gain_out,
    shift_out,
    out_ref,
    weight_ref,
    out_sems,
    weight_sems,
):
    slots = values_ref.shape[0] // 64
    pieces = plane_ref.shape[0]
    piece = weight_ref.shape[0] // pieces
    copies = []
    totals = jnp.zeros((1, 256), F32)
    for at in range(pieces):
        block = plane_ref[at].astype(F32)
        rows = pl.ds(at * piece, piece)
        weight_ref[rows] = block[0:piece]
        totals = totals + (block[piece : piece + 1] + block[piece + 1 : piece + 2])
        totals = totals + block[piece + 2 : piece + 3]
        copies.append(
            pltpu.make_async_copy(weight_ref.at[rows], weight_hbm.at[rows], weight_sems.at[at])
        )
        copies[-1].start()
    shift_sum, gain_sum = totals[:, 0:128], totals[:, 128:256]
    gain_out[...] = gain_sum
    shift_out[...] = shift_sum
    mean, rstd, voxels = norm_ref[0:1, :], norm_ref[1:2, :], norm_ref[2:3, :]
    gain = gain_ref[...]
    lane_in, lane_out = iota((128, 128), 0), iota((128, 128), 1)
    same = (lane_in // GROUP_CH == lane_out // GROUP_CH).astype(F32)

    stacked = jnp.concatenate(
        [gain * shift_sum, gain * gain_sum, jnp.zeros((6, 128), F32)], axis=0
    )
    grouped = exact_dot(stacked, same) / voxels
    constant, slope = rstd * grouped[0:1], rstd * rstd * grouped[1:2]
    chunk = slots // 4
    for slot in range(slots):
        rows = slice(slot * 64, slot * 64 + 64)
        centred = values_ref[rows, :].astype(F32) - mean
        result = part_ref[slot * PITCH : slot * PITCH + 64, :] - constant - centred * slope
        out_ref[rows, :] = jnp.where(slot < counts_ref[0], result, 0.0).astype(BF16)
        if slot % chunk == chunk - 1:
            at = slot // chunk
            rows = pl.ds(at * chunk * 64, chunk * 64)
            copies.append(
                pltpu.make_async_copy(out_ref.at[rows], out_hbm.at[rows], out_sems.at[at])
            )
            copies[-1].start()
    for copy in copies:
        copy.wait()


def body(features, cotangent, weight, gain, shift, counts, neighbours):
    slots, voxels, width = features.shape
    rows = slots * voxels
    n_plane = lax.axis_size("x") * lax.axis_size("y")
    n_line = lax.axis_size("z")
    n_slab = n_plane * n_line
    core = lax.axis_index("ch").astype(jnp.int32).reshape(1)
    turned_shape = jax.ShapeDtypeStruct((voxels, slots, width), BF16)
    face_shape = jax.ShapeDtypeStruct((16, slots, width), BF16)
    gain_row, shift_row = gain.reshape(1, width), shift.reshape(1, width)
    value_rows = features.reshape(rows, width)
    cotangent_rows = cotangent.reshape(rows, width)
    work = 2 * rows * 27 * width * 2 * width

    own, give, keep, sent = call(
        prepare_kernel,
        [
            turned_shape,
            face_shape,
            face_shape,
            jax.ShapeDtypeStruct((n_slab, 1, 128), F32),
        ],
        [SMEM, SMEM, HBM, HBM],
        [
            pltpu.VMEM((2, rows, width), BF16),
            pltpu.VMEM((slots * PITCH, width), F32),
            pltpu.VMEM(turned_shape.shape, BF16),
            pltpu.SemaphoreType.DMA((2, 4)),
            pltpu.SemaphoreType.DMA((3,)),
        ],
        [HBM, HBM, HBM, VMEM],
        mib=60,
    )(counts, core, cotangent_rows, value_rows)
    table = lax.all_to_all(sent, SLABS, 0, 0, tiled=True)
    cores = [(0, 1), (1, 0)]
    ups = [(i, i + 1) for i in range(n_slab - 1)]
    outward = [(2 * i, 2 * j) for i, j in ups] + [(2 * j + 1, 2 * i + 1) for i, j in ups]
    sent_planes = jnp.stack([keep, lax.ppermute(give, "ch", cores)])
    own_other = lax.ppermute(own, "ch", cores)
    received = lax.ppermute(sent_planes, SLABS + ("ch",), outward)

    cube = (4, 4, 4, slots, width)
    face = (4, 4, slots, width)
    middle_shape = (4, 6, 6, slots, 2 * width)
    middle = call(
        halo_kernel,
        jax.ShapeDtypeStruct(middle_shape, BF16),
        [SMEM, VMEM, ANY, ANY],
        [pltpu.SemaphoreType.DMA((2,))],
        flops=10**9,
        mib=24,
    )(
        core,
        neighbours,
        pltpu.with_memory_space_constraint(own.reshape(cube), pltpu.HBM),
        own_other.reshape(cube),
    )

    table, received = lax.optimization_barrier((table, received))
    theirs = lax.ppermute(received, "ch", cores)
    grid_shape = pltpu.HBM((6, 6, 6, slots, 2 * width), BF16)

    term_shape = jax.ShapeDtypeStruct((3, 9, width, 2 * width), BF16)
    weight_term, grid, norm = call(
        weight_grad_kernel,
        [term_shape, grid_shape, pltpu.HBM((8, 128), F32)],
        [SMEM, SMEM, VMEM, VMEM, VMEM, VMEM, ANY, ANY, VMEM, VMEM],
        [
            pltpu.VMEM((slots * PITCH, width), F32),
            pltpu.VMEM((2, 6, 6, slots, 2 * width), BF16),
            pltpu.VMEM((2, 4, 4, slots, 2 * width), BF16),
            pltpu.VMEM((4 * width, 16 * slots), BF16),
            pltpu.VMEM((3, width, 2 * width), F32),
            pltpu.VMEM(term_shape.shape, BF16),
            pltpu.SemaphoreType.DMA((4,)),
            pltpu.SemaphoreType.DMA((6,)),
            pltpu.SemaphoreType.DMA((3, len(BATCHES))),
        ],
        [HBM, HBM, VMEM],
        flops=work,
        mib=24,
    )(
        counts,
        core,
        neighbours,
        table,
        gain_row,
        shift_row,
        received.reshape((2,) + face),
        theirs.reshape((2,) + face),
        value_rows,
        middle,
    )
    piece = 27 * width // n_plane
    parts = lax.all_to_all(
        weight_term.reshape(n_plane, piece, 2 * width), PLANE, 0, 0, tiled=True
    )

    feature_part, sums = call(
        act_grad_kernel,
        [
            jax.ShapeDtypeStruct((slots * PITCH, width), F32),
            jax.ShapeDtypeStruct((1, 2 * width), F32),
        ],
        [SMEM] + [VMEM] * 7,
        [pltpu.VMEM((4, 16, slots, width), F32)] + [pltpu.VMEM((slots * PITCH, width), F32)] * 2,
        flops=work,
        mib=58,
    )(
        counts,
        norm,
        gain_row,
        shift_row,
        value_rows,
        cotangent_rows,
        weight.reshape(3, 9, width, 2 * width),
        grid,
    )

    part = jnp.sum(parts.astype(F32), axis=0).reshape(n_line, piece // n_line, 2 * width)
    part = jnp.concatenate(
        [part, jnp.broadcast_to(sums.reshape(1, 1, 2 * width), (n_line, 1, 2 * width))], axis=1
    )
    part = jnp.sum(lax.all_to_all(part, "z", 0, 0, tiled=True), axis=0)
    final = part[:-1].astype(BF16)
    line = jnp.broadcast_to(final[None], (n_line,) + final.shape)
    line = lax.all_to_all(line, "z", 0, 0, tiled=True).reshape(piece, 2 * width)
    line, part = lax.optimization_barrier((line, part))
    rest = part[-1:]
    split = []
    for _ in range(3):
        top = lax.reduce_precision(rest, 8, 7)
        split.append(top.astype(BF16))
        rest = rest - top
    line = jnp.concatenate([line] + split + [jnp.zeros((5, 2 * width), BF16)], axis=0)
    plane = jnp.broadcast_to(line[None], (n_plane,) + line.shape)
    plane = lax.all_to_all(plane, PLANE, 0, 0, tiled=True)
    grad_features, grad_weight, grad_gain, grad_shift = call(
        last_kernel,
        [
            jax.ShapeDtypeStruct((rows, width), BF16),
            jax.ShapeDtypeStruct((27 * width, 2 * width), F32),
            jax.ShapeDtypeStruct((1, width), F32),
            jax.ShapeDtypeStruct((1, width), F32),
        ],
        [SMEM] + [VMEM] * 5,
        [
            pltpu.VMEM((rows, width), BF16),
            pltpu.VMEM((27 * width, 2 * width), F32),
            pltpu.SemaphoreType.DMA((4,)),
            pltpu.SemaphoreType.DMA((n_plane,)),
        ],
        [HBM, HBM, VMEM, VMEM],
        mib=20,
    )(
        counts,
        norm,
        gain_row,
        plane,
        value_rows,
        feature_part,
    )
    return (
        grad_features.reshape(features.shape),
        grad_weight.reshape(27, width, 2 * width),
        grad_gain.reshape(width),
        grad_shift.reshape(width),
    )


def solution(mesh):
    slabs = mesh.devices.shape[0]
    inner = Mesh(mesh.devices.reshape(CUT[slabs] + (2,)), SLABS + ("ch",))
    in_specs = (
        P(SLABS, None, "ch"),
        P(SLABS, None, "ch"),
        P(None, "ch", None),
        P("ch"),
        P("ch"),
        P(SLABS),
        P(SLABS, None),
    )
    out_specs = (P(SLABS, None, "ch"), P(None, "ch", None), P("ch"), P("ch"))
    return jax.shard_map(body, mesh=inner, in_specs=in_specs, out_specs=out_specs, check_vma=False)
```

```python
import functools

import jax
import jax.numpy as jnp
from jax import lax
from jax.experimental import pallas as pl
from jax.experimental.pallas import tpu as pltpu
from jax.sharding import Mesh
from jax.sharding import PartitionSpec as P

GROUP_CH = 8
PITCH = 72
BATCHES = (3, 6, 8)
CUT = {128: (8, 4, 4), 8: (2, 2, 2), 4: (2, 2, 1)}
SLABS = ("z", "x", "y")
PLANE = ("x", "y")
F32 = jnp.float32
BF16 = jnp.bfloat16
VMEM = pl.BlockSpec(memory_space=pltpu.VMEM)
SMEM = pl.BlockSpec(memory_space=pltpu.SMEM)
HBM = pl.BlockSpec(memory_space=pltpu.HBM)
ANY = pl.BlockSpec(memory_space=pl.ANY)


def call(kernel, out_shape, in_specs, scratch=(), out_specs=VMEM, flops=0, mib=52, aliases=None):
    if isinstance(out_shape, (list, tuple)) and out_specs is VMEM:
        out_specs = [VMEM] * len(out_shape)
    return pl.pallas_call(
        kernel,
        out_shape=out_shape,
        in_specs=in_specs,
        out_specs=out_specs,
        scratch_shapes=list(scratch),
        input_output_aliases=aliases or {},
        compiler_params=pltpu.CompilerParams(vmem_limit_bytes=mib * 1024 * 1024),
        cost_estimate=pl.CostEstimate(flops=flops, bytes_accessed=0, transcendentals=0),
    )


def exact_dot(left, right):
    return jnp.dot(left, right, precision=lax.Precision.HIGHEST, preferred_element_type=F32)


def iota(shape, dim):
    return lax.broadcasted_iota(jnp.int32, shape, dim)


def turned(rows_ref, out_ref):
    slots = out_ref.shape[1]
    for voxel in range(64):
        out_ref[voxel] = rows_ref[pl.ds(voxel, slots, stride=PITCH), :].astype(out_ref.dtype)


def fetch(source, target, sems, pieces):
    step = source.shape[0] // pieces
    copies = [
        pltpu.make_async_copy(
            source.at[pl.ds(at * step, step)], target.at[pl.ds(at * step, step)], sems.at[at]
        )
        for at in range(pieces)
    ]
    for copy in copies:
        copy.start()
    return copies


def widen(held_ref, rows_ref, copies=()):
    slots = held_ref.shape[0] // 64
    step = slots // max(len(copies), 1)
    for slot in range(slots):
        if copies and slot % step == 0:
            copies[slot // step].wait()
        rows = held_ref[slot * 64 : slot * 64 + 64, :].astype(F32)
        rows_ref[slot * PITCH : slot * PITCH + 64, :] = rows


def prepare_kernel(
    counts_ref,
    core_ref,
    cotangent_hbm,
    values_hbm,
    own_hbm,
    give_hbm,
    keep_hbm,
    sent_ref,
    held_ref,
    rows_ref,
    own_ref,
    sems,
    out_sems,
):
    slots = own_ref.shape[1]
    turns = fetch(cotangent_hbm, held_ref.at[0], sems.at[0], 4)
    copies = fetch(values_hbm, held_ref.at[1], sems.at[1], 4)
    core = core_ref[0]
    count = counts_ref[0]
    widen(held_ref.at[0], rows_ref, turns)
    turned(rows_ref, own_ref)
    sends = [
        pltpu.make_async_copy(own_ref.at[pl.ds(48 * core, 16)], give_hbm, out_sems.at[0]),
        pltpu.make_async_copy(own_ref.at[pl.ds(48 - 48 * core, 16)], keep_hbm, out_sems.at[1]),
        pltpu.make_async_copy(own_ref, own_hbm, out_sems.at[2]),
    ]
    for send in sends:
        send.start()
    widen(held_ref.at[1], rows_ref, copies)

    def over_slots(term):
        total = jnp.zeros((8, 128), F32)
        for slot in range(slots):
            rows = term(rows_ref[slot * PITCH : slot * PITCH + 64, :]).reshape(8, 8, 128).sum(axis=0)
            total = total + jnp.where(slot < count, rows, 0.0)
        return jnp.broadcast_to(jnp.sum(total, axis=0, keepdims=True), (8, 128))

    lane_in, lane_out = iota((128, 128), 0), iota((128, 128), 1)
    same = (lane_in // GROUP_CH == lane_out // GROUP_CH).astype(F32)
    to_sum = (lane_in // GROUP_CH == lane_out).astype(F32)
    to_square = (lane_in // GROUP_CH + 16 == lane_out).astype(F32)
    total = over_slots(lambda rows: rows)
    entries = count.astype(F32) * (64.0 * GROUP_CH)
    mean = (exact_dot(total, same) / entries)[0:1]

    def centred(rows):
        apart = rows - mean
        return apart * apart

    squares = over_slots(centred)
    row = exact_dot(total, to_sum) + exact_dot(squares, to_square)
    row = row + jnp.where(iota((8, 128), 1) == 32, count.astype(F32), 0.0)
    sent_ref[...] = jnp.broadcast_to(row[0:1].reshape(1, 1, 128), sent_ref.shape)
    for send in sends:
        send.wait()


def lanes_of(core):
    mine = pl.ds(pl.multiple_of(core * 128, 128), 128)
    other = pl.ds(pl.multiple_of((1 - core) * 128, 128), 128)
    return mine, other


def side(at):
    return -1 if at == 0 else (1 if at == 5 else 0)


def source(at):
    return {0: 4, 5: 1}.get(at, at)


def offset_of(dx, b, c):
    return 9 * (dx + 1) + 3 * (side(b) + 1) + side(c) + 1


def choose(near, offset, first, last):
    columns = iota((near.shape[0], last - first), 1) + first
    return (near[:, offset : offset + 1] == columns).astype(F32).astype(BF16)


def sources(places):
    readers = {}
    for b, c in places:
        readers.setdefault((source(b), source(c)), []).append((b, c))
    return readers


def gathered(picks, table):
    rows = jnp.dot(jnp.concatenate(picks, axis=0), table, preferred_element_type=F32).astype(BF16)
    slots = picks[0].shape[0]
    return [rows[at * slots : at * slots + slots] for at in range(len(picks))]


def halo_kernel(core_ref, near_ref, own_ref, own_other_ref, middle_ref, sems):
    slots = near_ref.shape[0]
    mine, other = lanes_of(core_ref[0])
    centre = middle_ref.at[:, 1:5, 1:5]
    copies = [
        pltpu.make_async_copy(own_ref, centre.at[:, :, :, :, mine], sems.at[0]),
        pltpu.make_async_copy(own_other_ref, centre.at[:, :, :, :, other], sems.at[1]),
    ]
    for copy in copies:
        copy.start()
    near = near_ref[...]
    places = [(b, c) for b in range(6) for c in range(6) if side(b) or side(c)]
    picks = {
        offset: choose(near, offset, slots, 2 * slots)
        for offset in sorted({offset_of(0, b, c) for b, c in places})
    }
    for copy in copies:
        copy.wait()
    for plane in range(4):
        for (b, c), readers in sources(places).items():
            rows = gathered([picks[offset_of(0, *at)] for at in readers], middle_ref[plane, b, c])
            for at, block in zip(readers, rows):
                middle_ref[plane, at[0], at[1]] = block


def window(plane_ref, turn):
    slots = plane_ref.shape[2]
    block = plane_ref[pl.ds(2 - turn // 3, 4), pl.ds(2 - turn % 3, 4)]
    return block.reshape(16 * slots, 256)


def planes_of(plane):
    return max(0, plane - 2), min(3, plane) + 1


def weight_grad_kernel(
    counts_ref,
    core_ref,
    near_ref,
    table_ref,
    gain_ref,
    shift_ref,
    received_ref,
    theirs_ref,
    values_ref,
    middle_ref,
    out_hbm,
    grid_hbm,
    norm_ref,
    rows_ref,
    sides_ref,
    face_ref,
    act_ref,
    total_ref,
    out_ref,
    face_sems,
    plane_sems,
    out_sems,
):
    slots = middle_ref.shape[3]
    core = core_ref[0]
    mine, other = lanes_of(core)
    near_face, far_face = face_ref.at[core], face_ref.at[1 - core]
    faces = [
        pltpu.make_async_copy(received_ref.at[0], near_face.at[:, :, :, mine], face_sems.at[0]),
        pltpu.make_async_copy(received_ref.at[1], near_face.at[:, :, :, other], face_sems.at[1]),
        pltpu.make_async_copy(theirs_ref.at[0], far_face.at[:, :, :, other], face_sems.at[2]),
        pltpu.make_async_copy(theirs_ref.at[1], far_face.at[:, :, :, mine], face_sems.at[3]),
    ]
    for copy in faces:
        copy.start()
    table = table_ref[...]
    held = jnp.sum(table, axis=0)
    voxels = held[:, 32:33] * (64.0 * GROUP_CH)
    entries = table[:, :, 32:33] * (64.0 * GROUP_CH)
    mean = held / voxels
    apart = table / entries - mean.reshape(1, 1, 128)
    between = jnp.sum(apart * apart * entries, axis=0)
    lane_in, lane_out = iota((128, 128), 0), iota((128, 128), 1)
    from_sum = (lane_in == lane_out // GROUP_CH).astype(F32)
    from_square = (lane_in == lane_out // GROUP_CH + 16).astype(F32)

    stacked = jnp.concatenate([mean, between, held, jnp.zeros((5, 128), F32)], axis=0)
    spread = exact_dot(stacked, jnp.concatenate([from_sum, from_square], axis=1))
    mean = spread[0:1, 0:128]
    variance = (spread[1:2, 0:128] + spread[2:3, 128:256]) / voxels
    rstd = lax.rsqrt(variance + 1e-05)
    norm_ref[0:1, :] = mean
    norm_ref[1:2, :] = rstd
    norm_ref[2:3, :] = jnp.broadcast_to(voxels, (1, 128))
    norm_ref[3:8, :] = jnp.zeros((5, 128), F32)
    gain, shift = gain_ref[...], shift_ref[...]
    live = iota((slots, 128), 0) < counts_ref[0]
    widen(values_ref, rows_ref)
    for plane in range(4):
        pieces = []
        for voxel in range(plane * 16, plane * 16 + 16):
            normed = (rows_ref[pl.ds(voxel, slots, stride=PITCH), :] - mean) * rstd
            pre = normed * gain + shift
            pieces.append(jnp.where(live, pre / (1.0 + jnp.exp(-pre)), 0.0))
        rows = jnp.concatenate(pieces, axis=0)
        act_ref[plane * 128 : plane * 128 + 128, :] = rows.T.astype(BF16)
    for copy in faces:
        copy.wait()
    near = near_ref[...]
    places = [(b, c) for b in range(6) for c in range(6)]
    sends = []
    for which, dx in enumerate((-1, 1)):
        lowest = which * slots
        picks = {
            offset: choose(near, offset, lowest, lowest + 2 * slots)
            for offset in sorted({offset_of(dx, b, c) for b, c in places})
        }
        for (b, c), readers in sources(places).items():
            outer = face_ref[which, b - 1, c - 1]
            inner = middle_ref[3 - 3 * which, b, c]
            table = jnp.concatenate([outer, inner] if which == 0 else [inner, outer], axis=0)
            rows = gathered([picks[offset_of(dx, *at)] for at in readers], table)
            for at, block in zip(readers, rows):
                sides_ref[which, at[0], at[1]] = block
    planes = [sides_ref.at[0]] + [middle_ref.at[at] for at in range(4)] + [sides_ref.at[1]]
    for at, plane in enumerate(planes):
        sends.append(pltpu.make_async_copy(plane, grid_hbm.at[at], plane_sems.at[at]))
        sends[-1].start()
    for turn in range(9):
        seen = set()
        for plane in range(6):
            first, last = planes_of(plane)
            part = jnp.dot(
                act_ref[first * 128 : last * 128, :],
                window(planes[plane], turn),
                preferred_element_type=F32,
            )
            for at in range(first, last):
                step = at - plane + 2
                term = part[(at - first) * 128 : (at - first) * 128 + 128]
                if step in seen:
                    total_ref[step] += term
                else:
                    total_ref[step] = term
                    seen.add(step)
        for step in range(3):
            out_ref[step, turn] = total_ref[step].astype(BF16)
        if turn in BATCHES:
            batch = BATCHES.index(turn)
            first = BATCHES[batch - 1] + 1 if batch else 0
            part = pl.ds(first, turn + 1 - first)
            for step in range(3):
                sends.append(
                    pltpu.make_async_copy(
                        out_ref.at[step, part], out_hbm.at[step, part], out_sems.at[step, batch]
                    )
                )
                sends[-1].start()
    for send in sends:
        send.wait()


def act_grad_kernel(
    counts_ref,
    norm_ref,
    gain_ref,
    shift_ref,
    values_ref,
    cotangent_ref,
    weight_ref,
    grid_ref,
    out_ref,
    sums_ref,
    total_ref,
    rows_ref,
    cotangent_rows_ref,
):
    slots = grid_ref.shape[3]
    total_ref[...] = jnp.zeros_like(total_ref)
    widen(values_ref, rows_ref)
    widen(cotangent_ref, cotangent_rows_ref)

    @pl.loop(0, 9)
    def _(turn):
        for plane in range(6):
            first, last = planes_of(plane)
            low, high = first - plane + 2, last - plane + 2
            part = lax.dot_general(
                window(grid_ref.at[plane], turn),
                weight_ref[low:high, turn].reshape((high - low) * 128, 256),
                (((1,), (1,)), ((), ())),
                preferred_element_type=F32,
            )
            for at in range(first, last):
                term = part[:, (at - first) * 128 : (at - first) * 128 + 128]
                total_ref[at] += term.reshape(16, slots, 128)

    mean, rstd = norm_ref[0:1, :], norm_ref[1:2, :]
    gain, shift = gain_ref[...], shift_ref[...]
    live = iota((slots, 128), 0) < counts_ref[0]
    scale = rstd * gain
    shift_sum = jnp.zeros((8, 128), F32)
    gain_sum = jnp.zeros((8, 128), F32)
    for voxel in range(64):
        normed = (rows_ref[pl.ds(voxel, slots, stride=PITCH), :] - mean) * rstd
        pre = normed * gain + shift
        sig = 1.0 / (1.0 + jnp.exp(-pre))
        grad = total_ref[voxel // 16, voxel % 16] * sig * (1.0 + pre * (1.0 - sig))
        grad = jnp.where(live, grad, 0.0)
        places = pl.ds(voxel, slots, stride=PITCH)
        out_ref[places, :] = cotangent_rows_ref[places, :] + scale * grad
        shift_sum = shift_sum + grad.reshape(slots // 8, 8, 128).sum(axis=0)
        gain_sum = gain_sum + (grad * normed).reshape(slots // 8, 8, 128).sum(axis=0)
    sums_ref[:, 0:128] = jnp.sum(shift_sum, axis=0, keepdims=True)
    sums_ref[:, 128:256] = jnp.sum(gain_sum, axis=0, keepdims=True)


def last_kernel(
    counts_ref,
    norm_ref,
    gain_ref,
    plane_ref,
    values_ref,
    part_ref,
    out_hbm,
    weight_hbm,
    gain_out,
    shift_out,
    out_ref,
    weight_ref,
    out_sems,
    weight_sems,
):
    slots = values_ref.shape[0] // 64
    pieces = plane_ref.shape[0]
    piece = weight_ref.shape[0] // pieces
    copies = []
    totals = jnp.zeros((1, 256), F32)
    for at in range(pieces):
        block = plane_ref[at].astype(F32)
        rows = pl.ds(at * piece, piece)
        weight_ref[rows] = block[0:piece]
        totals = totals + (block[piece : piece + 1] + block[piece + 1 : piece + 2])
        totals = totals + block[piece + 2 : piece + 3]
        copies.append(
            pltpu.make_async_copy(weight_ref.at[rows], weight_hbm.at[rows], weight_sems.at[at])
        )
        copies[-1].start()
    shift_sum, gain_sum = totals[:, 0:128], totals[:, 128:256]
    gain_out[...] = gain_sum
    shift_out[...] = shift_sum
    mean, rstd, voxels = norm_ref[0:1, :], norm_ref[1:2, :], norm_ref[2:3, :]
    gain = gain_ref[...]
    lane_in, lane_out = iota((128, 128), 0), iota((128, 128), 1)
    same = (lane_in // GROUP_CH == lane_out // GROUP_CH).astype(F32)

    stacked = jnp.concatenate(
        [gain * shift_sum, gain * gain_sum, jnp.zeros((6, 128), F32)], axis=0
    )
    grouped = exact_dot(stacked, same) / voxels
    constant, slope = rstd * grouped[0:1], rstd * rstd * grouped[1:2]
    chunk = slots // 4
    for slot in range(slots):
        rows = slice(slot * 64, slot * 64 + 64)
        centred = values_ref[rows, :].astype(F32) - mean
        result = part_ref[slot * PITCH : slot * PITCH + 64, :] - constant - centred * slope
        out_ref[rows, :] = jnp.where(slot < counts_ref[0], result, 0.0).astype(BF16)
        if slot % chunk == chunk - 1:
            at = slot // chunk
            rows = pl.ds(at * chunk * 64, chunk * 64)
            copies.append(
                pltpu.make_async_copy(out_ref.at[rows], out_hbm.at[rows], out_sems.at[at])
            )
            copies[-1].start()
    for copy in copies:
        copy.wait()


def body(features, cotangent, weight, gain, shift, counts, neighbours):
    slots, voxels, width = features.shape
    rows = slots * voxels
    n_plane = lax.axis_size("x") * lax.axis_size("y")
    n_line = lax.axis_size("z")
    n_slab = n_plane * n_line
    core = lax.axis_index("ch").astype(jnp.int32).reshape(1)
    turned_shape = jax.ShapeDtypeStruct((voxels, slots, width), BF16)
    face_shape = jax.ShapeDtypeStruct((16, slots, width), BF16)
    gain_row, shift_row = gain.reshape(1, width), shift.reshape(1, width)
    value_rows = features.reshape(rows, width)
    cotangent_rows = cotangent.reshape(rows, width)
    work = 2 * rows * 27 * width * 2 * width

    own, give, keep, sent = call(
        prepare_kernel,
        [
            turned_shape,
            face_shape,
            face_shape,
            jax.ShapeDtypeStruct((n_slab, 1, 128), F32),
        ],
        [SMEM, SMEM, HBM, HBM],
        [
            pltpu.VMEM((2, rows, width), BF16),
            pltpu.VMEM((slots * PITCH, width), F32),
            pltpu.VMEM(turned_shape.shape, BF16),
            pltpu.SemaphoreType.DMA((2, 4)),
            pltpu.SemaphoreType.DMA((3,)),
        ],
        [HBM, HBM, HBM, VMEM],
        mib=36,
    )(
        counts,
        core,
        pltpu.with_memory_space_constraint(cotangent_rows, pltpu.HBM),
        pltpu.with_memory_space_constraint(value_rows, pltpu.HBM),
    )
    table = lax.all_to_all(sent, SLABS, 0, 0, tiled=True)
    cores = [(0, 1), (1, 0)]
    ups = [(i, i + 1) for i in range(n_slab - 1)]
    outward = [(2 * i, 2 * j) for i, j in ups] + [(2 * j + 1, 2 * i + 1) for i, j in ups]
    sent_planes = jnp.stack([keep, lax.ppermute(give, "ch", cores)])
    own_other = lax.ppermute(own, "ch", cores)
    received = lax.ppermute(sent_planes, SLABS + ("ch",), outward)

    cube = (4, 4, 4, slots, width)
    face = (4, 4, slots, width)
    middle_shape = (4, 6, 6, slots, 2 * width)
    middle = call(
        halo_kernel,
        jax.ShapeDtypeStruct(middle_shape, BF16),
        [SMEM, VMEM, ANY, ANY],
        [pltpu.SemaphoreType.DMA((2,))],
        flops=10**9,
        mib=24,
    )(
        core,
        neighbours,
        own.reshape(cube),
        own_other.reshape(cube),
    )

    table, received = lax.optimization_barrier((table, received))
    theirs = lax.ppermute(received, "ch", cores)
    grid_shape = pltpu.HBM((6, 6, 6, slots, 2 * width), BF16)

    term_shape = jax.ShapeDtypeStruct((3, 9, width, 2 * width), BF16)
    weight_term, grid, norm = call(
        weight_grad_kernel,
        [term_shape, grid_shape, pltpu.HBM((8, 128), F32)],
        [SMEM, SMEM, VMEM, VMEM, VMEM, VMEM, ANY, ANY, VMEM, VMEM],
        [
            pltpu.VMEM((slots * PITCH, width), F32),
            pltpu.VMEM((2, 6, 6, slots, 2 * width), BF16),
            pltpu.VMEM((2, 4, 4, slots, 2 * width), BF16),
            pltpu.VMEM((4 * width, 16 * slots), BF16),
            pltpu.VMEM((3, width, 2 * width), F32),
            pltpu.VMEM(term_shape.shape, BF16),
            pltpu.SemaphoreType.DMA((4,)),
            pltpu.SemaphoreType.DMA((6,)),
            pltpu.SemaphoreType.DMA((3, len(BATCHES))),
        ],
        [HBM, HBM, VMEM],
        flops=work,
        mib=24,
    )(
        counts,
        core,
        neighbours,
        table,
        gain_row,
        shift_row,
        received.reshape((2,) + face),
        theirs.reshape((2,) + face),
        value_rows,
        middle,
    )
    piece = 27 * width // n_plane
    parts = lax.all_to_all(
        weight_term.reshape(n_plane, piece, 2 * width), PLANE, 0, 0, tiled=True
    )

    feature_part, sums = call(
        act_grad_kernel,
        [
            jax.ShapeDtypeStruct((slots * PITCH, width), F32),
            jax.ShapeDtypeStruct((1, 2 * width), F32),
        ],
        [SMEM] + [VMEM] * 7,
        [pltpu.VMEM((4, 16, slots, width), F32)] + [pltpu.VMEM((slots * PITCH, width), F32)] * 2,
        flops=work,
        mib=58,
    )(
        counts,
        norm,
        gain_row,
        shift_row,
        value_rows,
        cotangent_rows,
        weight.reshape(3, 9, width, 2 * width),
        grid,
    )

    part = jnp.sum(parts.astype(F32), axis=0).reshape(n_line, piece // n_line, 2 * width)
    part = jnp.concatenate(
        [part, jnp.broadcast_to(sums.reshape(1, 1, 2 * width), (n_line, 1, 2 * width))], axis=1
    )
    part = jnp.sum(lax.all_to_all(part, "z", 0, 0, tiled=True), axis=0)
    final = part[:-1].astype(BF16)
    line = jnp.broadcast_to(final[None], (n_line,) + final.shape)
    line = lax.all_to_all(line, "z", 0, 0, tiled=True).reshape(piece, 2 * width)
    line, part = lax.optimization_barrier((line, part))
    rest = part[-1:]
    split = []
    for _ in range(3):
        top = lax.reduce_precision(rest, 8, 7)
        split.append(top.astype(BF16))
        rest = rest - top
    line = jnp.concatenate([line] + split + [jnp.zeros((5, 2 * width), BF16)], axis=0)
    plane = jnp.broadcast_to(line[None], (n_plane,) + line.shape)
    plane = lax.all_to_all(plane, PLANE, 0, 0, tiled=True)
    grad_features, grad_weight, grad_gain, grad_shift = call(
        last_kernel,
        [
            jax.ShapeDtypeStruct((rows, width), BF16),
            jax.ShapeDtypeStruct((27 * width, 2 * width), F32),
            jax.ShapeDtypeStruct((1, width), F32),
            jax.ShapeDtypeStruct((1, width), F32),
        ],
        [SMEM] + [VMEM] * 5,
        [
            pltpu.VMEM((rows, width), BF16),
            pltpu.VMEM((27 * width, 2 * width), F32),
            pltpu.SemaphoreType.DMA((4,)),
            pltpu.SemaphoreType.DMA((n_plane,)),
        ],
        [HBM, HBM, VMEM, VMEM],
        mib=20,
    )(
        counts,
        norm,
        gain_row,
        plane,
        value_rows,
        feature_part,
    )
    return (
        grad_features.reshape(features.shape),
        grad_weight.reshape(27, width, 2 * width),
        grad_gain.reshape(width),
        grad_shift.reshape(width),
    )


def solution(mesh):
    slabs = mesh.devices.shape[0]
    inner = Mesh(mesh.devices.reshape(CUT[slabs] + (2,)), SLABS + ("ch",))
    in_specs = (
        P(SLABS, None, "ch"),
        P(SLABS, None, "ch"),
        P(None, "ch", None),
        P("ch"),
        P("ch"),
        P(SLABS),
        P(SLABS, None),
    )
    out_specs = (P(SLABS, None, "ch"), P(None, "ch", None), P("ch"), P("ch"))
    return jax.shard_map(body, mesh=inner, in_specs=in_specs, out_specs=out_specs, check_vma=False)
```

```python
import functools

import jax
import jax.numpy as jnp
from jax import lax
from jax.experimental import pallas as pl
from jax.experimental.pallas import tpu as pltpu
from jax.sharding import Mesh
from jax.sharding import PartitionSpec as P

GROUP_CH = 8
PITCH = 72
BATCHES = (2, 5, 7, 8)
CUT = {128: (8, 4, 4), 8: (2, 2, 2), 4: (2, 2, 1)}
SLABS = ("z", "x", "y")
PLANE = ("x", "y")
F32 = jnp.float32
BF16 = jnp.bfloat16
VMEM = pl.BlockSpec(memory_space=pltpu.VMEM)
SMEM = pl.BlockSpec(memory_space=pltpu.SMEM)
HBM = pl.BlockSpec(memory_space=pltpu.HBM)
ANY = pl.BlockSpec(memory_space=pl.ANY)


def call(kernel, out_shape, in_specs, scratch=(), out_specs=VMEM, flops=0, mib=52, aliases=None):
    if isinstance(out_shape, (list, tuple)) and out_specs is VMEM:
        out_specs = [VMEM] * len(out_shape)
    return pl.pallas_call(
        kernel,
        out_shape=out_shape,
        in_specs=in_specs,
        out_specs=out_specs,
        scratch_shapes=list(scratch),
        input_output_aliases=aliases or {},
        compiler_params=pltpu.CompilerParams(vmem_limit_bytes=mib * 1024 * 1024),
        cost_estimate=pl.CostEstimate(flops=flops, bytes_accessed=0, transcendentals=0),
    )


def exact_dot(left, right):
    return jnp.dot(left, right, precision=lax.Precision.HIGHEST, preferred_element_type=F32)


def iota(shape, dim):
    return lax.broadcasted_iota(jnp.int32, shape, dim)


def turned(rows_ref, out_ref):
    slots = out_ref.shape[1]
    for voxel in range(64):
        out_ref[voxel] = rows_ref[pl.ds(voxel, slots, stride=PITCH), :].astype(out_ref.dtype)


def fetch(source, target, sems, pieces):
    step = source.shape[0] // pieces
    copies = [
        pltpu.make_async_copy(
            source.at[pl.ds(at * step, step)], target.at[pl.ds(at * step, step)], sems.at[at]
        )
        for at in range(pieces)
    ]
    for copy in copies:
        copy.start()
    return copies


def widen(held_ref, rows_ref, copies=()):
    slots = held_ref.shape[0] // 64
    step = slots // max(len(copies), 1)
    for slot in range(slots):
        if copies and slot % step == 0:
            copies[slot // step].wait()
        rows = held_ref[slot * 64 : slot * 64 + 64, :].astype(F32)
        rows_ref[slot * PITCH : slot * PITCH + 64, :] = rows


def prepare_kernel(
    counts_ref,
    core_ref,
    cotangent_hbm,
    values_hbm,
    own_hbm,
    give_hbm,
    keep_hbm,
    sent_ref,
    held_ref,
    rows_ref,
    own_ref,
    sems,
    out_sems,
):
    slots = own_ref.shape[1]
    turns = fetch(cotangent_hbm, held_ref.at[0], sems.at[0], 4)
    copies = fetch(values_hbm, held_ref.at[1], sems.at[1], 4)
    core = core_ref[0]
    count = counts_ref[0]
    widen(held_ref.at[0], rows_ref, turns)
    turned(rows_ref, own_ref)
    sends = [
        pltpu.make_async_copy(own_ref.at[pl.ds(48 * core, 16)], give_hbm, out_sems.at[0]),
        pltpu.make_async_copy(own_ref.at[pl.ds(48 - 48 * core, 16)], keep_hbm, out_sems.at[1]),
        pltpu.make_async_copy(own_ref, own_hbm, out_sems.at[2]),
    ]
    for send in sends:
        send.start()
    widen(held_ref.at[1], rows_ref, copies)

    def over_slots(term):
        total = jnp.zeros((8, 128), F32)
        for slot in range(slots):
            rows = term(rows_ref[slot * PITCH : slot * PITCH + 64, :]).reshape(8, 8, 128).sum(axis=0)
            total = total + jnp.where(slot < count, rows, 0.0)
        return jnp.broadcast_to(jnp.sum(total, axis=0, keepdims=True), (8, 128))

    lane_in, lane_out = iota((128, 128), 0), iota((128, 128), 1)
    same = (lane_in // GROUP_CH == lane_out // GROUP_CH).astype(F32)
    to_sum = (lane_in // GROUP_CH == lane_out).astype(F32)
    to_square = (lane_in // GROUP_CH + 16 == lane_out).astype(F32)
    total = over_slots(lambda rows: rows)
    entries = count.astype(F32) * (64.0 * GROUP_CH)
    mean = (exact_dot(total, same) / entries)[0:1]

    def centred(rows):
        apart = rows - mean
        return apart * apart

    squares = over_slots(centred)
    row = exact_dot(total, to_sum) / entries + exact_dot(squares, to_square)
    row = row + jnp.where(iota((8, 128), 1) == 32, count.astype(F32), 0.0)
    sent_ref[...] = jnp.broadcast_to(row[0:1].reshape(1, 1, 128), sent_ref.shape)
    for send in sends:
        send.wait()


def lanes_of(core):
    mine = pl.ds(pl.multiple_of(core * 128, 128), 128)
    other = pl.ds(pl.multiple_of((1 - core) * 128, 128), 128)
    return mine, other


def side(at):
    return -1 if at == 0 else (1 if at == 5 else 0)


def source(at):
    return {0: 4, 5: 1}.get(at, at)


def offset_of(dx, b, c):
    return 9 * (dx + 1) + 3 * (side(b) + 1) + side(c) + 1


def choose(near, offset, first, last):
    columns = iota((near.shape[0], last - first), 1) + first
    return (near[:, offset : offset + 1] == columns).astype(F32).astype(BF16)


def sources(places):
    readers = {}
    for b, c in places:
        readers.setdefault((source(b), source(c)), []).append((b, c))
    return readers


def gathered(picks, table):
    rows = jnp.dot(jnp.concatenate(picks, axis=0), table, preferred_element_type=F32).astype(BF16)
    slots = picks[0].shape[0]
    return [rows[at * slots : at * slots + slots] for at in range(len(picks))]


def halo_kernel(core_ref, near_ref, own_ref, own_other_ref, middle_ref, sems):
    slots = near_ref.shape[0]
    mine, other = lanes_of(core_ref[0])
    centre = middle_ref.at[:, 1:5, 1:5]
    copies = [
        pltpu.make_async_copy(own_ref, centre.at[:, :, :, :, mine], sems.at[0]),
        pltpu.make_async_copy(own_other_ref, centre.at[:, :, :, :, other], sems.at[1]),
    ]
    for copy in copies:
        copy.start()
    near = near_ref[...]
    places = [(b, c) for b in range(6) for c in range(6) if side(b) or side(c)]
    picks = {
        offset: choose(near, offset, slots, 2 * slots)
        for offset in sorted({offset_of(0, b, c) for b, c in places})
    }
    for copy in copies:
        copy.wait()
    for plane in range(4):
        for (b, c), readers in sources(places).items():
            rows = gathered([picks[offset_of(0, *at)] for at in readers], middle_ref[plane, b, c])
            for at, block in zip(readers, rows):
                middle_ref[plane, at[0], at[1]] = block


def window(plane_ref, turn):
    slots = plane_ref.shape[2]
    block = plane_ref[pl.ds(2 - turn // 3, 4), pl.ds(2 - turn % 3, 4)]
    return block.reshape(16 * slots, 256)


def planes_of(plane):
    return max(0, plane - 2), min(3, plane) + 1


def weight_grad_kernel(
    counts_ref,
    core_ref,
    near_ref,
    table_ref,
    gain_ref,
    shift_ref,
    received_ref,
    theirs_ref,
    values_ref,
    middle_ref,
    out_hbm,
    grid_hbm,
    norm_ref,
    rows_ref,
    sides_ref,
    face_ref,
    act_ref,
    total_ref,
    out_ref,
    face_sems,
    plane_sems,
    out_sems,
):
    slots = middle_ref.shape[3]
    core = core_ref[0]
    mine, other = lanes_of(core)
    near_face, far_face = face_ref.at[core], face_ref.at[1 - core]
    faces = [
        pltpu.make_async_copy(received_ref.at[0], near_face.at[:, :, :, mine], face_sems.at[0]),
        pltpu.make_async_copy(received_ref.at[1], near_face.at[:, :, :, other], face_sems.at[1]),
        pltpu.make_async_copy(theirs_ref.at[0], far_face.at[:, :, :, other], face_sems.at[2]),
        pltpu.make_async_copy(theirs_ref.at[1], far_face.at[:, :, :, mine], face_sems.at[3]),
    ]
    for copy in faces:
        copy.start()
    table = table_ref[...]
    held = jnp.sum(table, axis=0)
    voxels = held[:, 32:33] * (64.0 * GROUP_CH)
    entries = table[:, :, 32:33] * (64.0 * GROUP_CH)
    mean = jnp.sum(table * entries, axis=0) / voxels
    apart = table - mean.reshape(1, 1, 128)
    between = jnp.sum(apart * apart * entries, axis=0)
    lane_in, lane_out = iota((128, 128), 0), iota((128, 128), 1)
    from_sum = (lane_in == lane_out // GROUP_CH).astype(F32)
    from_square = (lane_in == lane_out // GROUP_CH + 16).astype(F32)

    stacked = jnp.concatenate([mean, between, held, jnp.zeros((5, 128), F32)], axis=0)
    spread = exact_dot(stacked, jnp.concatenate([from_sum, from_square], axis=1))
    mean = spread[0:1, 0:128]
    variance = (spread[1:2, 0:128] + spread[2:3, 128:256]) / voxels
    rstd = lax.rsqrt(variance + 1e-05)
    norm_ref[0:1, :] = mean
    norm_ref[1:2, :] = rstd
    norm_ref[2:3, :] = jnp.broadcast_to(voxels, (1, 128))
    norm_ref[3:8, :] = jnp.zeros((5, 128), F32)
    gain, shift = gain_ref[...], shift_ref[...]
    live = iota((slots, 128), 0) < counts_ref[0]
    widen(values_ref, rows_ref)
    for plane in range(4):
        pieces = []
        for voxel in range(plane * 16, plane * 16 + 16):
            normed = (rows_ref[pl.ds(voxel, slots, stride=PITCH), :] - mean) * rstd
            pre = normed * gain + shift
            pieces.append(jnp.where(live, pre / (1.0 + jnp.exp(-pre)), 0.0))
        rows = jnp.concatenate(pieces, axis=0)
        act_ref[plane * 128 : plane * 128 + 128, :] = rows.T.astype(BF16)
    for copy in faces:
        copy.wait()
    near = near_ref[...]
    places = [(b, c) for b in range(6) for c in range(6)]
    sends = []
    for which, dx in enumerate((-1, 1)):
        lowest = which * slots
        picks = {
            offset: choose(near, offset, lowest, lowest + 2 * slots)
            for offset in sorted({offset_of(dx, b, c) for b, c in places})
        }
        for (b, c), readers in sources(places).items():
            outer = face_ref[which, b - 1, c - 1]
            inner = middle_ref[3 - 3 * which, b, c]
            table = jnp.concatenate([outer, inner] if which == 0 else [inner, outer], axis=0)
            rows = gathered([picks[offset_of(dx, *at)] for at in readers], table)
            for at, block in zip(readers, rows):
                sides_ref[which, at[0], at[1]] = block
    planes = [sides_ref.at[0]] + [middle_ref.at[at] for at in range(4)] + [sides_ref.at[1]]
    for at, plane in enumerate(planes):
        sends.append(pltpu.make_async_copy(plane, grid_hbm.at[at], plane_sems.at[at]))
        sends[-1].start()
    for turn in range(9):
        seen = set()
        for plane in range(6):
            first, last = planes_of(plane)
            part = jnp.dot(
                act_ref[first * 128 : last * 128, :],
                window(planes[plane], turn),
                preferred_element_type=F32,
            )
            for at in range(first, last):
                step = at - plane + 2
                term = part[(at - first) * 128 : (at - first) * 128 + 128]
                if step in seen:
                    total_ref[step] += term
                else:
                    total_ref[step] = term
                    seen.add(step)
        for step in range(3):
            out_ref[step, turn] = total_ref[step].astype(BF16)
        if turn in BATCHES:
            batch = BATCHES.index(turn)
            first = BATCHES[batch - 1] + 1 if batch else 0
            part = pl.ds(first, turn + 1 - first)
            for step in range(3):
                sends.append(
                    pltpu.make_async_copy(
                        out_ref.at[step, part], out_hbm.at[step, part], out_sems.at[step, batch]
                    )
                )
                sends[-1].start()
    for send in sends:
        send.wait()


def act_grad_kernel(
    counts_ref,
    norm_ref,
    gain_ref,
    shift_ref,
    values_ref,
    cotangent_ref,
    weight_ref,
    grid_ref,
    out_ref,
    sums_ref,
    total_ref,
    rows_ref,
    cotangent_rows_ref,
):
    slots = grid_ref.shape[3]
    total_ref[...] = jnp.zeros_like(total_ref)
    widen(values_ref, rows_ref)
    widen(cotangent_ref, cotangent_rows_ref)

    @pl.loop(0, 9)
    def _(turn):
        for plane in range(6):
            first, last = planes_of(plane)
            low, high = first - plane + 2, last - plane + 2
            part = lax.dot_general(
                window(grid_ref.at[plane], turn),
                weight_ref[low:high, turn].reshape((high - low) * 128, 256),
                (((1,), (1,)), ((), ())),
                preferred_element_type=F32,
            )
            for at in range(first, last):
                term = part[:, (at - first) * 128 : (at - first) * 128 + 128]
                total_ref[at] += term.reshape(16, slots, 128)

    mean, rstd = norm_ref[0:1, :], norm_ref[1:2, :]
    gain, shift = gain_ref[...], shift_ref[...]
    live = iota((slots, 128), 0) < counts_ref[0]
    scale = rstd * gain
    shift_sum = jnp.zeros((8, 128), F32)
    gain_sum = jnp.zeros((8, 128), F32)
    for voxel in range(64):
        normed = (rows_ref[pl.ds(voxel, slots, stride=PITCH), :] - mean) * rstd
        pre = normed * gain + shift
        sig = 1.0 / (1.0 + jnp.exp(-pre))
        grad = total_ref[voxel // 16, voxel % 16] * sig * (1.0 + pre * (1.0 - sig))
        grad = jnp.where(live, grad, 0.0)
        places = pl.ds(voxel, slots, stride=PITCH)
        out_ref[places, :] = cotangent_rows_ref[places, :] + scale * grad
        shift_sum = shift_sum + grad.reshape(slots // 8, 8, 128).sum(axis=0)
        gain_sum = gain_sum + (grad * normed).reshape(slots // 8, 8, 128).sum(axis=0)
    sums_ref[:, 0:128] = jnp.sum(shift_sum, axis=0, keepdims=True)
    sums_ref[:, 128:256] = jnp.sum(gain_sum, axis=0, keepdims=True)


def last_kernel(
    counts_ref,
    norm_ref,
    gain_ref,
    plane_ref,
    values_ref,
    part_ref,
    out_hbm,
    weight_hbm,
    gain_out,
    shift_out,
    out_ref,
    weight_ref,
    out_sems,
    weight_sems,
):
    slots = values_ref.shape[0] // 64
    pieces = plane_ref.shape[0]
    piece = weight_ref.shape[0] // pieces
    copies = []
    totals = jnp.zeros((1, 256), F32)
    for at in range(pieces):
        block = plane_ref[at].astype(F32)
        rows = pl.ds(at * piece, piece)
        weight_ref[rows] = block[0:piece]
        totals = totals + (block[piece : piece + 1] + block[piece + 1 : piece + 2])
        totals = totals + block[piece + 2 : piece + 3]
        copies.append(
            pltpu.make_async_copy(weight_ref.at[rows], weight_hbm.at[rows], weight_sems.at[at])
        )
        copies[-1].start()
    shift_sum, gain_sum = totals[:, 0:128], totals[:, 128:256]
    gain_out[...] = gain_sum
    shift_out[...] = shift_sum
    mean, rstd, voxels = norm_ref[0:1, :], norm_ref[1:2, :], norm_ref[2:3, :]
    gain = gain_ref[...]
    lane_in, lane_out = iota((128, 128), 0), iota((128, 128), 1)
    same = (lane_in // GROUP_CH == lane_out // GROUP_CH).astype(F32)

    stacked = jnp.concatenate(
        [gain * shift_sum, gain * gain_sum, jnp.zeros((6, 128), F32)], axis=0
    )
    grouped = exact_dot(stacked, same) / voxels
    constant, slope = rstd * grouped[0:1], rstd * rstd * grouped[1:2]
    chunk = slots // 4
    for slot in range(slots):
        rows = slice(slot * 64, slot * 64 + 64)
        centred = values_ref[rows, :].astype(F32) - mean
        result = part_ref[slot * PITCH : slot * PITCH + 64, :] - constant - centred * slope
        out_ref[rows, :] = jnp.where(slot < counts_ref[0], result, 0.0).astype(BF16)
        if slot % chunk == chunk - 1:
            at = slot // chunk
            rows = pl.ds(at * chunk * 64, chunk * 64)
            copies.append(
                pltpu.make_async_copy(out_ref.at[rows], out_hbm.at[rows], out_sems.at[at])
            )
            copies[-1].start()
    for copy in copies:
        copy.wait()


def body(features, cotangent, weight, gain, shift, counts, neighbours):
    slots, voxels, width = features.shape
    rows = slots * voxels
    n_plane = lax.axis_size("x") * lax.axis_size("y")
    n_line = lax.axis_size("z")
    n_slab = n_plane * n_line
    core = lax.axis_index("ch").astype(jnp.int32).reshape(1)
    turned_shape = jax.ShapeDtypeStruct((voxels, slots, width), BF16)
    face_shape = jax.ShapeDtypeStruct((16, slots, width), BF16)
    gain_row, shift_row = gain.reshape(1, width), shift.reshape(1, width)
    value_rows = features.reshape(rows, width)
    cotangent_rows = cotangent.reshape(rows, width)
    work = 2 * rows * 27 * width * 2 * width

    own, give, keep, sent = call(
        prepare_kernel,
        [
            turned_shape,
            face_shape,
            face_shape,
            jax.ShapeDtypeStruct((n_slab, 1, 128), F32),
        ],
        [SMEM, SMEM, HBM, HBM],
        [
            pltpu.VMEM((2, rows, width), BF16),
            pltpu.VMEM((slots * PITCH, width), F32),
            pltpu.VMEM(turned_shape.shape, BF16),
            pltpu.SemaphoreType.DMA((2, 4)),
            pltpu.SemaphoreType.DMA((3,)),
        ],
        [HBM, HBM, HBM, VMEM],
        mib=36,
    )(
        counts,
        core,
        pltpu.with_memory_space_constraint(cotangent_rows, pltpu.HBM),
        pltpu.with_memory_space_constraint(value_rows, pltpu.HBM),
    )
    table = lax.all_to_all(sent, SLABS, 0, 0, tiled=True)
    cores = [(0, 1), (1, 0)]
    ups = [(i, i + 1) for i in range(n_slab - 1)]
    outward = [(2 * i, 2 * j) for i, j in ups] + [(2 * j + 1, 2 * i + 1) for i, j in ups]
    sent_planes = jnp.stack([keep, lax.ppermute(give, "ch", cores)])
    own_other = lax.ppermute(own, "ch", cores)
    received = lax.ppermute(sent_planes, SLABS + ("ch",), outward)

    cube = (4, 4, 4, slots, width)
    face = (4, 4, slots, width)
    middle_shape = (4, 6, 6, slots, 2 * width)
    middle = call(
        halo_kernel,
        jax.ShapeDtypeStruct(middle_shape, BF16),
        [SMEM, VMEM, ANY, ANY],
        [pltpu.SemaphoreType.DMA((2,))],
        flops=10**9,
        mib=24,
    )(
        core,
        neighbours,
        own.reshape(cube),
        own_other.reshape(cube),
    )

    table, received = lax.optimization_barrier((table, received))
    theirs = lax.ppermute(received, "ch", cores)
    grid_shape = pltpu.HBM((6, 6, 6, slots, 2 * width), BF16)

    term_shape = jax.ShapeDtypeStruct((3, 9, width, 2 * width), BF16)
    weight_term, grid, norm = call(
        weight_grad_kernel,
        [term_shape, grid_shape, pltpu.HBM((8, 128), F32)],
        [SMEM, SMEM, VMEM, VMEM, VMEM, VMEM, ANY, ANY, VMEM, VMEM],
        [
            pltpu.VMEM((slots * PITCH, width), F32),
            pltpu.VMEM((2, 6, 6, slots, 2 * width), BF16),
            pltpu.VMEM((2, 4, 4, slots, 2 * width), BF16),
            pltpu.VMEM((4 * width, 16 * slots), BF16),
            pltpu.VMEM((3, width, 2 * width), F32),
            pltpu.VMEM(term_shape.shape, BF16),
            pltpu.SemaphoreType.DMA((4,)),
            pltpu.SemaphoreType.DMA((6,)),
            pltpu.SemaphoreType.DMA((3, len(BATCHES))),
        ],
        [HBM, HBM, VMEM],
        flops=work,
        mib=24,
    )(
        counts,
        core,
        neighbours,
        table,
        gain_row,
        shift_row,
        received.reshape((2,) + face),
        theirs.reshape((2,) + face),
        value_rows,
        middle,
    )
    piece = 27 * width // n_plane
    parts = lax.all_to_all(
        weight_term.reshape(n_plane, piece, 2 * width), PLANE, 0, 0, tiled=True
    )

    feature_part, sums = call(
        act_grad_kernel,
        [
            jax.ShapeDtypeStruct((slots * PITCH, width), F32),
            jax.ShapeDtypeStruct((1, 2 * width), F32),
        ],
        [SMEM] + [VMEM] * 7,
        [pltpu.VMEM((4, 16, slots, width), F32)] + [pltpu.VMEM((slots * PITCH, width), F32)] * 2,
        flops=work,
        mib=58,
    )(
        counts,
        norm,
        gain_row,
        shift_row,
        value_rows,
        cotangent_rows,
        weight.reshape(3, 9, width, 2 * width),
        grid,
    )

    part = jnp.sum(parts.astype(F32), axis=0).reshape(n_line, piece // n_line, 2 * width)
    part = jnp.concatenate(
        [part, jnp.broadcast_to(sums.reshape(1, 1, 2 * width), (n_line, 1, 2 * width))], axis=1
    )
    part = jnp.sum(lax.all_to_all(part, "z", 0, 0, tiled=True), axis=0)
    final = part[:-1].astype(BF16)
    line = jnp.broadcast_to(final[None], (n_line,) + final.shape)
    line = lax.all_to_all(line, "z", 0, 0, tiled=True).reshape(piece, 2 * width)
    line, part = lax.optimization_barrier((line, part))
    rest = part[-1:]
    split = []
    for _ in range(3):
        top = lax.reduce_precision(rest, 8, 7)
        split.append(top.astype(BF16))
        rest = rest - top
    line = jnp.concatenate([line] + split + [jnp.zeros((5, 2 * width), BF16)], axis=0)
    plane = jnp.broadcast_to(line[None], (n_plane,) + line.shape)
    plane = lax.all_to_all(plane, PLANE, 0, 0, tiled=True)
    grad_features, grad_weight, grad_gain, grad_shift = call(
        last_kernel,
        [
            jax.ShapeDtypeStruct((rows, width), BF16),
            jax.ShapeDtypeStruct((27 * width, 2 * width), F32),
            jax.ShapeDtypeStruct((1, width), F32),
            jax.ShapeDtypeStruct((1, width), F32),
        ],
        [SMEM] + [VMEM] * 5,
        [
            pltpu.VMEM((rows, width), BF16),
            pltpu.VMEM((27 * width, 2 * width), F32),
            pltpu.SemaphoreType.DMA((4,)),
            pltpu.SemaphoreType.DMA((n_plane,)),
        ],
        [HBM, HBM, VMEM, VMEM],
        mib=20,
    )(
        counts,
        norm,
        gain_row,
        plane,
        value_rows,
        feature_part,
    )
    return (
        grad_features.reshape(features.shape),
        grad_weight.reshape(27, width, 2 * width),
        grad_gain.reshape(width),
        grad_shift.reshape(width),
    )


def solution(mesh):
    slabs = mesh.devices.shape[0]
    inner = Mesh(mesh.devices.reshape(CUT[slabs] + (2,)), SLABS + ("ch",))
    in_specs = (
        P(SLABS, None, "ch"),
        P(SLABS, None, "ch"),
        P(None, "ch", None),
        P("ch"),
        P("ch"),
        P(SLABS),
        P(SLABS, None),
    )
    out_specs = (P(SLABS, None, "ch"), P(None, "ch", None), P("ch"), P("ch"))
    return jax.shard_map(body, mesh=inner, in_specs=in_specs, out_specs=out_specs, check_vma=False)
```

```python
import functools

import jax
import jax.numpy as jnp
from jax import lax
from jax.experimental import pallas as pl
from jax.experimental.pallas import tpu as pltpu
from jax.sharding import Mesh
from jax.sharding import PartitionSpec as P

GROUP_CH = 8
PITCH = 72
BATCHES = (5, 8)
CUT = {128: (8, 4, 4), 8: (2, 2, 2), 4: (2, 2, 1)}
SLABS = ("z", "x", "y")
PLANE = ("x", "y")
F32 = jnp.float32
BF16 = jnp.bfloat16
VMEM = pl.BlockSpec(memory_space=pltpu.VMEM)
SMEM = pl.BlockSpec(memory_space=pltpu.SMEM)
HBM = pl.BlockSpec(memory_space=pltpu.HBM)
ANY = pl.BlockSpec(memory_space=pl.ANY)


def call(kernel, out_shape, in_specs, scratch=(), out_specs=VMEM, flops=0, mib=52, aliases=None):
    if isinstance(out_shape, (list, tuple)) and out_specs is VMEM:
        out_specs = [VMEM] * len(out_shape)
    return pl.pallas_call(
        kernel,
        out_shape=out_shape,
        in_specs=in_specs,
        out_specs=out_specs,
        scratch_shapes=list(scratch),
        input_output_aliases=aliases or {},
        compiler_params=pltpu.CompilerParams(vmem_limit_bytes=mib * 1024 * 1024),
        cost_estimate=pl.CostEstimate(flops=flops, bytes_accessed=0, transcendentals=0),
    )


def exact_dot(left, right):
    return jnp.dot(left, right, precision=lax.Precision.HIGHEST, preferred_element_type=F32)


def iota(shape, dim):
    return lax.broadcasted_iota(jnp.int32, shape, dim)


def turned(rows_ref, out_ref):
    slots = out_ref.shape[1]
    for voxel in range(64):
        out_ref[voxel] = rows_ref[pl.ds(voxel, slots, stride=PITCH), :].astype(out_ref.dtype)


def fetch(source, target, sems, pieces):
    step = source.shape[0] // pieces
    copies = [
        pltpu.make_async_copy(
            source.at[pl.ds(at * step, step)], target.at[pl.ds(at * step, step)], sems.at[at]
        )
        for at in range(pieces)
    ]
    for copy in copies:
        copy.start()
    return copies


def widen(held_ref, rows_ref, copies=()):
    slots = held_ref.shape[0] // 64
    step = slots // max(len(copies), 1)
    for slot in range(slots):
        if copies and slot % step == 0:
            copies[slot // step].wait()
        rows = held_ref[slot * 64 : slot * 64 + 64, :].astype(F32)
        rows_ref[slot * PITCH : slot * PITCH + 64, :] = rows


def prepare_kernel(
    counts_ref,
    core_ref,
    cotangent_hbm,
    values_hbm,
    own_hbm,
    give_hbm,
    keep_hbm,
    sent_ref,
    held_ref,
    rows_ref,
    own_ref,
    sems,
    out_sems,
):
    slots = own_ref.shape[1]
    turns = fetch(cotangent_hbm, held_ref.at[0], sems.at[0], 4)
    copies = fetch(values_hbm, held_ref.at[1], sems.at[1], 4)
    core = core_ref[0]
    count = counts_ref[0]
    widen(held_ref.at[0], rows_ref, turns)
    turned(rows_ref, own_ref)
    sends = [
        pltpu.make_async_copy(own_ref.at[pl.ds(48 * core, 16)], give_hbm, out_sems.at[0]),
        pltpu.make_async_copy(own_ref.at[pl.ds(48 - 48 * core, 16)], keep_hbm, out_sems.at[1]),
        pltpu.make_async_copy(own_ref, own_hbm, out_sems.at[2]),
    ]
    for send in sends:
        send.start()
    widen(held_ref.at[1], rows_ref, copies)

    def over_slots(term):
        total = jnp.zeros((8, 128), F32)
        for slot in range(slots):
            rows = term(rows_ref[slot * PITCH : slot * PITCH + 64, :]).reshape(8, 8, 128).sum(axis=0)
            total = total + jnp.where(slot < count, rows, 0.0)
        return jnp.broadcast_to(jnp.sum(total, axis=0, keepdims=True), (8, 128))

    lane_in, lane_out = iota((128, 128), 0), iota((128, 128), 1)
    same = (lane_in // GROUP_CH == lane_out // GROUP_CH).astype(F32)
    to_sum = (lane_in // GROUP_CH == lane_out).astype(F32)
    to_square = (lane_in // GROUP_CH + 16 == lane_out).astype(F32)
    total = over_slots(lambda rows: rows)
    entries = count.astype(F32) * (64.0 * GROUP_CH)
    mean = (exact_dot(total, same) / entries)[0:1]

    def centred(rows):
        apart = rows - mean
        return apart * apart

    squares = over_slots(centred)
    row = exact_dot(total, to_sum) + exact_dot(squares, to_square)
    row = row + jnp.where(iota((8, 128), 1) == 32, count.astype(F32), 0.0)
    sent_ref[...] = jnp.broadcast_to(row[0:1].reshape(1, 1, 128), sent_ref.shape)
    for send in sends:
        send.wait()


def lanes_of(core):
    mine = pl.ds(pl.multiple_of(core * 128, 128), 128)
    other = pl.ds(pl.multiple_of((1 - core) * 128, 128), 128)
    return mine, other


def side(at):
    return -1 if at == 0 else (1 if at == 5 else 0)


def source(at):
    return {0: 4, 5: 1}.get(at, at)


def offset_of(dx, b, c):
    return 9 * (dx + 1) + 3 * (side(b) + 1) + side(c) + 1


def choose(near, offset, first, last):
    columns = iota((near.shape[0], last - first), 1) + first
    return (near[:, offset : offset + 1] == columns).astype(F32).astype(BF16)


def sources(places):
    readers = {}
    for b, c in places:
        readers.setdefault((source(b), source(c)), []).append((b, c))
    return readers


def gathered(picks, table):
    rows = jnp.dot(jnp.concatenate(picks, axis=0), table, preferred_element_type=F32).astype(BF16)
    slots = picks[0].shape[0]
    return [rows[at * slots : at * slots + slots] for at in range(len(picks))]


def halo_kernel(core_ref, near_ref, own_ref, own_other_ref, middle_ref, sems):
    slots = near_ref.shape[0]
    mine, other = lanes_of(core_ref[0])
    centre = middle_ref.at[:, 1:5, 1:5]
    copies = [
        pltpu.make_async_copy(own_ref, centre.at[:, :, :, :, mine], sems.at[0]),
        pltpu.make_async_copy(own_other_ref, centre.at[:, :, :, :, other], sems.at[1]),
    ]
    for copy in copies:
        copy.start()
    near = near_ref[...]
    places = [(b, c) for b in range(6) for c in range(6) if side(b) or side(c)]
    picks = {
        offset: choose(near, offset, slots, 2 * slots)
        for offset in sorted({offset_of(0, b, c) for b, c in places})
    }
    for copy in copies:
        copy.wait()
    for plane in range(4):
        for (b, c), readers in sources(places).items():
            rows = gathered([picks[offset_of(0, *at)] for at in readers], middle_ref[plane, b, c])
            for at, block in zip(readers, rows):
                middle_ref[plane, at[0], at[1]] = block


def window(plane_ref, turn):
    slots = plane_ref.shape[2]
    block = plane_ref[pl.ds(2 - turn // 3, 4), pl.ds(2 - turn % 3, 4)]
    return block.reshape(16 * slots, 256)


def planes_of(plane):
    return max(0, plane - 2), min(3, plane) + 1


def weight_grad_kernel(
    counts_ref,
    core_ref,
    near_ref,
    table_ref,
    gain_ref,
    shift_ref,
    received_ref,
    theirs_ref,
    values_ref,
    middle_ref,
    out_hbm,
    grid_hbm,
    norm_ref,
    rows_ref,
    sides_ref,
    face_ref,
    act_ref,
    total_ref,
    out_ref,
    face_sems,
    plane_sems,
    out_sems,
):
    slots = middle_ref.shape[3]
    core = core_ref[0]
    mine, other = lanes_of(core)
    near_face, far_face = face_ref.at[core], face_ref.at[1 - core]
    faces = [
        pltpu.make_async_copy(received_ref.at[0], near_face.at[:, :, :, mine], face_sems.at[0]),
        pltpu.make_async_copy(received_ref.at[1], near_face.at[:, :, :, other], face_sems.at[1]),
        pltpu.make_async_copy(theirs_ref.at[0], far_face.at[:, :, :, other], face_sems.at[2]),
        pltpu.make_async_copy(theirs_ref.at[1], far_face.at[:, :, :, mine], face_sems.at[3]),
    ]
    for copy in faces:
        copy.start()
    table = table_ref[...]
    held = jnp.sum(table, axis=0)
    voxels = held[:, 32:33] * (64.0 * GROUP_CH)
    entries = table[:, :, 32:33] * (64.0 * GROUP_CH)
    mean = held / voxels
    apart = table / entries - mean.reshape(1, 1, 128)
    between = jnp.sum(apart * apart * entries, axis=0)
    lane_in, lane_out = iota((128, 128), 0), iota((128, 128), 1)
    from_sum = (lane_in == lane_out // GROUP_CH).astype(F32)
    from_square = (lane_in == lane_out // GROUP_CH + 16).astype(F32)

    stacked = jnp.concatenate([mean, between, held, jnp.zeros((5, 128), F32)], axis=0)
    spread = exact_dot(stacked, jnp.concatenate([from_sum, from_square], axis=1))
    mean = spread[0:1, 0:128]
    variance = (spread[1:2, 0:128] + spread[2:3, 128:256]) / voxels
    rstd = lax.rsqrt(variance + 1e-05)
    norm_ref[0:1, :] = mean
    norm_ref[1:2, :] = rstd
    norm_ref[2:3, :] = jnp.broadcast_to(voxels, (1, 128))
    norm_ref[3:8, :] = jnp.zeros((5, 128), F32)
    gain, shift = gain_ref[...], shift_ref[...]
    live = iota((slots, 128), 0) < counts_ref[0]
    widen(values_ref, rows_ref)
    for plane in range(4):
        pieces = []
        for voxel in range(plane * 16, plane * 16 + 16):
            normed = (rows_ref[pl.ds(voxel, slots, stride=PITCH), :] - mean) * rstd
            pre = normed * gain + shift
            pieces.append(jnp.where(live, pre / (1.0 + jnp.exp(-pre)), 0.0))
        rows = jnp.concatenate(pieces, axis=0)
        act_ref[plane * 128 : plane * 128 + 128, :] = rows.T.astype(BF16)
    for copy in faces:
        copy.wait()
    near = near_ref[...]
    places = [(b, c) for b in range(6) for c in range(6)]
    sends = []
    for which, dx in enumerate((-1, 1)):
        lowest = which * slots
        picks = {
            offset: choose(near, offset, lowest, lowest + 2 * slots)
            for offset in sorted({offset_of(dx, b, c) for b, c in places})
        }
        for (b, c), readers in sources(places).items():
            outer = face_ref[which, b - 1, c - 1]
            inner = middle_ref[3 - 3 * which, b, c]
            table = jnp.concatenate([outer, inner] if which == 0 else [inner, outer], axis=0)
            rows = gathered([picks[offset_of(dx, *at)] for at in readers], table)
            for at, block in zip(readers, rows):
                sides_ref[which, at[0], at[1]] = block
    planes = [sides_ref.at[0]] + [middle_ref.at[at] for at in range(4)] + [sides_ref.at[1]]
    for at, plane in enumerate(planes):
        sends.append(pltpu.make_async_copy(plane, grid_hbm.at[at], plane_sems.at[at]))
        sends[-1].start()
    for turn in range(9):
        seen = set()
        for plane in range(6):
            first, last = planes_of(plane)
            part = jnp.dot(
                act_ref[first * 128 : last * 128, :],
                window(planes[plane], turn),
                preferred_element_type=F32,
            )
            for at in range(first, last):
                step = at - plane + 2
                term = part[(at - first) * 128 : (at - first) * 128 + 128]
                if step in seen:
                    total_ref[step] += term
                else:
                    total_ref[step] = term
                    seen.add(step)
        for step in range(3):
            out_ref[step, turn] = total_ref[step].astype(BF16)
        if turn in BATCHES:
            batch = BATCHES.index(turn)
            first = BATCHES[batch - 1] + 1 if batch else 0
            part = pl.ds(first, turn + 1 - first)
            for step in range(3):
                sends.append(
                    pltpu.make_async_copy(
                        out_ref.at[step, part], out_hbm.at[step, part], out_sems.at[step, batch]
                    )
                )
                sends[-1].start()
    for send in sends:
        send.wait()


def act_grad_kernel(
    counts_ref,
    norm_ref,
    gain_ref,
    shift_ref,
    values_ref,
    cotangent_ref,
    weight_ref,
    grid_ref,
    out_ref,
    sums_ref,
    total_ref,
    rows_ref,
    cotangent_rows_ref,
):
    slots = grid_ref.shape[3]
    total_ref[...] = jnp.zeros_like(total_ref)
    widen(values_ref, rows_ref)
    widen(cotangent_ref, cotangent_rows_ref)

    @pl.loop(0, 9)
    def _(turn):
        for plane in range(6):
            first, last = planes_of(plane)
            low, high = first - plane + 2, last - plane + 2
            part = lax.dot_general(
                window(grid_ref.at[plane], turn),
                weight_ref[low:high, turn].reshape((high - low) * 128, 256),
                (((1,), (1,)), ((), ())),
                preferred_element_type=F32,
            )
            for at in range(first, last):
                term = part[:, (at - first) * 128 : (at - first) * 128 + 128]
                total_ref[at] += term.reshape(16, slots, 128)

    mean, rstd = norm_ref[0:1, :], norm_ref[1:2, :]
    gain, shift = gain_ref[...], shift_ref[...]
    live = iota((slots, 128), 0) < counts_ref[0]
    scale = rstd * gain
    shift_sum = jnp.zeros((8, 128), F32)
    gain_sum = jnp.zeros((8, 128), F32)
    for voxel in range(64):
        normed = (rows_ref[pl.ds(voxel, slots, stride=PITCH), :] - mean) * rstd
        pre = normed * gain + shift
        sig = 1.0 / (1.0 + jnp.exp(-pre))
        grad = total_ref[voxel // 16, voxel % 16] * sig * (1.0 + pre * (1.0 - sig))
        grad = jnp.where(live, grad, 0.0)
        places = pl.ds(voxel, slots, stride=PITCH)
        out_ref[places, :] = cotangent_rows_ref[places, :] + scale * grad
        shift_sum = shift_sum + grad.reshape(slots // 8, 8, 128).sum(axis=0)
        gain_sum = gain_sum + (grad * normed).reshape(slots // 8, 8, 128).sum(axis=0)
    sums_ref[:, 0:128] = jnp.sum(shift_sum, axis=0, keepdims=True)
    sums_ref[:, 128:256] = jnp.sum(gain_sum, axis=0, keepdims=True)


def last_kernel(
    counts_ref,
    norm_ref,
    gain_ref,
    plane_ref,
    values_ref,
    part_ref,
    out_hbm,
    weight_hbm,
    gain_out,
    shift_out,
    out_ref,
    weight_ref,
    out_sems,
    weight_sems,
):
    slots = values_ref.shape[0] // 64
    pieces = plane_ref.shape[0]
    piece = weight_ref.shape[0] // pieces
    copies = []
    totals = jnp.zeros((1, 256), F32)
    for at in range(pieces):
        block = plane_ref[at].astype(F32)
        rows = pl.ds(at * piece, piece)
        weight_ref[rows] = block[0:piece]
        totals = totals + (block[piece : piece + 1] + block[piece + 1 : piece + 2])
        totals = totals + block[piece + 2 : piece + 3]
        copies.append(
            pltpu.make_async_copy(weight_ref.at[rows], weight_hbm.at[rows], weight_sems.at[at])
        )
        copies[-1].start()
    shift_sum, gain_sum = totals[:, 0:128], totals[:, 128:256]
    gain_out[...] = gain_sum
    shift_out[...] = shift_sum
    mean, rstd, voxels = norm_ref[0:1, :], norm_ref[1:2, :], norm_ref[2:3, :]
    gain = gain_ref[...]
    lane_in, lane_out = iota((128, 128), 0), iota((128, 128), 1)
    same = (lane_in // GROUP_CH == lane_out // GROUP_CH).astype(F32)

    stacked = jnp.concatenate(
        [gain * shift_sum, gain * gain_sum, jnp.zeros((6, 128), F32)], axis=0
    )
    grouped = exact_dot(stacked, same) / voxels
    constant, slope = rstd * grouped[0:1], rstd * rstd * grouped[1:2]
    chunk = slots // 4
    for slot in range(slots):
        rows = slice(slot * 64, slot * 64 + 64)
        centred = values_ref[rows, :].astype(F32) - mean
        result = part_ref[slot * PITCH : slot * PITCH + 64, :] - constant - centred * slope
        out_ref[rows, :] = jnp.where(slot < counts_ref[0], result, 0.0).astype(BF16)
        if slot % chunk == chunk - 1:
            at = slot // chunk
            rows = pl.ds(at * chunk * 64, chunk * 64)
            copies.append(
                pltpu.make_async_copy(out_ref.at[rows], out_hbm.at[rows], out_sems.at[at])
            )
            copies[-1].start()
    for copy in copies:
        copy.wait()


def body(features, cotangent, weight, gain, shift, counts, neighbours):
    slots, voxels, width = features.shape
    rows = slots * voxels
    n_plane = lax.axis_size("x") * lax.axis_size("y")
    n_line = lax.axis_size("z")
    n_slab = n_plane * n_line
    core = lax.axis_index("ch").astype(jnp.int32).reshape(1)
    turned_shape = jax.ShapeDtypeStruct((voxels, slots, width), BF16)
    face_shape = jax.ShapeDtypeStruct((16, slots, width), BF16)
    gain_row, shift_row = gain.reshape(1, width), shift.reshape(1, width)
    value_rows = features.reshape(rows, width)
    cotangent_rows = cotangent.reshape(rows, width)
    work = 2 * rows * 27 * width * 2 * width

    own, give, keep, sent = call(
        prepare_kernel,
        [
            turned_shape,
            face_shape,
            face_shape,
            jax.ShapeDtypeStruct((n_slab, 1, 128), F32),
        ],
        [SMEM, SMEM, HBM, HBM],
        [
            pltpu.VMEM((2, rows, width), BF16),
            pltpu.VMEM((slots * PITCH, width), F32),
            pltpu.VMEM(turned_shape.shape, BF16),
            pltpu.SemaphoreType.DMA((2, 4)),
            pltpu.SemaphoreType.DMA((3,)),
        ],
        [HBM, HBM, HBM, VMEM],
        mib=36,
    )(
        counts,
        core,
        pltpu.with_memory_space_constraint(cotangent_rows, pltpu.HBM),
        pltpu.with_memory_space_constraint(value_rows, pltpu.HBM),
    )
    table = lax.all_to_all(sent, SLABS, 0, 0, tiled=True)
    cores = [(0, 1), (1, 0)]
    ups = [(i, i + 1) for i in range(n_slab - 1)]
    outward = [(2 * i, 2 * j) for i, j in ups] + [(2 * j + 1, 2 * i + 1) for i, j in ups]
    sent_planes = jnp.stack([keep, lax.ppermute(give, "ch", cores)])
    own_other = lax.ppermute(own, "ch", cores)
    received = lax.ppermute(sent_planes, SLABS + ("ch",), outward)

    cube = (4, 4, 4, slots, width)
    face = (4, 4, slots, width)
    middle_shape = (4, 6, 6, slots, 2 * width)
    middle = call(
        halo_kernel,
        jax.ShapeDtypeStruct(middle_shape, BF16),
        [SMEM, VMEM, ANY, ANY],
        [pltpu.SemaphoreType.DMA((2,))],
        flops=10**9,
        mib=24,
    )(
        core,
        neighbours,
        own.reshape(cube),
        own_other.reshape(cube),
    )

    table, received = lax.optimization_barrier((table, received))
    theirs = lax.ppermute(received, "ch", cores)
    grid_shape = pltpu.HBM((6, 6, 6, slots, 2 * width), BF16)

    term_shape = jax.ShapeDtypeStruct((3, 9, width, 2 * width), BF16)
    weight_term, grid, norm = call(
        weight_grad_kernel,
        [term_shape, grid_shape, pltpu.HBM((8, 128), F32)],
        [SMEM, SMEM, VMEM, VMEM, VMEM, VMEM, ANY, ANY, VMEM, VMEM],
        [
            pltpu.VMEM((slots * PITCH, width), F32),
            pltpu.VMEM((2, 6, 6, slots, 2 * width), BF16),
            pltpu.VMEM((2, 4, 4, slots, 2 * width), BF16),
            pltpu.VMEM((4 * width, 16 * slots), BF16),
            pltpu.VMEM((3, width, 2 * width), F32),
            pltpu.VMEM(term_shape.shape, BF16),
            pltpu.SemaphoreType.DMA((4,)),
            pltpu.SemaphoreType.DMA((6,)),
            pltpu.SemaphoreType.DMA((3, len(BATCHES))),
        ],
        [HBM, HBM, VMEM],
        flops=work,
        mib=24,
    )(
        counts,
        core,
        neighbours,
        table,
        gain_row,
        shift_row,
        received.reshape((2,) + face),
        theirs.reshape((2,) + face),
        value_rows,
        middle,
    )
    piece = 27 * width // n_plane
    parts = lax.all_to_all(
        weight_term.reshape(n_plane, piece, 2 * width), PLANE, 0, 0, tiled=True
    )

    feature_part, sums = call(
        act_grad_kernel,
        [
            jax.ShapeDtypeStruct((slots * PITCH, width), F32),
            jax.ShapeDtypeStruct((1, 2 * width), F32),
        ],
        [SMEM] + [VMEM] * 7,
        [pltpu.VMEM((4, 16, slots, width), F32)] + [pltpu.VMEM((slots * PITCH, width), F32)] * 2,
        flops=work,
        mib=58,
    )(
        counts,
        norm,
        gain_row,
        shift_row,
        value_rows,
        cotangent_rows,
        weight.reshape(3, 9, width, 2 * width),
        grid,
    )

    part = jnp.sum(parts.astype(F32), axis=0).reshape(n_line, piece // n_line, 2 * width)
    part = jnp.concatenate(
        [part, jnp.broadcast_to(sums.reshape(1, 1, 2 * width), (n_line, 1, 2 * width))], axis=1
    )
    part = jnp.sum(lax.all_to_all(part, "z", 0, 0, tiled=True), axis=0)
    final = part[:-1].astype(BF16)
    line = jnp.broadcast_to(final[None], (n_line,) + final.shape)
    line = lax.all_to_all(line, "z", 0, 0, tiled=True).reshape(piece, 2 * width)
    line, part = lax.optimization_barrier((line, part))
    rest = part[-1:]
    split = []
    for _ in range(3):
        top = lax.reduce_precision(rest, 8, 7)
        split.append(top.astype(BF16))
        rest = rest - top
    line = jnp.concatenate([line] + split + [jnp.zeros((5, 2 * width), BF16)], axis=0)
    plane = jnp.broadcast_to(line[None], (n_plane,) + line.shape)
    plane = lax.all_to_all(plane, PLANE, 0, 0, tiled=True)
    grad_features, grad_weight, grad_gain, grad_shift = call(
        last_kernel,
        [
            jax.ShapeDtypeStruct((rows, width), BF16),
            jax.ShapeDtypeStruct((27 * width, 2 * width), F32),
            jax.ShapeDtypeStruct((1, width), F32),
            jax.ShapeDtypeStruct((1, width), F32),
        ],
        [SMEM] + [VMEM] * 5,
        [
            pltpu.VMEM((rows, width), BF16),
            pltpu.VMEM((27 * width, 2 * width), F32),
            pltpu.SemaphoreType.DMA((4,)),
            pltpu.SemaphoreType.DMA((n_plane,)),
        ],
        [HBM, HBM, VMEM, VMEM],
        mib=20,
    )(
        counts,
        norm,
        gain_row,
        plane,
        value_rows,
        feature_part,
    )
    return (
        grad_features.reshape(features.shape),
        grad_weight.reshape(27, width, 2 * width),
        grad_gain.reshape(width),
        grad_shift.reshape(width),
    )


def solution(mesh):
    slabs = mesh.devices.shape[0]
    inner = Mesh(mesh.devices.reshape(CUT[slabs] + (2,)), SLABS + ("ch",))
    in_specs = (
        P(SLABS, None, "ch"),
        P(SLABS, None, "ch"),
        P(None, "ch", None),
        P("ch"),
        P("ch"),
        P(SLABS),
        P(SLABS, None),
    )
    out_specs = (P(SLABS, None, "ch"), P(None, "ch", None), P("ch"), P("ch"))
    return jax.shard_map(body, mesh=inner, in_specs=in_specs, out_specs=out_specs, check_vma=False)
```
